32 devices in a mesh: expert: 8 (over y, x, core), hidden: 4 (over z).
Axes of the slice: x: 2, y: 2, z: 4, core: 2. Of those that a mesh axis runs over, the one named last changes fastest.
Arguments:
- tokens: bfloat16 [16384, 1024], P(('expert', 'hidden')), may hold values from -6 to 6
- token_ids: int32 [16384], P(('expert', 'hidden')), may hold values from 0 to 8007, as said below
- hash_table: int32 [8008], replicated, may hold values from 0 to 15, as said below
- first_gain: float32 [1024], replicated, may hold values from 0.1 to 1.9
- first_bias: float32 [1024], replicated, may hold values from -2 to 2
- project_in: bfloat16 [1024, 3072], replicated, may hold values from -0.1875 to 0.1875
- project_out: bfloat16 [1024, 1024], replicated, may hold values from -2 to 2
- second_gain: float32 [1024], replicated, may hold values from 0.1 to 1.9
- second_bias: float32 [1024], replicated, may hold values from -2 to 2
- expert_in: bfloat16 [16, 1024, 4096], P('expert', None, 'hidden'), may hold values from -0.1875 to 0.1875
- expert_out: bfloat16 [16, 4096, 1024], P('expert', 'hidden'), may hold values from -0.09375 to 0.09375
- cotangent: bfloat16 [16384, 1024], P(('expert', 'hidden')), may hold values from -6 to 6
Outputs:
- block_out: bfloat16 [16384, 1024], P(('expert', 'hidden'))
- grad_tokens: float32 [16384, 1024], P(('expert', 'hidden'))
- grad_first_gain: float32 [1024], replicated
- grad_first_bias: float32 [1024], replicated
- grad_project_in: float32 [1024, 3072], replicated
- grad_project_out: float32 [1024, 1024], replicated
- grad_second_gain: float32 [1024], replicated
- grad_second_bias: float32 [1024], replicated
- grad_expert_in: float32 [16, 1024, 4096], P('expert', None, 'hidden')
- grad_expert_out: float32 [16, 4096, 1024], P('expert', 'hidden')
The draws below stay inside these ranges and needn't reach their ends.
Inputs may be any that keep to these rules, and one draw needn't show every extreme that they name: Every token id v has hash_table[v] = its expert; each expert is named by 500 ids or one more. `token_ids`: among one device's 512 tokens at most 96 map to one expert through hash_table, and some expert gets exactly 96.
All inputs are finite; a program needn't handle non-finite values.
Results may differ from the reference program's by a relative error of at most 0.013.
Values may be sent and summed in bfloat16 or wider, within the bound.
A program may use at most 256 MiB of HBM per device.

```python
import jax
import jax.numpy as jnp
from jax import lax

D = 1024
HEADS = 16
HEAD_DIM = 64
FF = 4096
VOCAB = 8008
SEQ = 512
TOK_DEV = 512
TOKENS = 16384
EXPERT_COUNT = 16
EXPERT_SLOTS = 96
N_EXPERT = 8
N_HIDDEN = 4


def shared_order(key):
    return jax.random.permutation(key, VOCAB).astype(jnp.int32)


def draw_hash_table(key, part):
    order = shared_order(key)
    return (order % EXPERT_COUNT).astype(jnp.int32)


def device_tokens(key, inverse):
    keys = jax.random.split(key, 5)
    score_levels = jax.random.randint(keys[0], (EXPERT_COUNT, 1), 0, EXPERT_SLOTS * 64, dtype=jnp.int32)
    step_count = jnp.arange(EXPERT_SLOTS, dtype=jnp.int32)[None, :] * 64
    random_noise = jax.random.permutation(keys[1], EXPERT_COUNT * EXPERT_SLOTS).astype(jnp.int32).reshape(EXPERT_COUNT, EXPERT_SLOTS)
    preferred_expert = jax.random.randint(keys[2], (), 0, EXPERT_COUNT, dtype=jnp.int32)
    extra_reward = jnp.where(jnp.arange(EXPERT_COUNT, dtype=jnp.int32)[:, None] == preferred_expert, 2 ** 30, 0).astype(jnp.int32)
    router_scores = (score_levels - step_count) * (EXPERT_COUNT * EXPERT_SLOTS) + random_noise + extra_reward
    chosen = lax.top_k(router_scores.reshape(-1), TOK_DEV)[1].astype(jnp.int32)
    owners = jax.random.permutation(keys[3], chosen // EXPERT_SLOTS)
    picks = jax.random.randint(keys[4], (TOK_DEV,), 0, VOCAB // EXPERT_COUNT, dtype=jnp.int32)
    return inverse[owners + EXPERT_COUNT * picks]


def draw_token_ids(key, part):
    order = shared_order(key)
    inverse = jnp.argsort(order).astype(jnp.int32)
    key = jax.random.fold_in(key, 23)
    keys = jax.random.split(key, N_EXPERT * N_HIDDEN)
    return jax.vmap(lambda each: device_tokens(each, inverse))(keys).reshape(-1).astype(jnp.int32)


def level_of(rng, dims, pieces, smallest, high):
    loudness = 1.0
    for dim, blocks in pieces:
        steps = jax.random.uniform(jax.random.fold_in(jax.random.fold_in(rng, 6), dim), (blocks,), jnp.float32, smallest / len(pieces), high / len(pieces))
        loudness = loudness * jnp.repeat(jnp.exp(steps), dims[dim] // blocks).reshape((-1,) + (1,) * (len(dims) - 1 - dim))
    return loudness


def scatter_about(stream_key, dims, scale, limit, cuts=(), held_as=jnp.bfloat16):
    entries = jax.random.normal(stream_key, dims, jnp.float32) * scale
    if len(cuts) > 0:
        entries = level_of(stream_key, dims, cuts, -0.22, 0.18) * entries
    return jnp.clip(entries, min=-limit, max=limit).astype(held_as)


def setup_inputs(seed: int = 0) -> dict:
    arg_keys = jax.random.split(jax.random.key(seed), 13)
    return {
        "tokens": scatter_about(arg_keys[0], (TOKENS, D), 1.0, 6.0, ((0, 32),)),
        "token_ids": draw_token_ids(jax.random.fold_in(arg_keys[12], 71), 0),
        "hash_table": draw_hash_table(jax.random.fold_in(arg_keys[12], 71), 0),
        "first_gain": jnp.clip(1.0 + 0.18 * jax.random.normal(arg_keys[3], (D,), jnp.float32), 0.1, 1.9),
        "first_bias": scatter_about(arg_keys[4], (D,), 0.3, 2.0, (), jnp.float32),
        "project_in": scatter_about(arg_keys[5], (D, 3 * D), D ** -0.5, 0.1875),
        "project_out": scatter_about(arg_keys[6], (D, D), (max(D * 4 // SEQ, 1)) ** -0.5, 2.0),
        "second_gain": jnp.clip(1.0 + 0.18 * jax.random.normal(arg_keys[7], (D,), jnp.float32), 0.1, 1.9),
        "second_bias": scatter_about(arg_keys[8], (D,), 0.3, 2.0, (), jnp.float32),
        "expert_in": scatter_about(arg_keys[9], (EXPERT_COUNT, D, FF), D ** -0.5, 0.1875, ((0, 8), (2, 4))),
        "expert_out": scatter_about(arg_keys[10], (EXPERT_COUNT, FF, D), FF ** -0.5, 0.09375, ((0, 8), (1, 4))),
        "cotangent": scatter_about(arg_keys[11], (TOKENS, D), 1.0, 6.0, ((0, 32),)),
    }


@jax.custom_vjp
def low(v):
    return lax.optimization_barrier(v.astype(jnp.bfloat16)).astype(jnp.float32)

@jax.custom_vjp
def low_back(v):
    return v

def low_keep(v):
    return (low(v), None)

def low_pass(kept, grad):
    return (grad,)

def back_keep(v):
    return (v, None)

def back_low(kept, grad):
    return (low(grad),)
low.defvjp(low_keep, low_pass)
low_back.defvjp(back_keep, back_low)

def layer_norm(values, gain, bias):
    centered = values - lax.optimization_barrier(jnp.mean(values, -1, keepdims=True))
    spread = lax.optimization_barrier(jnp.mean(centered * centered, -1, keepdims=True))
    return centered * lax.rsqrt(spread + 1e-05) * gain + bias

def forward(tokens, first_gain, first_bias, project_in, project_out, second_gain, second_bias, expert_in, expert_out, place):
    high = lax.Precision.HIGHEST

    def attend(inputs):
        normed = low(layer_norm(inputs, first_gain, first_bias))
        merged = low_back(low(jnp.dot(normed, project_in, precision=high)))
        parts = merged.reshape(SEQ, 3, HEADS, HEAD_DIM)
        router_scores = low_back(jnp.einsum('qhd,khd->hqk', parts[:, 0], parts[:, 1], precision=high) * HEAD_DIM ** (-0.5))
        later = lax.broadcasted_iota(jnp.int32, (SEQ, SEQ), 1)
        earlier = lax.broadcasted_iota(jnp.int32, (SEQ, SEQ), 0)
        router_scores = jnp.where(later <= earlier, router_scores, -1e+30)
        shares = low(jax.nn.softmax(router_scores, axis=-1))
        attended = low_back(low(jnp.einsum('hqk,khd->qhd', shares, parts[:, 2], precision=high))).reshape(SEQ, D)
        residual = inputs + low_back(jnp.dot(attended, project_out, precision=high))
        return (residual, layer_norm(residual, second_gain, second_bias))
    residual, second = lax.map(jax.checkpoint(attend), tokens.reshape(-1, SEQ, D))
    residual = residual.reshape(-1, D)
    sent = low_back(low(second.reshape(-1, D)))
    slots = jnp.zeros((EXPERT_COUNT * N_EXPERT * N_HIDDEN * EXPERT_SLOTS, D), jnp.float32).at[place].set(sent)
    slots = slots.reshape(EXPERT_COUNT, N_EXPERT * N_HIDDEN * EXPERT_SLOTS, D)
    cut = FF // N_HIDDEN

    def apply_expert(operands):
        members, weight_in, weight_out = operands
        total = jnp.zeros((members.shape[0], D), jnp.float32)
        for slice_index in range(N_HIDDEN):
            copied = low_back(members)
            before = low_back(jnp.dot(copied, weight_in[:, slice_index * cut:(slice_index + 1) * cut], precision=high))
            partial_sum = jnp.dot(low(jax.nn.gelu(before)), weight_out[slice_index * cut:(slice_index + 1) * cut], precision=high)
            total = total + low(partial_sum)
        return total
    produced = lax.map(jax.checkpoint(apply_expert), (slots, expert_in, expert_out))
    produced = low_back(low(produced)).reshape(-1, D)
    return residual + produced[place]

def reference(tokens, token_ids, hash_table, first_gain, first_bias, project_in, project_out, second_gain, second_bias, expert_in, expert_out, cotangent):
    owner = jnp.take(hash_table, token_ids).astype(jnp.int32).reshape(N_EXPERT * N_HIDDEN, TOK_DEV)
    onehot = (owner[:, :, None] == jnp.arange(EXPERT_COUNT, dtype=jnp.int32)[None, None, :]).astype(jnp.int32)
    before_count = jnp.cumsum(onehot, 1, dtype=jnp.int32) - onehot
    within = lax.optimization_barrier(jnp.sum(before_count * onehot, -1, dtype=jnp.int32))
    device = jnp.arange(N_EXPERT * N_HIDDEN, dtype=jnp.int32)[:, None]
    place = ((owner * (N_EXPERT * N_HIDDEN) + device) * EXPERT_SLOTS + within).reshape(-1).astype(jnp.int32)
    params = (tokens.astype(jnp.float32), first_gain.astype(jnp.float32), first_bias.astype(jnp.float32), project_in.astype(jnp.float32), project_out.astype(jnp.float32), second_gain.astype(jnp.float32), second_bias.astype(jnp.float32), expert_in.astype(jnp.float32), expert_out.astype(jnp.float32))

    def wrapped(*values):
        return forward(*values, place)
    result, pull = jax.vjp(wrapped, *params)
    grads = pull(cotangent.astype(jnp.float32))
    return (result.astype(jnp.bfloat16), grads[0], grads[1], grads[2], grads[3], grads[4], grads[5], grads[6], grads[7], grads[8])
```

```python
import functools

import jax
import jax.numpy as jnp
from jax import lax
from jax.experimental import pallas as pl
from jax.experimental.pallas import tpu as pltpu
from jax.sharding import PartitionSpec as P

HEADS = 16
HEAD_DIM = 64
SEQ = 512
TILE = 256
EPS = 1e-05
BF = jnp.bfloat16
F32 = jnp.float32


def layer_norm(values, gain, bias):
    centered = values - jnp.mean(values, -1, keepdims=True)
    spread = jnp.mean(centered * centered, -1, keepdims=True)
    return centered * lax.rsqrt(spread + EPS) * gain + bias


def causal_scores(query, keys):
    length = query.shape[0]
    scores = jnp.einsum(
        "qhd,khd->hqk", query, keys, preferred_element_type=F32
    ) * query.shape[-1] ** (-0.5)
    earlier = lax.broadcasted_iota(jnp.int32, (length, length), 0)
    later = lax.broadcasted_iota(jnp.int32, (length, length), 1)
    return jnp.where(later <= earlier, scores, -1e30)


def dot(a, b, dims=((1,), (0,))):
    return lax.dot_general(a, b, (dims, ((), ())), preferred_element_type=F32)


def expert_kernel(local_experts, has, x, cot, eid, w_in, w_out, act_o, dbef_o, part_o, dmem_o):
    tile = pl.program_id(0)
    outs = (act_o, dbef_o, part_o, dmem_o)

    @pl.when(has[tile, 0] == 0)
    def _():
        for out in outs:
            out[...] = jnp.zeros(out.shape, out.dtype)

    for expert in range(local_experts):

        @pl.when(has[tile, expert] > 0)
        def _(expert=expert):
            mine = eid[...] == float(expert)
            before = dot(x[...], w_in[expert])
            d_after = dot(cot[...], w_out[expert], ((1,), (1,)))
            square = before * before
            inner = 0.7978845608028654 * before * (1.0 + 0.044715 * square)
            tanh = jnp.tanh(inner)
            half = 0.5 * (1.0 + tanh)
            act = (before * half).astype(BF)
            slope = half + 0.5 * before * (1.0 - tanh * tanh) * (
                0.7978845608028654 * (1.0 + 0.134145 * square)
            )
            dbef = (d_after * slope).astype(BF)
            part = dot(act, w_out[expert])
            dmem = dot(dbef, w_in[expert], ((1,), (1,)))
            news = (act.astype(F32), dbef.astype(F32), part, dmem)
            for out, new in zip(outs, news):
                old = 0.0 if expert == 0 else out[...].astype(F32)
                out[...] = jnp.where(mine, new, old).astype(BF)


def expert_rows(x, cot, eid, has, w_in, w_out):
    rows, width = x.shape
    experts, _, hidden = w_in.shape
    tiles = rows // TILE
    row_block = pl.BlockSpec((TILE, width), lambda t, has: (t, 0))
    hid_block = pl.BlockSpec((TILE, hidden), lambda t, has: (t, 0))
    whole = lambda shape: pl.BlockSpec(shape, lambda t, has: (0, 0, 0), pipeline_mode=pl.Buffered(1))
    return pl.pallas_call(
        functools.partial(expert_kernel, experts),
        grid_spec=pltpu.PrefetchScalarGridSpec(
            num_scalar_prefetch=1,
            grid=(tiles,),
            in_specs=[
                row_block,
                row_block,
                pl.BlockSpec((TILE, 1), lambda t, has: (t, 0)),
                whole(w_in.shape),
                whole(w_out.shape),
            ],
            out_specs=[hid_block, hid_block, row_block, row_block],
        ),
        out_shape=[
            jax.ShapeDtypeStruct((rows, hidden), BF),
            jax.ShapeDtypeStruct((rows, hidden), BF),
            jax.ShapeDtypeStruct((rows, width), BF),
            jax.ShapeDtypeStruct((rows, width), BF),
        ],
        compiler_params=pltpu.CompilerParams(vmem_limit_bytes=56 * 2**20),
        cost_estimate=pl.CostEstimate(
            flops=8 * rows * width * hidden,
            bytes_accessed=2 * (w_in.size + w_out.size + 6 * rows * width),
            transcendentals=rows * hidden,
        ),
        name="expert_rows",
    )(has, x, cot, eid, w_in, w_out)


def expert_grad_kernel(has, x, cot, eid, act, dbef, g_in, g_out):
    expert, tile = pl.program_id(0), pl.program_id(1)

    @pl.when(tile == 0)
    def _():
        g_in[...] = jnp.zeros(g_in.shape, F32)
        g_out[...] = jnp.zeros(g_out.shape, F32)

    @pl.when(has[tile, expert] > 0)
    def _():
        mine = jnp.where(eid[...] == expert.astype(F32), 1.0, 0.0).astype(BF)
        g_in[0] += dot(x[...], dbef[...] * mine, ((0,), (0,)))
        g_out[0] += dot(act[...] * mine, cot[...], ((0,), (0,)))


def expert_grads(x, cot, eid, has, act, dbef):
    rows, width = x.shape
    hidden = act.shape[1]
    tiles, experts = has.shape
    row_block = pl.BlockSpec((TILE, width), lambda e, t, has: (t, 0))
    hid_block = pl.BlockSpec((TILE, hidden), lambda e, t, has: (t, 0))
    return pl.pallas_call(
        expert_grad_kernel,
        grid_spec=pltpu.PrefetchScalarGridSpec(
            num_scalar_prefetch=1,
            grid=(experts, tiles),
            in_specs=[
                row_block,
                row_block,
                pl.BlockSpec((TILE, 1), lambda e, t, has: (t, 0)),
                hid_block,
                hid_block,
            ],
            out_specs=[
                pl.BlockSpec((1, width, hidden), lambda e, t, has: (e, 0, 0)),
                pl.BlockSpec((1, hidden, width), lambda e, t, has: (e, 0, 0)),
            ],
        ),
        out_shape=[
            jax.ShapeDtypeStruct((experts, width, hidden), F32),
            jax.ShapeDtypeStruct((experts, hidden, width), F32),
        ],
        compiler_params=pltpu.CompilerParams(vmem_limit_bytes=56 * 2**20),
        cost_estimate=pl.CostEstimate(
            flops=4 * rows * width * hidden,
            bytes_accessed=8 * experts * width * hidden + 16 * rows * width,
            transcendentals=0,
        ),
        name="expert_grads",
    )(has, x, cot, eid, act, dbef)


def on_device(
    tokens,
    token_ids,
    hash_table,
    first_gain,
    first_bias,
    project_in,
    project_out,
    second_gain,
    second_bias,
    expert_in,
    expert_out,
    cotangent,
):
    rows_dev, width = tokens.shape
    expert_devs = lax.axis_size("expert")
    hidden_devs = lax.axis_size("hidden")
    local = expert_in.shape[0]
    experts = local * expert_devs
    capacity = 8 * ((3 * rows_dev + 8 * experts - 1) // (8 * experts))
    chunk = local * capacity
    scale = HEAD_DIM ** (-0.5)

    owner = hash_table.at[token_ids].get(mode="promise_in_bounds")
    expert_ids = jnp.arange(experts, dtype=jnp.int32)
    onehot = owner[:, None] == expert_ids[None, :]
    earlier = lax.broadcasted_iota(jnp.int32, (rows_dev, rows_dev), 1) < lax.broadcasted_iota(
        jnp.int32, (rows_dev, rows_dev), 0
    )
    before_count = jnp.dot(earlier.astype(BF), onehot.astype(BF), preferred_element_type=F32)
    counts = jnp.sum(onehot.astype(jnp.int32), 0)
    grouped = counts.reshape(expert_devs, local)
    first_slot = (
        jnp.cumsum(grouped, 1) - grouped + jnp.arange(expert_devs, dtype=jnp.int32)[:, None] * chunk
    ).reshape(experts)
    place = jnp.sum(
        jnp.where(onehot, before_count.astype(jnp.int32) + first_slot[None, :], 0), 1
    )
    all_counts = lax.all_gather(counts, ("expert", "hidden")).reshape(
        expert_devs, hidden_devs, expert_devs, local
    )
    group = lax.axis_index("expert")
    plane = lax.axis_index("hidden")
    group_counts = lax.dynamic_index_in_dim(all_counts, group, 2, keepdims=False)
    most = jnp.max(jnp.sum(all_counts, (0, 3)))

    def run(rows):
        send = (
            place[None, :] == jnp.arange(expert_devs * chunk, dtype=jnp.int32)[:, None]
        ).astype(BF)

        mine = lax.dynamic_index_in_dim(group_counts, plane, 1, keepdims=False)
        starts = jnp.cumsum(mine, 1) - mine
        totals = jnp.sum(mine, 0)
        bases = jnp.cumsum(mine, 0) - mine + (jnp.cumsum(totals) - totals)[None, :]
        slot = jnp.arange(chunk, dtype=jnp.int32)[None, :]
        target = jnp.full((expert_devs, chunk), -1, jnp.int32)
        for l in range(local):
            offset = slot - starts[:, l : l + 1]
            target = jnp.where(
                (offset >= 0) & (offset < mine[:, l : l + 1]), bases[:, l : l + 1] + offset, target
            )
        target = target.reshape(-1)
        pack = (target[None, :] == jnp.arange(rows, dtype=jnp.int32)[:, None]).astype(BF)
        plane_totals = jnp.sum(group_counts, 0)
        ends = jnp.cumsum(plane_totals, 1)
        row = jnp.arange(rows, dtype=jnp.int32)[None, :]
        eid = jnp.zeros((hidden_devs, rows), jnp.int32)
        for l in range(local):
            eid = eid + (row >= ends[:, l : l + 1]).astype(jnp.int32)
        eid = eid.reshape(-1, 1)
        has = jnp.stack(
            [jnp.any((eid == l).reshape(-1, TILE), 1).astype(jnp.int32) for l in range(local)], 1
        )
        eid = eid.astype(F32)

        def dispatch(values):
            slots = jnp.dot(send, values, preferred_element_type=F32).astype(BF)
            arrived = lax.all_to_all(
                slots.reshape(expert_devs, chunk, width), "expert", 0, 0, tiled=True
            )
            packed = jnp.dot(
                pack, arrived.reshape(-1, width), preferred_element_type=F32
            ).astype(BF)
            return lax.all_gather(packed, "hidden", axis=0, tiled=True)

        def give_back(partial):
            summed = lax.psum_scatter(partial, "hidden", scatter_dimension=0, tiled=True)
            slots = dot(pack, summed, ((0,), (0,))).astype(BF)
            returned = lax.all_to_all(
                slots.reshape(expert_devs, chunk, width), "expert", 0, 0, tiled=True
            )
            return dot(send, returned.reshape(-1, width), ((0,), (0,)))

        cot_rows = dispatch(cotangent)

        def attend(inputs):
            normed = layer_norm(inputs, first_gain, first_bias).astype(BF)
            merged = jnp.dot(normed, project_in, preferred_element_type=F32).astype(BF)
            parts = merged.reshape(SEQ, 3, HEADS, HEAD_DIM)
            scores = causal_scores(parts[:, 0], parts[:, 1])
            top = jnp.max(scores, -1, keepdims=True)
            weights = jnp.exp(scores - top)
            total = jnp.sum(weights, -1, keepdims=True)
            shares_low = (weights / total).astype(BF)
            attended = jnp.einsum(
                "hqk,khd->qhd", shares_low, parts[:, 2], preferred_element_type=F32
            )
            attended = attended.astype(BF).reshape(SEQ, width)
            residual = inputs + jnp.dot(attended, project_out, preferred_element_type=F32)
            return (residual, merged, attended, top + jnp.log(total))

        source = tokens.astype(F32)
        residual, merged, attended, log_total = attend(source)
        second, pull_second = jax.vjp(layer_norm, residual, second_gain, second_bias)
        x_rows = dispatch(second.astype(BF))
        act, dbef, part, dmem = expert_rows(x_rows, cot_rows, eid, has, expert_in, expert_out)
        d_second = give_back(dmem)
        produced = give_back(part)
        grad_expert_in, grad_expert_out = expert_grads(x_rows, cot_rows, eid, has, act, dbef)
        block_out = (residual + produced).astype(BF)
        d_residual, grad_second_gain, grad_second_bias = pull_second(d_second)
        d_residual = d_residual + cotangent.astype(F32)

        normed, pull_first = jax.vjp(layer_norm, source, first_gain, first_bias)
        d_branch = d_residual.astype(BF)
        grad_out = dot(attended, d_branch, ((0,), (0,)))
        d_attended = dot(d_branch, project_out, ((1,), (1,)))
        d_attended = d_attended.astype(BF).reshape(SEQ, HEADS, HEAD_DIM)
        parts = merged.reshape(SEQ, 3, HEADS, HEAD_DIM)
        query, keys, values = (parts[:, 0], parts[:, 1], parts[:, 2])
        shares = jnp.exp(causal_scores(query, keys) - log_total)
        d_shares = jnp.einsum("qhd,khd->hqk", d_attended, values, preferred_element_type=F32)
        d_scores = (shares * (d_shares - jnp.sum(shares * d_shares, -1, keepdims=True))).astype(BF)
        d_query = jnp.einsum("hqk,khd->qhd", d_scores, keys, preferred_element_type=F32) * scale
        d_keys = jnp.einsum("hqk,qhd->khd", d_scores, query, preferred_element_type=F32) * scale
        d_values = jnp.einsum(
            "hqk,qhd->khd", shares.astype(BF), d_attended, preferred_element_type=F32
        )
        d_merged = (
            jnp.stack([d_query, d_keys, d_values], 1).reshape(SEQ, 3 * width).astype(BF)
        )
        grad_in = dot(normed.astype(BF), d_merged, ((0,), (0,)))
        d_normed = dot(d_merged, project_in, ((1,), (1,)))
        d_source, grad_first_gain, grad_first_bias = pull_first(d_normed)
        small = jnp.stack([grad_first_gain, grad_first_bias, grad_second_gain, grad_second_bias])
        high = small.astype(BF)
        flat = jnp.concatenate(
            [
                grad_in.astype(BF).reshape(-1, width),
                grad_out.astype(BF),
                high,
                (small - high.astype(F32)).astype(BF),
            ]
        )
        flat = lax.psum(flat, ("expert", "hidden"))
        first = 3 * width
        second_end = first + width
        grad_in = flat[:first].astype(F32).reshape(width, 3 * width)
        grad_out = flat[first:second_end].astype(F32)
        small = flat[second_end : second_end + 4].astype(F32) + flat[second_end + 4 :].astype(F32)
        return (
            block_out,
            d_residual + d_source,
            small[0],
            small[1],
            grad_in,
            grad_out,
            small[2],
            small[3],
            grad_expert_in,
            grad_expert_out,
        )

    sizes = [size for size in (768, 896) if size < expert_devs * chunk] + [expert_devs * chunk]
    pick = sum((most > size).astype(jnp.int32) for size in sizes[:-1])
    return lax.switch(pick, [functools.partial(run, size) for size in sizes])


def solution(mesh):
    rows = P(("expert", "hidden"), None)
    w_in, w_out = P("expert", None, "hidden"), P("expert", "hidden", None)
    return jax.shard_map(
        on_device,
        mesh=mesh,
        in_specs=(
            rows,
            P(("expert", "hidden")),
            P(),
            P(),
            P(),
            P(),
            P(),
            P(),
            P(),
            w_in,
            w_out,
            rows,
        ),
        out_specs=(rows, rows, P(), P(), P(), P(), P(), P(), w_in, w_out),
        check_vma=False,
    )
```

```python
import functools

import jax
import jax.numpy as jnp
from jax import lax
from jax.experimental import pallas as pl
from jax.experimental.pallas import tpu as pltpu
from jax.sharding import PartitionSpec as P

HEADS = 16
HEAD_DIM = 64
TILE = 256
BLOCK = 256
QUAD = 256
EPS = 1e-05
BF = jnp.bfloat16
F32 = jnp.float32


def dot(a, b, dims=((1,), (0,))):
    return lax.dot_general(a, b, (dims, ((), ())), preferred_element_type=F32)


def expert_kernel(local_experts, has, x, cot, eid, w_in, w_out, act_o, dbef_o, part_o, dmem_o):
    tile = pl.program_id(0)
    outs = (act_o, dbef_o, part_o, dmem_o)

    @pl.when(has[tile, 0] == 0)
    def _():
        for out in outs:
            out[...] = jnp.zeros(out.shape, out.dtype)

    for expert in range(local_experts):

        @pl.when(has[tile, expert] > 0)
        def _(expert=expert):
            mine = eid[...] == float(expert)
            before = dot(x[...], w_in[expert])
            d_after = dot(cot[...], w_out[expert], ((1,), (1,)))
            square = before * before
            inner = 0.7978845608028654 * before * (1.0 + 0.044715 * square)
            tanh = jnp.tanh(inner)
            half = 0.5 * (1.0 + tanh)
            act = (before * half).astype(BF)
            slope = half + 0.5 * before * (1.0 - tanh * tanh) * (
                0.7978845608028654 * (1.0 + 0.134145 * square)
            )
            dbef = (d_after * slope).astype(BF)
            part = dot(act, w_out[expert])
            dmem = dot(dbef, w_in[expert], ((1,), (1,)))
            news = (act.astype(F32), dbef.astype(F32), part, dmem)
            for out, new in zip(outs, news):
                old = 0.0 if expert == 0 else out[...].astype(F32)
                out[...] = jnp.where(mine, new, old).astype(BF)


def expert_rows(x, cot, eid, has, w_in, w_out):
    rows, width = x.shape
    experts, _, hidden = w_in.shape
    tiles = rows // TILE
    row_block = pl.BlockSpec((TILE, width), lambda t, has: (t, 0))
    hid_block = pl.BlockSpec((TILE, hidden), lambda t, has: (t, 0))
    whole = lambda shape: pl.BlockSpec(shape, lambda t, has: (0, 0, 0), pipeline_mode=pl.Buffered(1))
    return pl.pallas_call(
        functools.partial(expert_kernel, experts),
        grid_spec=pltpu.PrefetchScalarGridSpec(
            num_scalar_prefetch=1,
            grid=(tiles,),
            in_specs=[
                row_block,
                row_block,
                pl.BlockSpec((TILE, 1), lambda t, has: (t, 0)),
                whole(w_in.shape),
                whole(w_out.shape),
            ],
            out_specs=[hid_block, hid_block, row_block, row_block],
        ),
        out_shape=[
            jax.ShapeDtypeStruct((rows, hidden), BF),
            jax.ShapeDtypeStruct((rows, hidden), BF),
            jax.ShapeDtypeStruct((rows, width), BF),
            jax.ShapeDtypeStruct((rows, width), BF),
        ],
        compiler_params=pltpu.CompilerParams(vmem_limit_bytes=56 * 2**20),
        cost_estimate=pl.CostEstimate(
            flops=8 * rows * width * hidden,
            bytes_accessed=2 * (w_in.size + w_out.size + 6 * rows * width),
            transcendentals=rows * hidden,
        ),
        name="expert_rows",
    )(has, x, cot, eid, w_in, w_out)


def expert_grad_kernel(has, x, cot, eid, act, dbef, g_in, g_out):
    expert, tile = pl.program_id(0), pl.program_id(1)

    @pl.when(tile == 0)
    def _():
        g_in[...] = jnp.zeros(g_in.shape, F32)
        g_out[...] = jnp.zeros(g_out.shape, F32)

    @pl.when(has[tile, expert] > 0)
    def _():
        mine = jnp.where(eid[...] == expert.astype(F32), 1.0, 0.0).astype(BF)
        g_in[0] += dot(x[...], dbef[...] * mine, ((0,), (0,)))
        g_out[0] += dot(act[...] * mine, cot[...], ((0,), (0,)))


def expert_grads(x, cot, eid, has, act, dbef):
    rows, width = x.shape
    hidden = act.shape[1]
    tiles, experts = has.shape
    row_block = pl.BlockSpec((TILE, width), lambda e, t, has: (t, 0))
    hid_block = pl.BlockSpec((TILE, hidden), lambda e, t, has: (t, 0))
    return pl.pallas_call(
        expert_grad_kernel,
        grid_spec=pltpu.PrefetchScalarGridSpec(
            num_scalar_prefetch=1,
            grid=(experts, tiles),
            in_specs=[
                row_block,
                row_block,
                pl.BlockSpec((TILE, 1), lambda e, t, has: (t, 0)),
                hid_block,
                hid_block,
            ],
            out_specs=[
                pl.BlockSpec((1, width, hidden), lambda e, t, has: (e, 0, 0)),
                pl.BlockSpec((1, hidden, width), lambda e, t, has: (e, 0, 0)),
            ],
        ),
        out_shape=[
            jax.ShapeDtypeStruct((experts, width, hidden), F32),
            jax.ShapeDtypeStruct((experts, hidden, width), F32),
        ],
        compiler_params=pltpu.CompilerParams(vmem_limit_bytes=56 * 2**20),
        cost_estimate=pl.CostEstimate(
            flops=4 * rows * width * hidden,
            bytes_accessed=8 * experts * width * hidden + 16 * rows * width,
            transcendentals=0,
        ),
        name="expert_grads",
    )(has, x, cot, eid, act, dbef)


def halves(pair):
    left = lax.broadcasted_iota(jnp.int32, pair.shape, 1) < HEAD_DIM
    zero = jnp.zeros_like(pair)
    return (jnp.where(left, pair, zero), jnp.where(left, zero, pair))


def join(first, second):
    left = lax.broadcasted_iota(jnp.int32, first.shape, 1) < HEAD_DIM
    return jnp.where(left, first, second)


def tri(block):
    later = lax.broadcasted_iota(jnp.int32, (block, block), 1)
    return later <= lax.broadcasted_iota(jnp.int32, (block, block), 0)


def normalise(values):
    centered = values - jnp.mean(values, -1, keepdims=True)
    spread = jnp.mean(centered * centered, -1, keepdims=True)
    root = lax.rsqrt(spread + EPS)
    return centered * root, root


def attend_kernel(
    tokens, w_q, w_k, w_v, w_o, gain1, bias1, gain2, bias2,
    residual, second, q_out, k_out, v_out, att_out, lse,
    normed,
):
    step = pl.program_id(0)
    rows = tokens.shape[0]
    lanes = 2 * HEAD_DIM

    @pl.when(step == 0)
    def _():
        source = tokens[...].astype(F32)
        normed[...] = (normalise(source)[0] * gain1[...] + bias1[...]).astype(BF)
        residual[...] = source
        lse[...] = jnp.zeros(lse.shape, F32)

    q_out[...] = dot(normed[...], w_q[...]).astype(BF)
    k_out[...] = dot(normed[...], w_k[...]).astype(BF)
    v_out[...] = dot(normed[...], w_v[...]).astype(BF)
    width = q_out.shape[1]
    keep = tri(BLOCK)
    lane = lax.broadcasted_iota(jnp.int32, (BLOCK, lse.shape[1]), 1)
    for pair in range(width // lanes):
        cols = slice(pair * lanes, (pair + 1) * lanes)
        query = q_out[:, cols] * jnp.asarray(HEAD_DIM**-0.5, BF)
        keys = halves(k_out[:, cols])
        values = v_out[:, cols]
        for q_block in range(rows // BLOCK):
            q_rows = slice(q_block * BLOCK, (q_block + 1) * BLOCK)
            results = []
            for head in range(2):
                scores = []
                for k_block in range(q_block + 1):
                    k_rows = slice(k_block * BLOCK, (k_block + 1) * BLOCK)
                    part = dot(query[q_rows], keys[head][k_rows], ((1,), (1,)))
                    scores.append(jnp.where(keep, part, -1e30) if k_block == q_block else part)
                top = functools.reduce(jnp.maximum, [jnp.max(s, -1, keepdims=True) for s in scores])
                weights = [jnp.exp(s - top) for s in scores]
                total = sum(jnp.sum(w, -1, keepdims=True) for w in weights)
                share = 1.0 / total
                out = sum(
                    dot((w * share).astype(BF), values[k * BLOCK : (k + 1) * BLOCK])
                    for k, w in enumerate(weights)
                )
                results.append(out)
                index = step * (width // HEAD_DIM) + 2 * pair + head
                lse[q_rows, :] = jnp.where(lane == index, top + jnp.log(total), lse[q_rows, :])
            att_out[q_rows, cols] = join(*results).astype(BF)
    residual[...] += dot(att_out[...], w_o[...])

    @pl.when(step == pl.num_programs(0) - 1)
    def _():
        second[...] = (normalise(residual[...])[0] * gain2[...] + bias2[...]).astype(BF)


def attend(tokens, project_in, project_out, gain1, bias1, gain2, bias2):
    rows, width = tokens.shape
    steps = width // QUAD
    whole = lambda shape: pl.BlockSpec(shape, lambda j: (0, 0))
    third = lambda k: pl.BlockSpec((width, QUAD), lambda j: (0, k * steps + j))
    cols = pl.BlockSpec((rows, QUAD), lambda j: (0, j))
    vector = whole((1, width))
    low = jax.ShapeDtypeStruct((rows, width), BF)
    return pl.pallas_call(
        attend_kernel,
        grid=(steps,),
        in_specs=[whole((rows, width)), third(0), third(1), third(2),
            pl.BlockSpec((QUAD, width), lambda j: (j, 0)), vector, vector, vector, vector],
        out_specs=[whole((rows, width)), whole((rows, width)), cols, cols, cols, cols, whole((rows, 128))],
        out_shape=[jax.ShapeDtypeStruct((rows, width), F32), low, low, low, low, low,
            jax.ShapeDtypeStruct((rows, 128), F32)],
        scratch_shapes=[pltpu.VMEM((rows, width), BF)],
        compiler_params=pltpu.CompilerParams(vmem_limit_bytes=56 * 2**20),
        cost_estimate=pl.CostEstimate(flops=10 * rows * width * width, bytes_accessed=20 * 2**20,
            transcendentals=HEADS * rows * rows),
        name="attend",
    )(tokens, project_in, project_in, project_in, project_out, *(v.reshape(1, width) for v in (gain1, bias1, gain2, bias2)))


def layer_norm_back(d_normed, xhat, root, gain):
    scaled = d_normed * gain
    d_values = root * (
        scaled
        - jnp.mean(scaled, -1, keepdims=True)
        - xhat * jnp.mean(scaled * xhat, -1, keepdims=True)
    )
    sums = (jnp.sum(d_normed * xhat, 0, keepdims=True), jnp.sum(d_normed, 0, keepdims=True))
    return d_values, sums


def attend_back_kernel(
    tokens, residual, d_second, cot, q, k, v, att, lse, w_q, w_k, w_v, w_o, gain1, bias1, gain2,
    grad_tokens, grads,
    normed, d_branch, d_normed, small,
):
    step = pl.program_id(0)
    rows, width = tokens.shape
    lanes = 2 * HEAD_DIM
    scale = jnp.asarray(HEAD_DIM**-0.5, BF)

    @pl.when(step == 0)
    def _():
        xhat, root = normalise(residual[...])
        d_values, sums = layer_norm_back(d_second[...].astype(F32), xhat, root, gain2[...])
        d_residual = cot[...].astype(F32) + d_values
        grad_tokens[...] = d_residual
        d_branch[...] = d_residual.astype(BF)
        small[...] = jnp.zeros(small.shape, F32)
        small[2:3, :], small[3:4, :] = sums
        normed[...] = (
            normalise(tokens[...].astype(F32))[0] * gain1[...] + bias1[...]
        ).astype(BF)
        d_normed[...] = jnp.zeros(d_normed.shape, F32)

    quad = q.shape[1]
    place = lambda third: pl.ds(pl.multiple_of(third * width + step * quad, quad), quad)
    grads[pl.ds(pl.multiple_of(step * quad, quad), quad), 3 * width :] = dot(
        att[...], d_branch[...], ((0,), (0,))
    ).astype(BF)
    d_att = dot(d_branch[...], w_o[...], ((1,), (1,))).astype(BF)
    keep = tri(BLOCK)
    blocks = rows // BLOCK
    cut = lambda array, block: array[block * BLOCK : (block + 1) * BLOCK]
    d_q, d_k, d_v = [], [], []
    lane = lax.broadcasted_iota(jnp.int32, (BLOCK, lse.shape[1]), 1)
    for pair in range(quad // lanes):
        cols = slice(pair * lanes, (pair + 1) * lanes)
        query = q[:, cols] * scale
        key, value, d_pair = k[:, cols], v[:, cols], d_att[:, cols]
        keys, values = halves(key), halves(value)
        pair_q, pair_k, pair_v = [], [], []
        for head in range(2):
            index = step * (quad // HEAD_DIM) + 2 * pair + head
            q_parts = []
            k_parts, v_parts = [0.0] * blocks, [0.0] * blocks
            for q_block in range(blocks):
                q_rows = slice(q_block * BLOCK, (q_block + 1) * BLOCK)
                level = jnp.sum(jnp.where(lane == index, lse[q_rows, :], 0.0), -1, keepdims=True)
                shares, d_shares, inner = [], [], 0.0
                for k_block in range(q_block + 1):
                    scores = dot(cut(query, q_block), cut(keys[head], k_block), ((1,), (1,)))
                    share = jnp.exp(scores - level)
                    if k_block == q_block:
                        share = jnp.where(keep, share, 0.0)
                    d_share = dot(cut(d_pair, q_block), cut(values[head], k_block), ((1,), (1,)))
                    inner = inner + jnp.sum(share * d_share, -1, keepdims=True)
                    shares.append(share)
                    d_shares.append(d_share)
                total = 0.0
                for k_block in range(q_block + 1):
                    d_scores = (shares[k_block] * (d_shares[k_block] - inner)).astype(BF)
                    total = total + dot(d_scores, cut(key, k_block))
                    k_parts[k_block] += dot(d_scores, cut(query, q_block), ((0,), (0,)))
                    v_parts[k_block] += dot(
                        shares[k_block].astype(BF), cut(d_pair, q_block), ((0,), (0,))
                    )
                q_parts.append(total * HEAD_DIM**-0.5)
            pair_q.append(jnp.concatenate(q_parts, 0))
            pair_k.append(jnp.concatenate(k_parts, 0))
            pair_v.append(jnp.concatenate(v_parts, 0))
        d_q.append(join(*pair_q).astype(BF))
        d_k.append(join(*pair_k).astype(BF))
        d_v.append(join(*pair_v).astype(BF))
    total = 0.0
    for third, (parts, weight) in enumerate(((d_q, w_q), (d_k, w_k), (d_v, w_v))):
        d_third = jnp.concatenate(parts, 1)
        grads[:width, place(third)] = dot(normed[...], d_third, ((0,), (0,))).astype(BF)
        total = total + dot(d_third, weight[...], ((1,), (1,)))
    d_normed[...] += total

    @pl.when(step == pl.num_programs(0) - 1)
    def _():
        xhat, root = normalise(tokens[...].astype(F32))
        d_values, sums = layer_norm_back(d_normed[...], xhat, root, gain1[...])
        grad_tokens[...] += d_values
        small[0:1, :], small[1:2, :] = sums
        exact = small[...]
        high = exact.astype(BF)
        grads[width : width + 8, :width] = high
        grads[width + 8 :, :width] = (exact - high.astype(F32)).astype(BF)
        grads[width:, width:] = jnp.zeros((16, 3 * width), BF)


def attend_back(tokens, residual, d_second, cot, q, k, v, att, lse, project_in, project_out, gain1, bias1, gain2):
    rows, width = tokens.shape
    steps = width // QUAD
    whole = lambda shape: pl.BlockSpec(shape, lambda j: (0, 0))
    third = lambda k: pl.BlockSpec((width, QUAD), lambda j: (0, k * steps + j))
    cols = pl.BlockSpec((rows, QUAD), lambda j: (0, j))
    full, vector = whole((rows, width)), whole((1, width))
    return pl.pallas_call(
        attend_back_kernel,
        grid=(steps,),
        in_specs=[full, full, full, full, cols, cols, cols, cols, whole((rows, 128)),
            third(0), third(1), third(2), pl.BlockSpec((QUAD, width), lambda j: (j, 0)), vector, vector, vector],
        out_specs=[full, whole((width + 16, 4 * width))],
        out_shape=[jax.ShapeDtypeStruct((rows, width), F32), jax.ShapeDtypeStruct((width + 16, 4 * width), BF)],
        scratch_shapes=[pltpu.VMEM((rows, width), BF), pltpu.VMEM((rows, width), BF),
            pltpu.VMEM((rows, width), F32), pltpu.VMEM((8, width), F32)],
        compiler_params=pltpu.CompilerParams(vmem_limit_bytes=56 * 2**20),
        cost_estimate=pl.CostEstimate(flops=20 * rows * width * width, bytes_accessed=32 * 2**20,
            transcendentals=HEADS * rows * rows),
        name="attend_back",
    )(tokens, residual, d_second, cot, q, k, v, att, lse, project_in, project_in, project_in, project_out,
      *(x.reshape(1, width) for x in (gain1, bias1, gain2)))


MESH = pl.DeviceIdType.MESH


def remote(src, dst, send_sem, recv_sem, device):
    return pltpu.make_async_remote_copy(
        src_ref=src,
        dst_ref=dst,
        send_sem=send_sem,
        recv_sem=recv_sem,
        device_id=device,
        device_id_type=MESH,
    )


def ones_where(mask):
    return jnp.where(mask, 1.0, 0.0).astype(BF)


def pass_kernel(
    rows, pieces,
    x, place, target, target_rows, cot_in, eid, w_in, w_out,
    x_all, cot_all, act_o, dbef_o, part_o, d_second,
    slots, arrived, packed_x, packed_c, returned, d_part, from_down, from_up, x_tile, c_tile, stage,
    plane_send, plane_recv, back_send, back_recv, ag_send, ag_recv, rs_send, rs_down, rs_up, local_sem, stage_sem,
):
    me, plane = lax.axis_index("expert"), lax.axis_index("hidden")
    devices, chunk, width = slots.shape
    experts = w_in.shape[0]
    height = rows // pieces
    side = lax.div(plane, 2)
    r = plane + side * (3 - 2 * plane)
    middle = r == 1
    step = 1 - 2 * side
    up, down = {"hidden": plane + step}, {"hidden": plane - step}
    physical = lambda rel: rel + side * (3 - 2 * rel)
    part_of = lambda j: pl.ds(pl.multiple_of(j * height, 16), height)

    barrier = pltpu.get_barrier_semaphore()

    def greet(off, carry):
        peer = {"expert": lax.rem(me + off, devices)}
        pl.semaphore_signal(barrier, inc=1, device_id=peer, device_id_type=MESH)
        return carry

    lax.fori_loop(1, devices, greet, 0)
    pl.semaphore_signal(barrier, inc=1, device_id=up, device_id_type=MESH)

    @pl.when(middle)
    def _():
        pl.semaphore_signal(barrier, inc=1, device_id=down, device_id_type=MESH)

    pl.semaphore_wait(barrier, devices + r)

    def slots_of(device):
        row = lax.broadcasted_iota(jnp.int32, (chunk, x.shape[0]), 0) + device * chunk
        return dot(ones_where(row == place[...]), x[...]).astype(BF)

    def dispatch_copy(off, to, frm):
        return remote(
            slots.at[to], arrived.at[frm], plane_send.at[off], plane_recv.at[off], {"expert": to}
        )

    def dispatch(off, carry):
        peer = lax.rem(me + off, devices)
        slots[peer] = slots_of(peer)
        dispatch_copy(off, peer, me).start()
        return carry

    lax.fori_loop(1, devices, dispatch, 0)
    arrived[me] = slots_of(me)

    def pack(source, j):
        row = lax.broadcasted_iota(jnp.int32, (height, devices * chunk), 0) + j * height
        flat = source[...].reshape(devices * chunk, width)
        return dot(ones_where(row == target[...]), flat).astype(BF)

    alls, packs = (x_all, cot_all), (packed_x, packed_c)

    def gather_copy(kind, way, block, j, own):
        source = packs[kind].at[part_of(j)] if own else alls[kind].at[block, part_of(j)]
        return remote(
            source,
            alls[kind].at[block, part_of(j)],
            ag_send.at[kind, way, block, j],
            ag_recv.at[kind, block, j],
            down if way else up,
        )

    def send_own(kind, source):
        def body(j, carry):
            packs[kind][part_of(j)] = pack(source, j)
            gather_copy(kind, 0, plane, j, True).start()

            @pl.when(middle)
            def _():
                gather_copy(kind, 1, plane, j, True).start()

            return carry

        lax.fori_loop(0, pieces, body, 0)

    def keep_own(kind):
        return pltpu.make_async_copy(packs[kind], alls[kind].at[plane], local_sem.at[kind])

    send_own(1, cot_in)
    keep_own(1).start()

    def dispatch_done(off, carry):
        dispatch_copy(off, me, lax.rem(me - off + devices, devices)).wait_recv()
        return carry

    lax.fori_loop(1, devices, dispatch_done, 0)
    send_own(0, arrived)
    keep_own(0).start()
    keep_own(1).wait()
    keep_own(0).wait()

    def got(kind, rel, j):
        gather_copy(kind, 0, physical(rel), j, False).wait_recv()

    def relay(kind, rel, way, j):
        got(kind, rel, j)
        gather_copy(kind, way, physical(rel), j, False).start()

    def sum_copy(rel, j, buffer, index, sems, device):
        return remote(
            d_part.at[physical(rel), part_of(j)],
            buffer.at[index, part_of(j)],
            rs_send.at[rel, j],
            sems.at[index, j],
            device,
        )

    def add(rel, j, buffer, index, sems):
        sum_copy(rel, j, buffer, index, sems, up).wait_recv()
        block = physical(rel)
        here = d_part[block, part_of(j)].astype(F32)
        d_part[block, part_of(j)] = (here + buffer[index, part_of(j)].astype(F32)).astype(BF)

    outs = (act_o, dbef_o, part_o)

    def stage_copy(index, block, j):
        return pltpu.make_async_copy(
            stage.at[index], outs[index].at[block, part_of(j)], stage_sem.at[index]
        )

    def tile(p, j):
        @pl.when((p == 0) & middle)
        def _():
            relay(1, 0, 0, j)
            relay(1, 2, 1, j)

        @pl.when((p == 1) & middle)
        def _():
            relay(0, 0, 0, j)
            relay(0, 2, 1, j)
            relay(1, 3, 1, j)

        @pl.when((p == 2) & middle)
        def _():
            relay(0, 3, 1, j)

        @pl.when((p > 0) & (r == 0))
        def _():
            got(1, p, j)
            got(0, p, j)

        block = physical(jnp.where(p < 2, lax.rem(p + r, 2), p))
        loads = [
            pltpu.make_async_copy(a.at[block, part_of(j)], t, local_sem.at[i])
            for i, (a, t) in enumerate(((x_all, x_tile), (cot_all, c_tile)))
        ]
        for load in loads:
            load.start()
        for load in loads:
            load.wait()
        start = pl.multiple_of(block * rows + j * height, 16)
        owner = eid[pl.ds(start, height), :]
        mine = [owner == float(e) for e in range(experts)]

        def choose(results):
            total = jnp.where(mine[0], results[0], 0.0)
            for mask, result in zip(mine[1:], results[1:]):
                total = jnp.where(mask, result, total)
            return total

        before = choose([dot(x_tile[...], w_in[e]) for e in range(experts)])
        d_after = choose([dot(c_tile[...], w_out[e], ((1,), (1,))) for e in range(experts)])
        square = before * before
        tanh = jnp.tanh(0.7978845608028654 * before * (1.0 + 0.044715 * square))
        half = 0.5 * (1.0 + tanh)
        slope = half + 0.5 * before * (1.0 - tanh * tanh) * (
            0.7978845608028654 * (1.0 + 0.134145 * square)
        )

        @pl.when((p > 0) | (j > 0))
        def _():
            for index in range(3):
                stage_copy(index, block, j).wait()

        stage[0] = (before * half).astype(BF)
        stage[1] = (d_after * slope).astype(BF)
        d_part[block, part_of(j)] = choose(
            [dot(stage[1], w_in[e], ((1,), (1,))) for e in range(experts)]
        ).astype(BF)

        @pl.when((p > 0) & (r == 0))
        def _():
            sum_copy(p, j, from_down, p - 1, rs_down, up).start()

        @pl.when((p == 3) & middle)
        def _():
            add(2, j, from_down, 1, rs_down)
            sum_copy(2, j, from_up, 1, rs_up, up).start()

        stage[2] = choose([dot(stage[0], w_out[e]) for e in range(experts)]).astype(BF)
        for index in range(3):
            stage_copy(index, block, j).start()

    def phase(p, carry):
        return lax.fori_loop(0, pieces, lambda j, c: (tile(p, j), c)[1], carry)

    lax.fori_loop(0, 4, phase, 0)
    for index in range(3):
        stage_copy(index, plane, 0).wait()

    @pl.when(middle)
    def _():
        def body(j, carry):
            @pl.when(j < pieces)
            def _():
                add(3, j, from_down, 2, rs_down)
                sum_copy(3, j, from_up, 0, rs_up, up).start()

            @pl.when(j > 0)
            def _():
                add(0, j - 1, from_up, 0, rs_up)
                sum_copy(0, j - 1, from_up, 0, rs_up, down).start()

            return carry

        lax.fori_loop(0, pieces + 1, body, 0)

    def last(j, carry):
        @pl.when(middle)
        def _():
            add(1, j, from_down, 0, rs_down)
            add(1, j, from_up, 1, rs_up)

        @pl.when(r == 0)
        def _():
            add(0, j, from_up, 0, rs_up)

        return carry

    lax.fori_loop(0, pieces, last, 0)

    def dispatch_sent(off, carry):
        peer = lax.rem(me + off, devices)
        dispatch_copy(off, peer, me).wait_send()
        return carry

    lax.fori_loop(1, devices, dispatch_sent, 0)

    def back_slots(device):
        row = lax.broadcasted_iota(jnp.int32, (rows, chunk), 0)
        return dot(ones_where(row == target_rows[device]), d_part[plane], ((0,), (0,))).astype(BF)

    def back_copy(off, to, frm):
        return remote(
            slots.at[to], returned.at[frm], back_send.at[off], back_recv.at[off], {"expert": to}
        )

    def back(off, carry):
        peer = lax.rem(me + off, devices)
        slots[peer] = back_slots(peer)
        back_copy(off, peer, me).start()
        return carry

    lax.fori_loop(1, devices, back, 0)
    returned[me] = back_slots(me)

    def back_done(off, carry):
        back_copy(off, me, lax.rem(me - off + devices, devices)).wait_recv()
        return carry

    lax.fori_loop(1, devices, back_done, 0)
    slot = lax.broadcasted_iota(jnp.int32, (devices * chunk, x.shape[0]), 0)
    flat = returned[...].reshape(devices * chunk, width)
    d_second[...] = dot(ones_where(slot == place[...]), flat, ((0,), (0,))).astype(BF)

    def back_sent(off, carry):
        back_copy(off, lax.rem(me + off, devices), me).wait_send()
        return carry

    lax.fori_loop(1, devices, back_sent, 0)

    def sent(j, carry):
        for kind in range(2):
            gather_copy(kind, 0, plane, j, True).wait_send()

        @pl.when(middle)
        def _():
            for kind in range(2):
                gather_copy(kind, 1, plane, j, True).wait_send()
                gather_copy(kind, 0, physical(0), j, False).wait_send()
                for rel in (2, 3):
                    gather_copy(kind, 1, physical(rel), j, False).wait_send()
            for rel in (0, 2, 3):
                sum_copy(rel, j, from_up, 0, rs_up, up).wait_send()

        @pl.when(r == 0)
        def _():
            for rel in (1, 2, 3):
                sum_copy(rel, j, from_up, 0, rs_up, up).wait_send()

        return carry

    lax.fori_loop(0, pieces, sent, 0)


def expert_pass(rows, pieces, number, x, place, target, cot_in, eid, w_in, w_out):
    devices, chunk, width = cot_in.shape
    hidden = w_in.shape[2]
    planes = eid.shape[0] // rows
    height = rows // pieces
    here, there = pl.BlockSpec(memory_space=pltpu.VMEM), pl.BlockSpec(memory_space=pl.ANY)
    dma = pltpu.SemaphoreType.DMA
    wide = jax.ShapeDtypeStruct((planes, rows, width), BF)
    return pl.pallas_call(
        functools.partial(pass_kernel, rows, pieces),
        in_specs=[here] * 8,
        out_specs=[there] * 5 + [here],
        out_shape=[wide] * 5 + [jax.ShapeDtypeStruct(x.shape, BF)],
        scratch_shapes=[
            pltpu.VMEM((devices, chunk, width), BF),
            pltpu.VMEM((devices, chunk, width), BF),
            pltpu.VMEM((rows, width), BF),
            pltpu.VMEM((rows, width), BF),
            pltpu.VMEM((devices, chunk, width), BF),
            pltpu.VMEM((planes, rows, width), BF),
            pltpu.VMEM((3, rows, width), BF),
            pltpu.VMEM((2, rows, width), BF),
            pltpu.VMEM((height, width), BF),
            pltpu.VMEM((height, width), BF),
            pltpu.VMEM((3, height, hidden), BF),
            dma((devices,)),
            dma((devices,)),
            dma((devices,)),
            dma((devices,)),
            dma((2, 2, planes, pieces)),
            dma((2, planes, pieces)),
            dma((planes, pieces)),
            dma((3, pieces)),
            dma((2, pieces)),
            dma((2,)),
            dma((3,)),
        ],
        compiler_params=pltpu.CompilerParams(
            collective_id=number, has_side_effects=True, vmem_limit_bytes=62 * 2**20
        ),
        cost_estimate=pl.CostEstimate(
            flops=16 * planes * rows * width * hidden,
            bytes_accessed=16 * planes * rows * width,
            transcendentals=planes * rows * hidden,
        ),
        name="expert_pass",
    )(x, place.reshape(1, -1), target.reshape(1, -1), target.reshape(devices, 1, chunk), cot_in, eid, w_in, w_out)


def on_device(
    tokens,
    token_ids,
    hash_table,
    first_gain,
    first_bias,
    project_in,
    project_out,
    second_gain,
    second_bias,
    expert_in,
    expert_out,
    cotangent,
):
    rows_dev, width = tokens.shape
    expert_devs = lax.axis_size("expert")
    hidden_devs = lax.axis_size("hidden")
    local = expert_in.shape[0]
    experts = local * expert_devs
    capacity = 8 * ((3 * rows_dev + 8 * experts - 1) // (8 * experts))
    chunk = local * capacity

    owner = hash_table.at[token_ids].get(mode="promise_in_bounds")
    expert_ids = jnp.arange(experts, dtype=jnp.int32)
    onehot = owner[:, None] == expert_ids[None, :]
    earlier = lax.broadcasted_iota(jnp.int32, (rows_dev, rows_dev), 1) < lax.broadcasted_iota(
        jnp.int32, (rows_dev, rows_dev), 0
    )
    before_count = jnp.dot(earlier.astype(BF), onehot.astype(BF), preferred_element_type=F32)
    counts = jnp.sum(onehot.astype(jnp.int32), 0)
    grouped = counts.reshape(expert_devs, local)
    first_slot = (
        jnp.cumsum(grouped, 1) - grouped + jnp.arange(expert_devs, dtype=jnp.int32)[:, None] * chunk
    ).reshape(experts)
    place = jnp.sum(
        jnp.where(onehot, before_count.astype(jnp.int32) + first_slot[None, :], 0), 1
    )
    all_counts = lax.all_gather(counts, ("expert", "hidden")).reshape(
        expert_devs, hidden_devs, expert_devs, local
    )
    group = lax.axis_index("expert")
    plane = lax.axis_index("hidden")
    group_counts = lax.dynamic_index_in_dim(all_counts, group, 2, keepdims=False)
    most = jnp.max(jnp.sum(all_counts, (0, 3)))

    def run(rows, pieces, number):
        send = (
            place[None, :] == jnp.arange(expert_devs * chunk, dtype=jnp.int32)[:, None]
        ).astype(BF)

        mine = lax.dynamic_index_in_dim(group_counts, plane, 1, keepdims=False)
        starts = jnp.cumsum(mine, 1) - mine
        totals = jnp.sum(mine, 0)
        bases = jnp.cumsum(mine, 0) - mine + (jnp.cumsum(totals) - totals)[None, :]
        slot = jnp.arange(chunk, dtype=jnp.int32)[None, :]
        target = jnp.full((expert_devs, chunk), -1, jnp.int32)
        for l in range(local):
            offset = slot - starts[:, l : l + 1]
            target = jnp.where(
                (offset >= 0) & (offset < mine[:, l : l + 1]), bases[:, l : l + 1] + offset, target
            )
        target = target.reshape(-1)
        pack = (target[None, :] == jnp.arange(rows, dtype=jnp.int32)[:, None]).astype(BF)
        plane_totals = jnp.sum(group_counts, 0)
        ends = jnp.cumsum(plane_totals, 1)
        row = jnp.arange(rows, dtype=jnp.int32)[None, :]
        eid = jnp.zeros((hidden_devs, rows), jnp.int32)
        for l in range(local):
            eid = eid + (row >= ends[:, l : l + 1]).astype(jnp.int32)
        eid = eid.reshape(-1, 1)
        has = jnp.stack(
            [jnp.any((eid == l).reshape(-1, TILE), 1).astype(jnp.int32) for l in range(local)], 1
        )
        eid = eid.astype(F32)

        def dispatch(values):
            slots = jnp.dot(send, values, preferred_element_type=F32).astype(BF)
            arrived = lax.all_to_all(
                slots.reshape(expert_devs, chunk, width), "expert", 0, 0, tiled=True
            )
            packed = jnp.dot(
                pack, arrived.reshape(-1, width), preferred_element_type=F32
            ).astype(BF)
            return lax.all_gather(packed, "hidden", axis=0, tiled=True)

        def give_back(partial):
            summed = lax.psum_scatter(partial, "hidden", scatter_dimension=0, tiled=True)
            slots = dot(pack, summed, ((0,), (0,))).astype(BF)
            returned = lax.all_to_all(
                slots.reshape(expert_devs, chunk, width), "expert", 0, 0, tiled=True
            )
            return dot(send, returned.reshape(-1, width), ((0,), (0,))).astype(BF)

        special = hidden_devs == 4 and rows < expert_devs * chunk
        if not special:
            cot_rows = dispatch(cotangent)

        residual, second, query, keys, values, attended, lse = attend(
            tokens, project_in, project_out, first_gain, first_bias, second_gain, second_bias
        )
        if special:
            cot_slots = jnp.dot(send, cotangent, preferred_element_type=F32).astype(BF)
            cot_arrived = lax.all_to_all(
                cot_slots.reshape(expert_devs, chunk, width), "expert", 0, 0, tiled=True
            )
            *wide, d_second = expert_pass(
                rows, pieces, number, second, place, target, cot_arrived, eid, expert_in, expert_out
            )
            x_rows, cot_rows, act, dbef, part = (w.reshape(-1, width) for w in wide)
        else:
            x_rows = dispatch(second)
            act, dbef, part, dmem = expert_rows(x_rows, cot_rows, eid, has, expert_in, expert_out)
            d_second = give_back(dmem)
        produced = give_back(part)
        grad_expert_in, grad_expert_out = expert_grads(x_rows, cot_rows, eid, has, act, dbef)
        block_out = (residual + produced.astype(F32)).astype(BF)
        grad_tokens, flat = attend_back(
            tokens, residual, d_second, cotangent, query, keys, values, attended, lse,
            project_in, project_out, first_gain, first_bias, second_gain,
        )
        flat = lax.psum(flat, ("expert", "hidden")).astype(F32)
        grad_in, grad_out = flat[:width, : 3 * width], flat[:width, 3 * width :]
        small = flat[width : width + 8, :width] + flat[width + 8 :, :width]
        return (
            block_out,
            grad_tokens,
            small[0],
            small[1],
            grad_in,
            grad_out,
            small[2],
            small[3],
            grad_expert_in,
            grad_expert_out,
        )

    most_rows = expert_devs * chunk
    plans = [(768, 3, 1), (896, 4, 2)]
    plans = [plan for plan in plans if plan[0] < most_rows] + [(most_rows, 0, 0)]
    pick = sum((most > plan[0]).astype(jnp.int32) for plan in plans[:-1])
    return lax.switch(pick, [functools.partial(run, *plan) for plan in plans])


def solution(mesh):
    rows = P(("expert", "hidden"), None)
    w_in, w_out = P("expert", None, "hidden"), P("expert", "hidden", None)
    return jax.shard_map(
        on_device,
        mesh=mesh,
        in_specs=(
            rows,
            P(("expert", "hidden")),
            P(),
            P(),
            P(),
            P(),
            P(),
            P(),
            P(),
            w_in,
            w_out,
            rows,
        ),
        out_specs=(rows, rows, P(), P(), P(), P(), P(), P(), w_in, w_out),
        check_vma=False,
    )
```

```python
import functools

import jax
import jax.numpy as jnp
from jax import lax
from jax.experimental import pallas as pl
from jax.experimental.pallas import tpu as pltpu
from jax.sharding import PartitionSpec as P

HEADS = 16
HEAD_DIM = 64
TILE = 256
BLOCK = 256
QUAD = 256
EPS = 1e-05
BF = jnp.bfloat16
F32 = jnp.float32


def dot(a, b, dims=((1,), (0,))):
    return lax.dot_general(a, b, (dims, ((), ())), preferred_element_type=F32)


def expert_kernel(local_experts, has, x, cot, eid, w_in, w_out, act_o, dbef_o, part_o, dmem_o):
    tile = pl.program_id(0)
    outs = (act_o, dbef_o, part_o, dmem_o)

    @pl.when(has[tile, 0] == 0)
    def _():
        for out in outs:
            out[...] = jnp.zeros(out.shape, out.dtype)

    for expert in range(local_experts):

        @pl.when(has[tile, expert] > 0)
        def _(expert=expert):
            mine = eid[...] == float(expert)
            before = dot(x[...], w_in[expert])
            d_after = dot(cot[...], w_out[expert], ((1,), (1,)))
            square = before * before
            inner = 0.7978845608028654 * before * (1.0 + 0.044715 * square)
            tanh = jnp.tanh(inner)
            half = 0.5 * (1.0 + tanh)
            act = (before * half).astype(BF)
            slope = half + 0.5 * before * (1.0 - tanh * tanh) * (
                0.7978845608028654 * (1.0 + 0.134145 * square)
            )
            dbef = (d_after * slope).astype(BF)
            part = dot(act, w_out[expert])
            dmem = dot(dbef, w_in[expert], ((1,), (1,)))
            news = (act.astype(F32), dbef.astype(F32), part, dmem)
            for out, new in zip(outs, news):
                old = 0.0 if expert == 0 else out[...].astype(F32)
                out[...] = jnp.where(mine, new, old).astype(BF)


def expert_rows(x, cot, eid, has, w_in, w_out):
    rows, width = x.shape
    experts, _, hidden = w_in.shape
    tiles = rows // TILE
    row_block = pl.BlockSpec((TILE, width), lambda t, has: (t, 0))
    hid_block = pl.BlockSpec((TILE, hidden), lambda t, has: (t, 0))
    whole = lambda shape: pl.BlockSpec(shape, lambda t, has: (0, 0, 0), pipeline_mode=pl.Buffered(1))
    return pl.pallas_call(
        functools.partial(expert_kernel, experts),
        grid_spec=pltpu.PrefetchScalarGridSpec(
            num_scalar_prefetch=1,
            grid=(tiles,),
            in_specs=[
                row_block,
                row_block,
                pl.BlockSpec((TILE, 1), lambda t, has: (t, 0)),
                whole(w_in.shape),
                whole(w_out.shape),
            ],
            out_specs=[hid_block, hid_block, row_block, row_block],
        ),
        out_shape=[
            jax.ShapeDtypeStruct((rows, hidden), BF),
            jax.ShapeDtypeStruct((rows, hidden), BF),
            jax.ShapeDtypeStruct((rows, width), BF),
            jax.ShapeDtypeStruct((rows, width), BF),
        ],
        compiler_params=pltpu.CompilerParams(vmem_limit_bytes=56 * 2**20),
        cost_estimate=pl.CostEstimate(
            flops=8 * rows * width * hidden,
            bytes_accessed=2 * (w_in.size + w_out.size + 6 * rows * width),
            transcendentals=rows * hidden,
        ),
        name="expert_rows",
    )(has, x, cot, eid, w_in, w_out)


def expert_grad_kernel(has, x, cot, eid, act, dbef, g_in, g_out):
    expert, tile = pl.program_id(0), pl.program_id(1)

    @pl.when(tile == 0)
    def _():
        g_in[...] = jnp.zeros(g_in.shape, F32)
        g_out[...] = jnp.zeros(g_out.shape, F32)

    @pl.when(has[tile, expert] > 0)
    def _():
        mine = jnp.where(eid[...] == expert.astype(F32), 1.0, 0.0).astype(BF)
        g_in[0] += dot(x[...], dbef[...] * mine, ((0,), (0,)))
        g_out[0] += dot(act[...] * mine, cot[...], ((0,), (0,)))


def expert_grads(x, cot, eid, has, act, dbef):
    rows, width = x.shape
    hidden = act.shape[1]
    tiles, experts = has.shape
    row_block = pl.BlockSpec((TILE, width), lambda e, t, has: (t, 0))
    hid_block = pl.BlockSpec((TILE, hidden), lambda e, t, has: (t, 0))
    return pl.pallas_call(
        expert_grad_kernel,
        grid_spec=pltpu.PrefetchScalarGridSpec(
            num_scalar_prefetch=1,
            grid=(experts, tiles),
            in_specs=[
                row_block,
                row_block,
                pl.BlockSpec((TILE, 1), lambda e, t, has: (t, 0)),
                hid_block,
                hid_block,
            ],
            out_specs=[
                pl.BlockSpec((1, width, hidden), lambda e, t, has: (e, 0, 0)),
                pl.BlockSpec((1, hidden, width), lambda e, t, has: (e, 0, 0)),
            ],
        ),
        out_shape=[
            jax.ShapeDtypeStruct((experts, width, hidden), F32),
            jax.ShapeDtypeStruct((experts, hidden, width), F32),
        ],
        compiler_params=pltpu.CompilerParams(vmem_limit_bytes=56 * 2**20),
        cost_estimate=pl.CostEstimate(
            flops=4 * rows * width * hidden,
            bytes_accessed=8 * experts * width * hidden + 16 * rows * width,
            transcendentals=0,
        ),
        name="expert_grads",
    )(has, x, cot, eid, act, dbef)


def halves(pair):
    left = lax.broadcasted_iota(jnp.int32, pair.shape, 1) < HEAD_DIM
    zero = jnp.zeros_like(pair)
    return (jnp.where(left, pair, zero), jnp.where(left, zero, pair))


def join(first, second):
    left = lax.broadcasted_iota(jnp.int32, first.shape, 1) < HEAD_DIM
    return jnp.where(left, first, second)


def tri(block):
    later = lax.broadcasted_iota(jnp.int32, (block, block), 1)
    return later <= lax.broadcasted_iota(jnp.int32, (block, block), 0)


def normalise(values):
    centered = values - jnp.mean(values, -1, keepdims=True)
    spread = jnp.mean(centered * centered, -1, keepdims=True)
    root = lax.rsqrt(spread + EPS)
    return centered * root, root


def attend_kernel(
    tokens, w_q, w_k, w_v, w_o, gain1, bias1, gain2, bias2,
    residual, second, q_out, k_out, v_out, att_out, lse,
    normed,
):
    step = pl.program_id(0)
    rows = tokens.shape[0]
    lanes = 2 * HEAD_DIM

    @pl.when(step == 0)
    def _():
        source = tokens[...].astype(F32)
        normed[...] = (normalise(source)[0] * gain1[...] + bias1[...]).astype(BF)
        residual[...] = source
        lse[...] = jnp.zeros(lse.shape, F32)

    q_out[0] = dot(normed[...], w_q[...]).astype(BF)
    k_out[0] = dot(normed[...], w_k[...]).astype(BF)
    v_out[0] = dot(normed[...], w_v[...]).astype(BF)
    width = q_out.shape[2]
    keep = tri(BLOCK)
    lane = lax.broadcasted_iota(jnp.int32, (BLOCK, lse.shape[1]), 1)
    for pair in range(width // lanes):
        cols = slice(pair * lanes, (pair + 1) * lanes)
        query = q_out[0, :, cols] * jnp.asarray(HEAD_DIM**-0.5, BF)
        keys = halves(k_out[0, :, cols])
        values = v_out[0, :, cols]
        for q_block in range(rows // BLOCK):
            q_rows = slice(q_block * BLOCK, (q_block + 1) * BLOCK)
            results = []
            for head in range(2):
                scores = []
                for k_block in range(q_block + 1):
                    k_rows = slice(k_block * BLOCK, (k_block + 1) * BLOCK)
                    part = dot(query[q_rows], keys[head][k_rows], ((1,), (1,)))
                    scores.append(jnp.where(keep, part, -1e30) if k_block == q_block else part)
                top = functools.reduce(jnp.maximum, [jnp.max(s, -1, keepdims=True) for s in scores])
                weights = [jnp.exp(s - top) for s in scores]
                total = sum(jnp.sum(w, -1, keepdims=True) for w in weights)
                share = 1.0 / total
                out = sum(
                    dot((w * share).astype(BF), values[k * BLOCK : (k + 1) * BLOCK])
                    for k, w in enumerate(weights)
                )
                results.append(out)
                index = step * (width // HEAD_DIM) + 2 * pair + head
                lse[q_rows, :] = jnp.where(lane == index, top + jnp.log(total), lse[q_rows, :])
            att_out[0, q_rows, cols] = join(*results).astype(BF)
    residual[...] += dot(att_out[0], w_o[...])

    @pl.when(step == pl.num_programs(0) - 1)
    def _():
        second[...] = (normalise(residual[...])[0] * gain2[...] + bias2[...]).astype(BF)


def attend(tokens, project_in, project_out, gain1, bias1, gain2, bias2):
    rows, width = tokens.shape
    steps = width // QUAD
    whole = lambda shape: pl.BlockSpec(shape, lambda j: (0, 0))
    third = lambda k: pl.BlockSpec((width, QUAD), lambda j: (0, k * steps + j))
    cols = pl.BlockSpec((1, rows, QUAD), lambda j: (j, 0, 0))
    vector = whole((1, width))
    low = jax.ShapeDtypeStruct((rows, width), BF)
    split = jax.ShapeDtypeStruct((steps, rows, QUAD), BF)
    return pl.pallas_call(
        attend_kernel,
        grid=(steps,),
        in_specs=[whole((rows, width)), third(0), third(1), third(2),
            pl.BlockSpec((QUAD, width), lambda j: (j, 0)), vector, vector, vector, vector],
        out_specs=[whole((rows, width)), whole((rows, width)), cols, cols, cols, cols, whole((rows, 128))],
        out_shape=[jax.ShapeDtypeStruct((rows, width), F32), low, split, split, split, split,
            jax.ShapeDtypeStruct((rows, 128), F32)],
        scratch_shapes=[pltpu.VMEM((rows, width), BF)],
        compiler_params=pltpu.CompilerParams(vmem_limit_bytes=56 * 2**20),
        cost_estimate=pl.CostEstimate(flops=10 * rows * width * width, bytes_accessed=20 * 2**20,
            transcendentals=HEADS * rows * rows),
        name="attend",
    )(tokens, project_in, project_in, project_in, project_out, *(v.reshape(1, width) for v in (gain1, bias1, gain2, bias2)))


def layer_norm_back(d_normed, xhat, root, gain):
    scaled = d_normed * gain
    d_values = root * (
        scaled
        - jnp.mean(scaled, -1, keepdims=True)
        - xhat * jnp.mean(scaled * xhat, -1, keepdims=True)
    )
    sums = (jnp.sum(d_normed * xhat, 0, keepdims=True), jnp.sum(d_normed, 0, keepdims=True))
    return d_values, sums


def attend_back_kernel(
    tokens, residual, d_second, cot, q, k, v, att, lse, w_q, w_k, w_v, w_o, gain1, bias1, gain2,
    grad_tokens, grads,
    normed, d_branch, d_normed, small,
):
    step = pl.program_id(0)
    rows, width = tokens.shape
    lanes = 2 * HEAD_DIM
    scale = jnp.asarray(HEAD_DIM**-0.5, BF)

    @pl.when(step == 0)
    def _():
        xhat, root = normalise(residual[...])
        d_values, sums = layer_norm_back(d_second[...].astype(F32), xhat, root, gain2[...])
        d_residual = cot[...].astype(F32) + d_values
        grad_tokens[...] = d_residual
        d_branch[...] = d_residual.astype(BF)
        small[...] = jnp.zeros(small.shape, F32)
        small[2:3, :], small[3:4, :] = sums
        normed[...] = (
            normalise(tokens[...].astype(F32))[0] * gain1[...] + bias1[...]
        ).astype(BF)
        d_normed[...] = jnp.zeros(d_normed.shape, F32)

    quad = q.shape[2]
    place = lambda third: pl.ds(pl.multiple_of(third * width + step * quad, quad), quad)
    grads[pl.ds(pl.multiple_of(step * quad, quad), quad), 3 * width :] = dot(
        att[0], d_branch[...], ((0,), (0,))
    ).astype(BF)
    d_att = dot(d_branch[...], w_o[...], ((1,), (1,))).astype(BF)
    d_thirds = attention_back(step, q, k, v, d_att, lse, scale, lanes, 0)
    total = 0.0
    for third, (d_third, weight) in enumerate(zip(d_thirds, (w_q, w_k, w_v))):
        grads[:width, place(third)] = dot(normed[...], d_third, ((0,), (0,))).astype(BF)
        total = total + dot(d_third, weight[...], ((1,), (1,)))
    d_normed[...] += total

    @pl.when(step == pl.num_programs(0) - 1)
    def _():
        xhat, root = normalise(tokens[...].astype(F32))
        d_values, sums = layer_norm_back(d_normed[...], xhat, root, gain1[...])
        grad_tokens[...] += d_values
        small[0:1, :], small[1:2, :] = sums
        exact = small[...]
        high = exact.astype(BF)
        grads[width : width + 8, :width] = high
        grads[width + 8 :, :width] = (exact - high.astype(F32)).astype(BF)
        grads[width:, width:] = jnp.zeros((16, 3 * width), BF)


def attend_back(tokens, residual, d_second, cot, q, k, v, att, lse, project_in, project_out, gain1, bias1, gain2):
    rows, width = tokens.shape
    steps = width // QUAD
    whole = lambda shape: pl.BlockSpec(shape, lambda j: (0, 0))
    third = lambda k: pl.BlockSpec((width, QUAD), lambda j: (0, k * steps + j))
    cols = pl.BlockSpec((1, rows, QUAD), lambda j: (j, 0, 0))
    full, vector = whole((rows, width)), whole((1, width))
    return pl.pallas_call(
        attend_back_kernel,
        grid=(steps,),
        in_specs=[full, full, full, full, cols, cols, cols, cols, whole((rows, 128)),
            third(0), third(1), third(2), pl.BlockSpec((QUAD, width), lambda j: (j, 0)), vector, vector, vector],
        out_specs=[full, whole((width + 16, 4 * width))],
        out_shape=[jax.ShapeDtypeStruct((rows, width), F32), jax.ShapeDtypeStruct((width + 16, 4 * width), BF)],
        scratch_shapes=[pltpu.VMEM((rows, width), BF), pltpu.VMEM((rows, width), BF),
            pltpu.VMEM((rows, width), F32), pltpu.VMEM((8, width), F32)],
        compiler_params=pltpu.CompilerParams(vmem_limit_bytes=56 * 2**20),
        cost_estimate=pl.CostEstimate(flops=20 * rows * width * width, bytes_accessed=32 * 2**20,
            transcendentals=HEADS * rows * rows),
        name="attend_back",
    )(tokens, residual, d_second, cot, q, k, v, att, lse, project_in, project_in, project_in, project_out,
      *(x.reshape(1, width) for x in (gain1, bias1, gain2)))


MESH = pl.DeviceIdType.MESH


def remote(src, dst, send_sem, recv_sem, device):
    return pltpu.make_async_remote_copy(
        src_ref=src,
        dst_ref=dst,
        send_sem=send_sem,
        recv_sem=recv_sem,
        device_id=device,
        device_id_type=MESH,
    )


def ones_where(mask):
    return jnp.where(mask, 1.0, 0.0).astype(BF)


def pass_kernel(
    rows, pieces,
    x, place, target, target_rows, cot_in, eid, w_in, w_out,
    x_all, cot_all, act_o, dbef_o, part_o, d_second,
    slots, arrived, packed_x, packed_c, returned, d_part, from_down, from_up, x_tile, c_tile, stage,
    plane_send, plane_recv, back_send, back_recv, ag_send, ag_recv, rs_send, rs_down, rs_up, local_sem, stage_sem,
):
    me, plane = lax.axis_index("expert"), lax.axis_index("hidden")
    devices, chunk, width = slots.shape
    experts = w_in.shape[0]
    height = rows // pieces
    side = lax.div(plane, 2)
    r = plane + side * (3 - 2 * plane)
    middle = r == 1
    step = 1 - 2 * side
    up, down = {"hidden": plane + step}, {"hidden": plane - step}
    physical = lambda rel: rel + side * (3 - 2 * rel)
    part_of = lambda j: pl.ds(pl.multiple_of(j * height, 16), height)

    barrier = pltpu.get_barrier_semaphore()

    def greet(off, carry):
        peer = {"expert": lax.rem(me + off, devices)}
        pl.semaphore_signal(barrier, inc=1, device_id=peer, device_id_type=MESH)
        return carry

    lax.fori_loop(1, devices, greet, 0)
    pl.semaphore_signal(barrier, inc=1, device_id=up, device_id_type=MESH)

    @pl.when(middle)
    def _():
        pl.semaphore_signal(barrier, inc=1, device_id=down, device_id_type=MESH)

    pl.semaphore_wait(barrier, devices + r)

    def slots_of(device):
        row = lax.broadcasted_iota(jnp.int32, (chunk, x.shape[0]), 0) + device * chunk
        return dot(ones_where(row == place[...]), x[...]).astype(BF)

    def dispatch_copy(off, to, frm):
        return remote(
            slots.at[to], arrived.at[frm], plane_send.at[off], plane_recv.at[off], {"expert": to}
        )

    def dispatch(off, carry):
        peer = lax.rem(me + off, devices)
        slots[peer] = slots_of(peer)
        dispatch_copy(off, peer, me).start()
        return carry

    lax.fori_loop(1, devices, dispatch, 0)
    arrived[me] = slots_of(me)

    def pack(source, j):
        row = lax.broadcasted_iota(jnp.int32, (height, devices * chunk), 0) + j * height
        flat = source[...].reshape(devices * chunk, width)
        return dot(ones_where(row == target[...]), flat).astype(BF)

    alls, packs = (x_all, cot_all), (packed_x, packed_c)

    def gather_copy(kind, way, block, j, own):
        source = packs[kind].at[part_of(j)] if own else alls[kind].at[block, part_of(j)]
        return remote(
            source,
            alls[kind].at[block, part_of(j)],
            ag_send.at[kind, way, block, j],
            ag_recv.at[kind, block, j],
            down if way else up,
        )

    def send_own(kind, source):
        def body(j, carry):
            packs[kind][part_of(j)] = pack(source, j)
            gather_copy(kind, 0, plane, j, True).start()

            @pl.when(middle)
            def _():
                gather_copy(kind, 1, plane, j, True).start()

            return carry

        lax.fori_loop(0, pieces, body, 0)

    def keep_own(kind):
        return pltpu.make_async_copy(packs[kind], alls[kind].at[plane], local_sem.at[kind])

    send_own(1, cot_in)
    keep_own(1).start()

    def dispatch_done(off, carry):
        dispatch_copy(off, me, lax.rem(me - off + devices, devices)).wait_recv()
        return carry

    lax.fori_loop(1, devices, dispatch_done, 0)
    send_own(0, arrived)
    keep_own(0).start()
    keep_own(1).wait()
    keep_own(0).wait()

    def got(kind, rel, j):
        gather_copy(kind, 0, physical(rel), j, False).wait_recv()

    def relay(kind, rel, way, j):
        got(kind, rel, j)
        gather_copy(kind, way, physical(rel), j, False).start()

    def sum_copy(rel, j, buffer, index, sems, device):
        return remote(
            d_part.at[physical(rel), part_of(j)],
            buffer.at[index, part_of(j)],
            rs_send.at[rel, j],
            sems.at[index, j],
            device,
        )

    def add(rel, j, buffer, index, sems):
        sum_copy(rel, j, buffer, index, sems, up).wait_recv()
        block = physical(rel)
        here = d_part[block, part_of(j)].astype(F32)
        d_part[block, part_of(j)] = (here + buffer[index, part_of(j)].astype(F32)).astype(BF)

    outs = (act_o, dbef_o, part_o)

    def stage_copy(index, block, j):
        return pltpu.make_async_copy(
            stage.at[index], outs[index].at[block, part_of(j)], stage_sem.at[index]
        )

    def tile(p, j):
        @pl.when((p == 0) & middle)
        def _():
            relay(1, 0, 0, j)
            relay(1, 2, 1, j)

        @pl.when((p == 1) & middle)
        def _():
            relay(0, 0, 0, j)
            relay(0, 2, 1, j)
            relay(1, 3, 1, j)

        @pl.when((p == 2) & middle)
        def _():
            relay(0, 3, 1, j)

        @pl.when((p > 0) & (r == 0))
        def _():
            got(1, p, j)
            got(0, p, j)

        block = physical(jnp.where(p < 2, lax.rem(p + r, 2), p))
        loads = [
            pltpu.make_async_copy(a.at[block, part_of(j)], t, local_sem.at[i])
            for i, (a, t) in enumerate(((x_all, x_tile), (cot_all, c_tile)))
        ]
        for load in loads:
            load.start()
        for load in loads:
            load.wait()
        start = pl.multiple_of(block * rows + j * height, 16)
        owner = eid[pl.ds(start, height), :]
        mine = [owner == float(e) for e in range(experts)]

        def choose(results):
            total = jnp.where(mine[0], results[0], 0.0)
            for mask, result in zip(mine[1:], results[1:]):
                total = jnp.where(mask, result, total)
            return total

        before = choose([dot(x_tile[...], w_in[e]) for e in range(experts)])
        d_after = choose([dot(c_tile[...], w_out[e], ((1,), (1,))) for e in range(experts)])
        square = before * before
        tanh = jnp.tanh(0.7978845608028654 * before * (1.0 + 0.044715 * square))
        half = 0.5 * (1.0 + tanh)
        slope = half + 0.5 * before * (1.0 - tanh * tanh) * (
            0.7978845608028654 * (1.0 + 0.134145 * square)
        )

        @pl.when((p > 0) | (j > 0))
        def _():
            for index in range(3):
                stage_copy(index, block, j).wait()

        stage[0] = (before * half).astype(BF)
        stage[1] = (d_after * slope).astype(BF)
        d_part[block, part_of(j)] = choose(
            [dot(stage[1], w_in[e], ((1,), (1,))) for e in range(experts)]
        ).astype(BF)

        @pl.when((p > 0) & (r == 0))
        def _():
            sum_copy(p, j, from_down, p - 1, rs_down, up).start()

        @pl.when((p == 3) & middle)
        def _():
            add(2, j, from_down, 1, rs_down)
            sum_copy(2, j, from_up, 1, rs_up, up).start()

        stage[2] = choose([dot(stage[0], w_out[e]) for e in range(experts)]).astype(BF)
        for index in range(3):
            stage_copy(index, block, j).start()

    def phase(p, carry):
        return lax.fori_loop(0, pieces, lambda j, c: (tile(p, j), c)[1], carry)

    lax.fori_loop(0, 4, phase, 0)
    for index in range(3):
        stage_copy(index, plane, 0).wait()

    @pl.when(middle)
    def _():
        def body(j, carry):
            @pl.when(j < pieces)
            def _():
                add(3, j, from_down, 2, rs_down)
                sum_copy(3, j, from_up, 0, rs_up, up).start()

            @pl.when(j > 0)
            def _():
                add(0, j - 1, from_up, 0, rs_up)
                sum_copy(0, j - 1, from_up, 0, rs_up, down).start()

            return carry

        lax.fori_loop(0, pieces + 1, body, 0)

    def last(j, carry):
        @pl.when(middle)
        def _():
            add(1, j, from_down, 0, rs_down)
            add(1, j, from_up, 1, rs_up)

        @pl.when(r == 0)
        def _():
            add(0, j, from_up, 0, rs_up)

        return carry

    lax.fori_loop(0, pieces, last, 0)

    def dispatch_sent(off, carry):
        peer = lax.rem(me + off, devices)
        dispatch_copy(off, peer, me).wait_send()
        return carry

    lax.fori_loop(1, devices, dispatch_sent, 0)

    def back_slots(device):
        row = lax.broadcasted_iota(jnp.int32, (rows, chunk), 0)
        return dot(ones_where(row == target_rows[device]), d_part[plane], ((0,), (0,))).astype(BF)

    def back_copy(off, to, frm):
        return remote(
            slots.at[to], returned.at[frm], back_send.at[off], back_recv.at[off], {"expert": to}
        )

    def back(off, carry):
        peer = lax.rem(me + off, devices)
        slots[peer] = back_slots(peer)
        back_copy(off, peer, me).start()
        return carry

    lax.fori_loop(1, devices, back, 0)
    returned[me] = back_slots(me)

    def back_done(off, carry):
        back_copy(off, me, lax.rem(me - off + devices, devices)).wait_recv()
        return carry

    lax.fori_loop(1, devices, back_done, 0)
    slot = lax.broadcasted_iota(jnp.int32, (devices * chunk, x.shape[0]), 0)
    flat = returned[...].reshape(devices * chunk, width)
    d_second[...] = dot(ones_where(slot == place[...]), flat, ((0,), (0,))).astype(BF)

    def back_sent(off, carry):
        back_copy(off, lax.rem(me + off, devices), me).wait_send()
        return carry

    lax.fori_loop(1, devices, back_sent, 0)

    def sent(j, carry):
        for kind in range(2):
            gather_copy(kind, 0, plane, j, True).wait_send()

        @pl.when(middle)
        def _():
            for kind in range(2):
                gather_copy(kind, 1, plane, j, True).wait_send()
                gather_copy(kind, 0, physical(0), j, False).wait_send()
                for rel in (2, 3):
                    gather_copy(kind, 1, physical(rel), j, False).wait_send()
            for rel in (0, 2, 3):
                sum_copy(rel, j, from_up, 0, rs_up, up).wait_send()

        @pl.when(r == 0)
        def _():
            for rel in (1, 2, 3):
                sum_copy(rel, j, from_up, 0, rs_up, up).wait_send()

        return carry

    lax.fori_loop(0, pieces, sent, 0)


def expert_pass(rows, pieces, number, x, place, target, cot_in, eid, w_in, w_out):
    devices, chunk, width = cot_in.shape
    hidden = w_in.shape[2]
    planes = eid.shape[0] // rows
    height = rows // pieces
    here, there = pl.BlockSpec(memory_space=pltpu.VMEM), pl.BlockSpec(memory_space=pl.ANY)
    dma = pltpu.SemaphoreType.DMA
    wide = jax.ShapeDtypeStruct((planes, rows, width), BF)
    return pl.pallas_call(
        functools.partial(pass_kernel, rows, pieces),
        in_specs=[here] * 8,
        out_specs=[there] * 5 + [here],
        out_shape=[wide] * 5 + [jax.ShapeDtypeStruct(x.shape, BF)],
        scratch_shapes=[
            pltpu.VMEM((devices, chunk, width), BF),
            pltpu.VMEM((devices, chunk, width), BF),
            pltpu.VMEM((rows, width), BF),
            pltpu.VMEM((rows, width), BF),
            pltpu.VMEM((devices, chunk, width), BF),
            pltpu.VMEM((planes, rows, width), BF),
            pltpu.VMEM((3, rows, width), BF),
            pltpu.VMEM((2, rows, width), BF),
            pltpu.VMEM((height, width), BF),
            pltpu.VMEM((height, width), BF),
            pltpu.VMEM((3, height, hidden), BF),
            dma((devices,)),
            dma((devices,)),
            dma((devices,)),
            dma((devices,)),
            dma((2, 2, planes, pieces)),
            dma((2, planes, pieces)),
            dma((planes, pieces)),
            dma((3, pieces)),
            dma((2, pieces)),
            dma((2,)),
            dma((3,)),
        ],
        compiler_params=pltpu.CompilerParams(
            collective_id=number, has_side_effects=True, vmem_limit_bytes=62 * 2**20
        ),
        cost_estimate=pl.CostEstimate(
            flops=16 * planes * rows * width * hidden,
            bytes_accessed=16 * planes * rows * width,
            transcendentals=planes * rows * hidden,
        ),
        name="expert_pass",
    )(x, place.reshape(1, -1), target.reshape(1, -1), target.reshape(devices, 1, chunk), cot_in, eid, w_in, w_out)


def tail_kernel(
    tokens, residual, d_second, cot, q, k, v, att, lse, project_in, project_out, gain1, bias1, gain2,
    grad_tokens, summed_grads, small_out,
    w_in, w_out, normed, d_branch, d_normed, grads, small, small_plane, small_near, small_far,
    core_buf, half_buf, plane_buf,
    ar_send, ar_recv, near_send, near_recv, far_send, far_recv,
    w_sem, local_sem,
):
    me, plane = lax.axis_index("expert"), lax.axis_index("hidden")
    devices, planes = lax.axis_size("expert"), lax.axis_size("hidden")
    width = tokens.shape[1]
    quads, tall, quad = grads.shape
    other = lambda off: {"expert": lax.rem(me + off, devices)}
    across = lambda off: {"hidden": lax.rem(plane + off, planes)}

    barrier = pltpu.get_barrier_semaphore()

    def greet(off, carry):
        pl.semaphore_signal(barrier, inc=1, device_id=other(off), device_id_type=MESH)
        return carry

    lax.fori_loop(1, devices, greet, 0)
    for off in range(1, planes):
        pl.semaphore_signal(barrier, inc=1, device_id=across(off), device_id_type=MESH)

    def weights(j, slot):
        cols = lambda third: pl.ds(pl.multiple_of(third * width + j * quad, quad), quad)
        copies = [
            pltpu.make_async_copy(project_in.at[:, cols(third)], w_in.at[slot, third], w_sem.at[slot, third])
            for third in range(3)
        ]
        rows_out = pl.ds(pl.multiple_of(j * quad, quad), quad)
        copies.append(pltpu.make_async_copy(project_out.at[rows_out], w_out.at[slot], w_sem.at[slot, 3]))
        return copies

    for copy in weights(0, 0):
        copy.start()
    pl.semaphore_wait(barrier, devices - 1 + planes - 1)

    bits = devices.bit_length() - 1
    bit = lambda i: lax.rem(lax.div(me, 1 << i), 2)
    partner = lambda i: {"expert": me + (1 << i) * (1 - 2 * bit(i))}
    half = tall // 2
    part = half // 2
    orders = [list(range(1, bits)), list(range(bits - 1, 0, -1))]
    levels = bits - 1
    last = part >> levels
    slice_len = last // planes

    def segment(a, level):
        start = bit(0) * half + a * part
        for i in range(level):
            start = start + bit(orders[a][i]) * (part >> (i + 1))
        return start

    def span(start, length):
        return pl.ds(pl.multiple_of(start, 16), length)

    slot_of = {}

    def sems(name, c):
        index = slot_of.setdefault(name, len(slot_of))
        return ar_send.at[index, c], ar_recv.at[index, c]

    def core_copy(c):
        source = grads.at[c, span((1 - bit(0)) * half, half)]
        return [remote(source, core_buf.at[c], *sems("core", c), partner(0))]

    def core_end(c):
        keep = span(bit(0) * half, half)
        grads[c, keep] = (grads[c, keep].astype(F32) + core_buf[c].astype(F32)).astype(BF)

    def halve_copy(level, c):
        copies = []
        length = part >> (level + 1)
        for a in range(2):
            i = orders[a][level]
            source = grads.at[c, span(segment(a, level) + (1 - bit(i)) * length, length)]
            buffer = half_buf.at[c, a, pl.ds(part - (part >> level), length)]
            copies.append(remote(source, buffer, *sems(("half", level, a), c), partner(i)))
        return copies

    def halve_end(level, c):
        length = part >> (level + 1)
        for a in range(2):
            keep = span(segment(a, level + 1), length)
            other_half = half_buf[c, a, pl.ds(part - (part >> level), length)]
            grads[c, keep] = (grads[c, keep].astype(F32) + other_half.astype(F32)).astype(BF)

    def plane_span(a, p):
        return span(segment(a, levels) + p * slice_len, slice_len)

    def plane_copy(c):
        copies = []
        for a in range(2):
            for off in range(1, planes):
                source = grads.at[c, plane_span(a, lax.rem(plane + off, planes))]
                buffer = plane_buf.at[c, a, off - 1]
                copies.append(remote(source, buffer, *sems(("plane", a, off), c), across(off)))
        return copies

    def plane_end(c):
        for a in range(2):
            keep = plane_span(a, plane)
            total = grads[c, keep].astype(F32)
            for off in range(planes - 1):
                total = total + plane_buf[c, a, off].astype(F32)
            grads[c, keep] = total.astype(BF)
        copies = [
            pltpu.make_async_copy(
                grads.at[c, plane_span(a, plane)],
                summed_grads.at[c, plane_span(a, plane)],
                local_sem.at[a],
            )
            for a in range(2)
        ]
        for copy in copies:
            copy.start()
        for copy in copies:
            copy.wait()

    def spread_copy(c):
        copies = []
        for a in range(2):
            for off in range(1, planes):
                keep = plane_span(a, plane)
                source, there = grads.at[c, keep], summed_grads.at[c, keep]
                copies.append(remote(source, there, *sems(("spread", a, off), c), across(off)))
        return copies

    def double_copy(level, c):
        copies = []
        for a in range(2):
            have = summed_grads.at[c, span(segment(a, level + 1), part >> (level + 1))]
            names = sems(("double", level, a), c)
            copies.append(remote(have, have, *names, partner(orders[a][level])))
        return copies

    def core_back_copy(c):
        have = summed_grads.at[c, span(bit(0) * half, half)]
        return [remote(have, have, *sems("core_back", c), partner(0))]

    nothing = lambda c: None
    stages = [(core_copy, core_end)]
    for level in range(levels):
        stages.append((functools.partial(halve_copy, level), functools.partial(halve_end, level)))
    stages.append((plane_copy, plane_end))
    stages.append((spread_copy, nothing))
    for level in reversed(range(levels)):
        stages.append((functools.partial(double_copy, level), nothing))
    stages.append((core_back_copy, nothing))

    def finish(stage, c):
        copies, end = stages[stage]
        for copy in copies(c):
            copy.wait_recv()
        for copy in copies(c):
            copy.wait_send()
        end(c)

    def near_copy(off):
        return remote(
            small, small_near.at[off - 1], near_send.at[off - 1], near_recv.at[off - 1], other(off)
        )

    def far_copy(off):
        return remote(
            small_plane, small_far.at[off - 1], far_send.at[off - 1], far_recv.at[off - 1], across(off)
        )

    def each_near(act):
        def body(off, carry):
            act(near_copy(off))
            return carry

        lax.fori_loop(1, devices, body, 0)

    scale = jnp.asarray(HEAD_DIM**-0.5, BF)
    lanes = 2 * HEAD_DIM
    xhat2, root2 = normalise(residual[...])
    d_values, sums = layer_norm_back(d_second[...].astype(F32), xhat2, root2, gain2[...])
    d_residual = cot[...].astype(F32) + d_values
    grad_tokens[...] = d_residual
    d_branch[...] = d_residual.astype(BF)
    small[...] = jnp.zeros(small.shape, F32)
    small[2:3, :], small[3:4, :] = sums
    normed[...] = (normalise(tokens[...].astype(F32))[0] * gain1[...] + bias1[...]).astype(BF)
    d_normed[...] = jnp.zeros(d_normed.shape, F32)

    def quarter(j):
        slot = lax.rem(j, 2)
        for copy in weights(j, slot):
            copy.wait()

        @pl.when(j < quads - 1)
        def _():
            for copy in weights(j + 1, 1 - slot):
                copy.start()

        out = dot(att[j], d_branch[...], ((0,), (0,))).astype(BF)
        for m in range(width // quad):
            grads[j, 3 * width + m * quad : 3 * width + (m + 1) * quad] = out[:, m * quad : (m + 1) * quad]
        d_att = dot(d_branch[...], w_out[slot], ((1,), (1,))).astype(BF)
        d_thirds = attention_back(j, q, k, v, d_att, lse, scale, lanes)
        total = 0.0
        for third, d_third in enumerate(d_thirds):
            grads[j, third * width : (third + 1) * width] = dot(
                normed[...], d_third, ((0,), (0,))
            ).astype(BF)
            total = total + dot(d_third, w_in[slot, third], ((1,), (1,)))
        d_normed[...] += total

        @pl.when(j == quads - 1)
        def _():
            xhat, root = normalise(tokens[...].astype(F32))
            d_first, first_sums = layer_norm_back(d_normed[...], xhat, root, gain1[...])
            grad_tokens[...] += d_first
            small[0:1, :], small[1:2, :] = first_sums

    count = len(stages)

    def tick(t, carry):
        @pl.when(t < quads)
        def _():
            quarter(t)
            for copy in stages[0][0](t):
                copy.start()

        for stage in range(count, 0, -1):
            c = t - stage

            @pl.when((c >= 0) & (c < quads))
            def _(stage=stage, c=c):
                finish(stage - 1, c)
                if stage < count:
                    for copy in stages[stage][0](c):
                        copy.start()

        @pl.when(t == quads - 1)
        def _():
            each_near(lambda copy: copy.start())

        @pl.when(t == quads + 1)
        def _():
            each_near(lambda copy: copy.wait_recv())
            each_near(lambda copy: copy.wait_send())
            total = small[...]
            for off in range(devices - 1):
                total = total + small_near[off]
            small_plane[...] = total
            for off in range(1, planes):
                far_copy(off).start()

        @pl.when(t == quads + 3)
        def _():
            for off in range(1, planes):
                far_copy(off).wait_recv()
            for off in range(1, planes):
                far_copy(off).wait_send()
            total = small_plane[...]
            for off in range(planes - 1):
                total = total + small_far[off]
            small_out[...] = total

        return carry

    lax.fori_loop(0, quads + count, tick, 0)


def attention_back(j, q, k, v, d_att, lse, scale, lanes, at=None):
    at = j if at is None else at
    rows, quad = d_att.shape
    keep = tri(BLOCK)
    blocks = rows // BLOCK
    cut = lambda array, block: array[block * BLOCK : (block + 1) * BLOCK]
    d_q, d_k, d_v = [], [], []
    lane = lax.broadcasted_iota(jnp.int32, (BLOCK, lse.shape[1]), 1)
    for pair in range(quad // lanes):
        cols = slice(pair * lanes, (pair + 1) * lanes)
        query = q[at, :, cols] * scale
        key, value, d_pair = k[at, :, cols], v[at, :, cols], d_att[:, cols]
        keys, values = halves(key), halves(value)
        pair_q, pair_k, pair_v = [], [], []
        for head in range(2):
            index = j * (quad // HEAD_DIM) + 2 * pair + head
            q_parts = []
            k_parts, v_parts = [0.0] * blocks, [0.0] * blocks
            for q_block in range(blocks):
                level = jnp.sum(
                    jnp.where(lane == index, lse[q_block * BLOCK : (q_block + 1) * BLOCK, :], 0.0),
                    -1,
                    keepdims=True,
                )
                shares, d_shares, inner = [], [], 0.0
                for k_block in range(q_block + 1):
                    scores = dot(cut(query, q_block), cut(keys[head], k_block), ((1,), (1,)))
                    share = jnp.exp(scores - level)
                    if k_block == q_block:
                        share = jnp.where(keep, share, 0.0)
                    d_share = dot(cut(d_pair, q_block), cut(values[head], k_block), ((1,), (1,)))
                    inner = inner + jnp.sum(share * d_share, -1, keepdims=True)
                    shares.append(share)
                    d_shares.append(d_share)
                total = 0.0
                for k_block in range(q_block + 1):
                    d_scores = (shares[k_block] * (d_shares[k_block] - inner)).astype(BF)
                    total = total + dot(d_scores, cut(key, k_block))
                    k_parts[k_block] += dot(d_scores, cut(query, q_block), ((0,), (0,)))
                    v_parts[k_block] += dot(
                        shares[k_block].astype(BF), cut(d_pair, q_block), ((0,), (0,))
                    )
                q_parts.append(total * HEAD_DIM**-0.5)
            pair_q.append(jnp.concatenate(q_parts, 0))
            pair_k.append(jnp.concatenate(k_parts, 0))
            pair_v.append(jnp.concatenate(v_parts, 0))
        d_q.append(join(*pair_q).astype(BF))
        d_k.append(join(*pair_k).astype(BF))
        d_v.append(join(*pair_v).astype(BF))
    return [jnp.concatenate(parts, 1) for parts in (d_q, d_k, d_v)]


def tail(
    number, devices, planes, tokens, residual, d_second, cot, q, k, v, att, lse, project_in, project_out,
    gain1, bias1, gain2,
):
    tokens_dev, width = tokens.shape
    quads, _, quad = q.shape
    tall = 4 * width
    bits = devices.bit_length() - 1
    part = tall // 4
    slice_len = (part >> (bits - 1)) // planes
    slots = 2 + 4 * (bits - 1) + 4 * (planes - 1)
    here, there = pl.BlockSpec(memory_space=pltpu.VMEM), pl.BlockSpec(memory_space=pl.ANY)
    dma = pltpu.SemaphoreType.DMA
    low = lambda *shape: pltpu.VMEM(shape, BF)
    full = lambda *shape: pltpu.VMEM(shape, F32)
    return pl.pallas_call(
        tail_kernel,
        in_specs=[here] * 9 + [there] * 2 + [here] * 3,
        out_specs=[here, there, here],
        out_shape=[
            jax.ShapeDtypeStruct((tokens_dev, width), F32),
            jax.ShapeDtypeStruct((quads, tall, quad), BF),
            jax.ShapeDtypeStruct((8, width), F32),
        ],
        scratch_shapes=[
            low(2, 3, width, quad),
            low(2, quad, width),
            low(tokens_dev, width),
            low(tokens_dev, width),
            full(tokens_dev, width),
            low(quads, tall, quad),
            full(8, width),
            full(8, width),
            full(devices - 1, 8, width),
            full(planes - 1, 8, width),
            low(quads, tall // 2, quad),
            low(quads, 2, part - (part >> (bits - 1)), quad),
            low(quads, 2, planes - 1, slice_len, quad),
            dma((slots, quads)),
            dma((slots, quads)),
            dma((devices - 1,)),
            dma((devices - 1,)),
            dma((planes - 1,)),
            dma((planes - 1,)),
            dma((2, 4)),
            dma((2,)),
        ],
        compiler_params=pltpu.CompilerParams(
            collective_id=number, has_side_effects=True, vmem_limit_bytes=62 * 2**20
        ),
        cost_estimate=pl.CostEstimate(
            flops=20 * tokens_dev * width * width,
            bytes_accessed=64 * 2**20,
            transcendentals=HEADS * tokens_dev * tokens_dev,
        ),
        name="tail",
    )(
        tokens, residual, d_second, cot, q, k, v, att, lse, project_in, project_out,
        *(x.reshape(1, width) for x in (gain1, bias1, gain2)),
    )


def spread_kernel(summed, grad_in, grad_out):
    third = pl.program_id(1)

    @pl.when(third < 3)
    def _():
        grad_in[...] = summed[0].astype(F32)

    @pl.when(third == 3)
    def _():
        quad = summed.shape[2]
        for m in range(grad_out.shape[1] // quad):
            rows = slice(m * quad, (m + 1) * quad)
            grad_out[:, rows] = summed[0, rows].astype(F32)


def spread(summed):
    quads, tall, quad = summed.shape
    width = tall // 4
    return pl.pallas_call(
        spread_kernel,
        grid=(quads, 4),
        in_specs=[pl.BlockSpec((1, width, quad), lambda j, t: (j, t, 0))],
        out_specs=[
            pl.BlockSpec((width, quad), lambda j, t: (0, jnp.minimum(t, 2) * quads + j)),
            pl.BlockSpec((quad, width), lambda j, t: (j, 0)),
        ],
        out_shape=[
            jax.ShapeDtypeStruct((width, 3 * width), F32),
            jax.ShapeDtypeStruct((width, width), F32),
        ],
        compiler_params=pltpu.CompilerParams(vmem_limit_bytes=40 * 2**20),
        name="spread",
    )(summed)


def census_kernel(counts, out, near_send, near_recv, far_send, far_recv):
    me, plane = lax.axis_index("expert"), lax.axis_index("hidden")
    planes, devices = out.shape[:2]
    other = lambda off: {"expert": lax.rem(me + off, devices)}
    across = lambda off: {"hidden": lax.rem(plane + off, planes)}
    barrier = pltpu.get_barrier_semaphore()
    for off in range(1, devices):
        pl.semaphore_signal(barrier, inc=1, device_id=other(off), device_id_type=MESH)
    for off in range(1, planes):
        pl.semaphore_signal(barrier, inc=1, device_id=across(off), device_id_type=MESH)
    out[plane, me] = counts[...]
    pl.semaphore_wait(barrier, devices + planes - 2)

    def near(off, source):
        piece = out.at[plane, source]
        return remote(piece, piece, near_send.at[off], near_recv.at[off], other(off))

    def far(off, source):
        piece = out.at[source]
        return remote(piece, piece, far_send.at[off], far_recv.at[off], across(off))

    for off in range(1, devices):
        near(off, me).start()
    for off in range(1, devices):
        near(off, lax.rem(me - off + devices, devices)).wait_recv()
    for off in range(1, planes):
        far(off, plane).start()
    for off in range(1, planes):
        far(off, lax.rem(plane - off + planes, planes)).wait_recv()
    for off in range(1, devices):
        near(off, me).wait_send()
    for off in range(1, planes):
        far(off, plane).wait_send()


def census(counts, devices, planes):
    here = pl.BlockSpec(memory_space=pltpu.VMEM)
    dma = pltpu.SemaphoreType.DMA
    tile = jnp.zeros((8, 128), jnp.int32).at[0, : counts.shape[0]].set(counts)
    out = pl.pallas_call(
        census_kernel,
        in_specs=[here],
        out_specs=here,
        out_shape=jax.ShapeDtypeStruct((planes, devices, 8, 128), jnp.int32),
        scratch_shapes=[dma((devices,)), dma((devices,)), dma((planes,)), dma((planes,))],
        compiler_params=pltpu.CompilerParams(collective_id=0, has_side_effects=True),
        name="census",
    )(tile)
    return out[:, :, 0, : counts.shape[0]]


def on_device(
    tokens,
    token_ids,
    hash_table,
    first_gain,
    first_bias,
    project_in,
    project_out,
    second_gain,
    second_bias,
    expert_in,
    expert_out,
    cotangent,
):
    rows_dev, width = tokens.shape
    expert_devs = lax.axis_size("expert")
    hidden_devs = lax.axis_size("hidden")
    local = expert_in.shape[0]
    experts = local * expert_devs
    capacity = 8 * ((3 * rows_dev + 8 * experts - 1) // (8 * experts))
    chunk = local * capacity

    owner = hash_table.at[token_ids].get(mode="promise_in_bounds")
    expert_ids = jnp.arange(experts, dtype=jnp.int32)
    onehot = owner[:, None] == expert_ids[None, :]
    earlier = lax.broadcasted_iota(jnp.int32, (rows_dev, rows_dev), 1) < lax.broadcasted_iota(
        jnp.int32, (rows_dev, rows_dev), 0
    )
    before_count = jnp.dot(earlier.astype(BF), onehot.astype(BF), preferred_element_type=F32)
    counts = jnp.sum(onehot.astype(jnp.int32), 0)
    grouped = counts.reshape(expert_devs, local)
    first_slot = (
        jnp.cumsum(grouped, 1) - grouped + jnp.arange(expert_devs, dtype=jnp.int32)[:, None] * chunk
    ).reshape(experts)
    place = jnp.sum(
        jnp.where(onehot, before_count.astype(jnp.int32) + first_slot[None, :], 0), 1
    )
    all_counts = census(counts, expert_devs, hidden_devs).reshape(
        hidden_devs, expert_devs, expert_devs, local
    )
    group = lax.axis_index("expert")
    plane = lax.axis_index("hidden")
    group_counts = lax.dynamic_index_in_dim(all_counts, group, 2, keepdims=False)
    most = jnp.max(jnp.sum(all_counts, (1, 3)))

    def run(rows, pieces, number):
        send = (
            place[None, :] == jnp.arange(expert_devs * chunk, dtype=jnp.int32)[:, None]
        ).astype(BF)

        mine = lax.dynamic_index_in_dim(group_counts, plane, 0, keepdims=False)
        starts = jnp.cumsum(mine, 1) - mine
        totals = jnp.sum(mine, 0)
        bases = jnp.cumsum(mine, 0) - mine + (jnp.cumsum(totals) - totals)[None, :]
        slot = jnp.arange(chunk, dtype=jnp.int32)[None, :]
        target = jnp.full((expert_devs, chunk), -1, jnp.int32)
        for l in range(local):
            offset = slot - starts[:, l : l + 1]
            target = jnp.where(
                (offset >= 0) & (offset < mine[:, l : l + 1]), bases[:, l : l + 1] + offset, target
            )
        target = target.reshape(-1)
        pack = (target[None, :] == jnp.arange(rows, dtype=jnp.int32)[:, None]).astype(BF)
        plane_totals = jnp.sum(group_counts, 1)
        ends = jnp.cumsum(plane_totals, 1)
        row = jnp.arange(rows, dtype=jnp.int32)[None, :]
        eid = jnp.zeros((hidden_devs, rows), jnp.int32)
        for l in range(local):
            eid = eid + (row >= ends[:, l : l + 1]).astype(jnp.int32)
        eid = eid.reshape(-1, 1)
        has = jnp.stack(
            [jnp.any((eid == l).reshape(-1, TILE), 1).astype(jnp.int32) for l in range(local)], 1
        )
        eid = eid.astype(F32)

        def dispatch(values):
            slots = jnp.dot(send, values, preferred_element_type=F32).astype(BF)
            arrived = lax.all_to_all(
                slots.reshape(expert_devs, chunk, width), "expert", 0, 0, tiled=True
            )
            packed = jnp.dot(
                pack, arrived.reshape(-1, width), preferred_element_type=F32
            ).astype(BF)
            return lax.all_gather(packed, "hidden", axis=0, tiled=True)

        def give_back(partial):
            summed = lax.psum_scatter(partial, "hidden", scatter_dimension=0, tiled=True)
            return collect(dot(pack, summed, ((0,), (0,))).astype(BF))

        def collect(slots):
            returned = lax.all_to_all(
                slots.reshape(expert_devs, chunk, width), "expert", 0, 0, tiled=True
            )
            return dot(send, returned.reshape(-1, width), ((0,), (0,))).astype(BF)

        special = hidden_devs == 4 and rows < expert_devs * chunk
        if not special:
            cot_rows = dispatch(cotangent)

        residual, second, query, keys, values, attended, lse = attend(
            tokens, project_in, project_out, first_gain, first_bias, second_gain, second_bias
        )
        if special:
            cot_slots = jnp.dot(send, cotangent, preferred_element_type=F32).astype(BF)
            cot_arrived = lax.all_to_all(
                cot_slots.reshape(expert_devs, chunk, width), "expert", 0, 0, tiled=True
            )
            *wide, d_second = expert_pass(
                rows, pieces, number, second, place, target, cot_arrived, eid, expert_in, expert_out
            )
            x_rows, cot_rows, act, dbef, part = (w.reshape(-1, width) for w in wide)
            grad_tokens, summed, small = tail(
                number + 8, expert_devs, hidden_devs, tokens, residual, d_second, cotangent, query, keys, values,
                attended, lse, project_in, project_out, first_gain, first_bias, second_gain,
            )
            own = lax.psum_scatter(part, "hidden", scatter_dimension=0, tiled=True)
            own, summed = lax.optimization_barrier((own, summed))
            slots = dot(pack, own, ((0,), (0,))).astype(BF)
            slots, act = lax.optimization_barrier((slots, act))
            produced = collect(slots)
            grad_in, grad_out = spread(summed)
        else:
            x_rows = dispatch(second)
            act, dbef, part, dmem = expert_rows(x_rows, cot_rows, eid, has, expert_in, expert_out)
            d_second = give_back(dmem)
            produced = give_back(part)
            grad_tokens, flat = attend_back(
                tokens, residual, d_second, cotangent, query, keys, values, attended, lse,
                project_in, project_out, first_gain, first_bias, second_gain,
            )
            flat = lax.psum(flat, ("expert", "hidden")).astype(F32)
            grad_in, grad_out = flat[:width, : 3 * width], flat[:width, 3 * width :]
            small = flat[width : width + 8, :width] + flat[width + 8 :, :width]
        grad_expert_in, grad_expert_out = expert_grads(x_rows, cot_rows, eid, has, act, dbef)
        block_out = (residual + produced.astype(F32)).astype(BF)
        return (
            block_out,
            grad_tokens,
            small[0],
            small[1],
            grad_in,
            grad_out,
            small[2],
            small[3],
            grad_expert_in,
            grad_expert_out,
        )

    most_rows = expert_devs * chunk
    plans = [(768, 3, 1), (832, 4, 2), (896, 4, 3)]
    plans = [plan for plan in plans if plan[0] < most_rows] + [(most_rows, 0, 0)]
    pick = sum((most > plan[0]).astype(jnp.int32) for plan in plans[:-1])
    return lax.switch(pick, [functools.partial(run, *plan) for plan in plans])


def solution(mesh):
    rows = P(("expert", "hidden"), None)
    w_in, w_out = P("expert", None, "hidden"), P("expert", "hidden", None)
    return jax.shard_map(
        on_device,
        mesh=mesh,
        in_specs=(
            rows,
            P(("expert", "hidden")),
            P(),
            P(),
            P(),
            P(),
            P(),
            P(),
            P(),
            w_in,
            w_out,
            rows,
        ),
        out_specs=(rows, rows, P(), P(), P(), P(), P(), P(), w_in, w_out),
        check_vma=False,
    )
```

```python
import functools

import jax
import jax.numpy as jnp
from jax import lax
from jax.experimental import pallas as pl
from jax.experimental.pallas import tpu as pltpu
from jax.sharding import PartitionSpec as P

HEADS = 16
HEAD_DIM = 64
TILE = 256
BLOCK = 256
QUAD = 256
EPS = 1e-05
BF = jnp.bfloat16
F32 = jnp.float32


def dot(a, b, dims=((1,), (0,))):
    return lax.dot_general(a, b, (dims, ((), ())), preferred_element_type=F32)


def expert_kernel(local_experts, has, x, cot, eid, w_in, w_out, act_o, dbef_o, part_o, dmem_o):
    tile = pl.program_id(0)
    outs = (act_o, dbef_o, part_o, dmem_o)

    @pl.when(has[tile, 0] == 0)
    def _():
        for out in outs:
            out[...] = jnp.zeros(out.shape, out.dtype)

    for expert in range(local_experts):

        @pl.when(has[tile, expert] > 0)
        def _(expert=expert):
            mine = eid[...] == float(expert)
            before = dot(x[...], w_in[expert])
            d_after = dot(cot[...], w_out[expert], ((1,), (1,)))
            square = before * before
            inner = 0.7978845608028654 * before * (1.0 + 0.044715 * square)
            tanh = jnp.tanh(inner)
            half = 0.5 * (1.0 + tanh)
            act = (before * half).astype(BF)
            slope = half + 0.5 * before * (1.0 - tanh * tanh) * (
                0.7978845608028654 * (1.0 + 0.134145 * square)
            )
            dbef = (d_after * slope).astype(BF)
            part = dot(act, w_out[expert])
            dmem = dot(dbef, w_in[expert], ((1,), (1,)))
            news = (act.astype(F32), dbef.astype(F32), part, dmem)
            for out, new in zip(outs, news):
                old = 0.0 if expert == 0 else out[...].astype(F32)
                out[...] = jnp.where(mine, new, old).astype(BF)


def expert_rows(x, cot, eid, has, w_in, w_out):
    rows, width = x.shape
    experts, _, hidden = w_in.shape
    tiles = rows // TILE
    row_block = pl.BlockSpec((TILE, width), lambda t, has: (t, 0))
    hid_block = pl.BlockSpec((TILE, hidden), lambda t, has: (t, 0))
    whole = lambda shape: pl.BlockSpec(shape, lambda t, has: (0, 0, 0), pipeline_mode=pl.Buffered(1))
    return pl.pallas_call(
        functools.partial(expert_kernel, experts),
        grid_spec=pltpu.PrefetchScalarGridSpec(
            num_scalar_prefetch=1,
            grid=(tiles,),
            in_specs=[
                row_block,
                row_block,
                pl.BlockSpec((TILE, 1), lambda t, has: (t, 0)),
                whole(w_in.shape),
                whole(w_out.shape),
            ],
            out_specs=[hid_block, hid_block, row_block, row_block],
        ),
        out_shape=[
            jax.ShapeDtypeStruct((rows, hidden), BF),
            jax.ShapeDtypeStruct((rows, hidden), BF),
            jax.ShapeDtypeStruct((rows, width), BF),
            jax.ShapeDtypeStruct((rows, width), BF),
        ],
        compiler_params=pltpu.CompilerParams(vmem_limit_bytes=56 * 2**20),
        cost_estimate=pl.CostEstimate(
            flops=8 * rows * width * hidden,
            bytes_accessed=2 * (w_in.size + w_out.size + 6 * rows * width),
            transcendentals=rows * hidden,
        ),
        name="expert_rows",
    )(has, x, cot, eid, w_in, w_out)


def expert_grad_kernel(owner, tile, count, x, cot, eid, act, dbef, g_in, g_out):
    visit = pl.program_id(0)
    expert = owner[visit]

    @pl.when((visit == 0) | (owner[jnp.maximum(visit - 1, 0)] != expert))
    def _():
        g_in[...] = jnp.zeros(g_in.shape, F32)
        g_out[...] = jnp.zeros(g_out.shape, F32)

    @pl.when(visit < count[0])
    def _():
        mine = jnp.where(eid[...] == expert.astype(F32), 1.0, 0.0).astype(BF)
        g_in[0] += dot(x[...], dbef[...] * mine, ((0,), (0,)))
        g_out[0] += dot(act[...] * mine, cot[...], ((0,), (0,)))


def expert_grads(x, cot, eid, has, act, dbef):
    rows, width = x.shape
    hidden = act.shape[1]
    tiles, experts = has.shape
    wanted = has.at[0].set(1).T.reshape(-1)
    order = jnp.cumsum(wanted) - 1
    most = tiles + experts * 4
    count = jnp.sum(wanted).reshape(1)
    visit = jnp.minimum(jnp.arange(most, dtype=jnp.int32), count - 1)
    chosen = (wanted[None, :] > 0) & (order[None, :] == visit[:, None])
    index = jnp.sum(jnp.where(chosen, jnp.arange(tiles * experts, dtype=jnp.int32)[None, :], 0), 1)
    owner, tile = index // tiles, index % tiles
    row_block = pl.BlockSpec((TILE, width), lambda v, owner, tile, count: (tile[v], 0))
    hid_block = pl.BlockSpec((TILE, hidden), lambda v, owner, tile, count: (tile[v], 0))
    return pl.pallas_call(
        expert_grad_kernel,
        grid_spec=pltpu.PrefetchScalarGridSpec(
            num_scalar_prefetch=3,
            grid=(most,),
            in_specs=[
                row_block,
                row_block,
                pl.BlockSpec((TILE, 1), lambda v, owner, tile, count: (tile[v], 0)),
                hid_block,
                hid_block,
            ],
            out_specs=[
                pl.BlockSpec((1, width, hidden), lambda v, owner, tile, count: (owner[v], 0, 0)),
                pl.BlockSpec((1, hidden, width), lambda v, owner, tile, count: (owner[v], 0, 0)),
            ],
        ),
        out_shape=[
            jax.ShapeDtypeStruct((experts, width, hidden), F32),
            jax.ShapeDtypeStruct((experts, hidden, width), F32),
        ],
        compiler_params=pltpu.CompilerParams(vmem_limit_bytes=56 * 2**20),
        cost_estimate=pl.CostEstimate(
            flops=2 * rows * width * hidden,
            bytes_accessed=8 * experts * width * hidden + 6 * rows * width,
            transcendentals=0,
        ),
        name="expert_grads",
    )(owner, tile, count, x, cot, eid, act, dbef)


MESH = pl.DeviceIdType.MESH


def remote(src, dst, send_sem, recv_sem, device):
    return pltpu.make_async_remote_copy(
        src_ref=src,
        dst_ref=dst,
        send_sem=send_sem,
        recv_sem=recv_sem,
        device_id=device,
        device_id_type=MESH,
    )


def position(plane):
    side = lax.div(plane, 2)
    return side, plane + side * (3 - 2 * plane)


def ones_where(mask):
    return jnp.where(mask, 1.0, 0.0).astype(BF)


def halves(pair):
    left = lax.broadcasted_iota(jnp.int32, pair.shape, 1) < HEAD_DIM
    zero = jnp.zeros_like(pair)
    return (jnp.where(left, pair, zero), jnp.where(left, zero, pair))


def join(first, second):
    left = lax.broadcasted_iota(jnp.int32, first.shape, 1) < HEAD_DIM
    return jnp.where(left, first, second)


def tri(block):
    later = lax.broadcasted_iota(jnp.int32, (block, block), 1)
    return later <= lax.broadcasted_iota(jnp.int32, (block, block), 0)


def normalise(values):
    centered = values - jnp.mean(values, -1, keepdims=True)
    spread = jnp.mean(centered * centered, -1, keepdims=True)
    root = lax.rsqrt(spread + EPS)
    return centered * root, root


def attend_kernel(
    tokens, w_q, w_k, w_v, w_o, gain1, bias1, gain2, bias2, place, cot, counts,
    residual, second, q_out, k_out, v_out, att_out, lse, cot_col, all_counts, places,
    normed, known, known_places, col_send, col_recv, near_send, near_recv, far_send, far_recv,
    place_send, place_recv, local_sem,
):
    step = pl.program_id(0)
    rows = tokens.shape[0]
    lanes = 2 * HEAD_DIM
    me, plane = lax.axis_index("expert"), lax.axis_index("hidden")
    planes, devices = known.shape[:2]
    side, r = position(plane)
    middle = r == 1
    step_up = 1 - 2 * side
    up, down = {"hidden": plane + step_up}, {"hidden": plane - step_up}
    other = lambda off: {"expert": lax.rem(me + off, devices)}
    across = lambda off: {"hidden": lax.rem(plane + off, planes)}
    sender = lambda off: lax.rem(me - off + devices, devices)

    def col_copy(way, below):
        piece = cot_col.at[plane]
        return remote(cot, piece, col_send.at[way], col_recv.at[below], down if way else up)

    def place_copy(off, source):
        piece = known_places.at[source]
        return remote(piece, piece, place_send.at[off], place_recv.at[off], across(off))

    def near_copy(off, source):
        piece = known.at[plane, source]
        return remote(piece, piece, near_send.at[off], near_recv.at[off], other(off))

    def far_copy(off, source):
        piece = known.at[source]
        return remote(piece, piece, far_send.at[off], far_recv.at[off], across(off))

    def own_copy():
        return pltpu.make_async_copy(cot, cot_col.at[plane], local_sem)

    def each(act, count):
        def body(off, carry):
            act(off)
            return carry

        lax.fori_loop(1, count, body, 0)

    @pl.when(step == 0)
    def _():
        barrier = pltpu.get_barrier_semaphore()

        def greet(device):
            pl.semaphore_signal(barrier, inc=1, device_id=device, device_id_type=MESH)

        each(lambda off: greet(other(off)), devices)
        each(lambda off: greet(across(off)), planes)
        known[plane, me] = counts[...]
        known_places[plane] = jnp.broadcast_to(place[...], known_places.shape[1:])
        pl.semaphore_wait(barrier, devices + planes - 2)
        each(lambda off: near_copy(off, me).start(), devices)
        each(lambda off: place_copy(off, plane).start(), planes)

        @pl.when(r == 0)
        def _():
            col_copy(0, 0).start()

        @pl.when(middle)
        def _():
            col_copy(0, 1).start()
            col_copy(1, 1).start()

        own_copy().start()

    @pl.when(step == 1)
    def _():
        each(lambda off: near_copy(off, sender(off)).wait_recv(), devices)
        each(lambda off: far_copy(off, plane).start(), planes)

    @pl.when(step == 0)
    def _():
        source = tokens[...].astype(F32)
        normed[...] = (normalise(source)[0] * gain1[...] + bias1[...]).astype(BF)
        residual[...] = source
        lse[...] = jnp.zeros(lse.shape, F32)

    q_out[0] = dot(normed[...], w_q[...]).astype(BF)
    k_out[0] = dot(normed[...], w_k[...]).astype(BF)
    v_out[0] = dot(normed[...], w_v[...]).astype(BF)
    width = q_out.shape[2]
    keep = tri(BLOCK)
    lane = lax.broadcasted_iota(jnp.int32, (BLOCK, lse.shape[1]), 1)
    for pair in range(width // lanes):
        cols = slice(pair * lanes, (pair + 1) * lanes)
        query = q_out[0, :, cols] * jnp.asarray(HEAD_DIM**-0.5, BF)
        keys = halves(k_out[0, :, cols])
        values = v_out[0, :, cols]
        for q_block in range(rows // BLOCK):
            q_rows = slice(q_block * BLOCK, (q_block + 1) * BLOCK)
            results = []
            for head in range(2):
                scores = []
                for k_block in range(q_block + 1):
                    k_rows = slice(k_block * BLOCK, (k_block + 1) * BLOCK)
                    part = dot(query[q_rows], keys[head][k_rows], ((1,), (1,)))
                    scores.append(jnp.where(keep, part, -1e30) if k_block == q_block else part)
                top = functools.reduce(jnp.maximum, [jnp.max(s, -1, keepdims=True) for s in scores])
                weights = [jnp.exp(s - top) for s in scores]
                total = sum(jnp.sum(w, -1, keepdims=True) for w in weights)
                share = 1.0 / total
                out = sum(
                    dot((w * share).astype(BF), values[k * BLOCK : (k + 1) * BLOCK])
                    for k, w in enumerate(weights)
                )
                results.append(out)
                index = step * (width // HEAD_DIM) + 2 * pair + head
                lse[q_rows, :] = jnp.where(lane == index, top + jnp.log(total), lse[q_rows, :])
            att_out[0, q_rows, cols] = join(*results).astype(BF)
    residual[...] += dot(att_out[0], w_o[...])

    @pl.when(step == pl.num_programs(0) - 1)
    def _():
        second[...] = (normalise(residual[...])[0] * gain2[...] + bias2[...]).astype(BF)
        each(lambda off: far_copy(off, lax.rem(plane - off + planes, planes)).wait_recv(), planes)
        each(lambda off: place_copy(off, lax.rem(plane - off + planes, planes)).wait_recv(), planes)
        all_counts[...] = known[...]
        places[...] = known_places[...]
        own_copy().wait()
        col_copy(0, 1).wait_recv()
        col_copy(0, 0).wait_send()

        @pl.when(middle)
        def _():
            col_copy(0, 0).wait_recv()
            col_copy(1, 1).wait_send()

        each(lambda off: place_copy(off, plane).wait_send(), planes)
        each(lambda off: near_copy(off, me).wait_send(), devices)
        each(lambda off: far_copy(off, plane).wait_send(), planes)


def attend(
    devices, planes, tokens, project_in, project_out, gain1, bias1, gain2, bias2, place, cot, counts
):
    rows, width = tokens.shape
    dma = pltpu.SemaphoreType.DMA
    counts = jnp.broadcast_to(jnp.pad(counts, (0, 128 - counts.shape[0]))[None, :], (8, 128))
    known = (planes, devices, 8, 128)
    steps = width // QUAD
    whole = lambda shape: pl.BlockSpec(shape, lambda j: (0, 0))
    third = lambda k: pl.BlockSpec((width, QUAD), lambda j: (0, k * steps + j))
    cols = pl.BlockSpec((1, rows, QUAD), lambda j: (j, 0, 0))
    vector = whole((1, width))
    low = jax.ShapeDtypeStruct((rows, width), BF)
    split = jax.ShapeDtypeStruct((steps, rows, QUAD), BF)
    return pl.pallas_call(
        attend_kernel,
        grid=(steps,),
        in_specs=[whole((rows, width)), third(0), third(1), third(2),
            pl.BlockSpec((QUAD, width), lambda j: (j, 0)), vector, vector, vector, vector,
            whole((1, rows)), whole((rows, width)), whole((8, 128))],
        out_specs=[whole((rows, width)), whole((rows, width)), cols, cols, cols, cols, whole((rows, 128)),
            pl.BlockSpec(memory_space=pl.ANY), pl.BlockSpec(known, lambda j: (0, 0, 0, 0)),
            pl.BlockSpec((planes, 8, rows), lambda j: (0, 0, 0))],
        out_shape=[jax.ShapeDtypeStruct((rows, width), F32), low, split, split, split, split,
            jax.ShapeDtypeStruct((rows, 128), F32), jax.ShapeDtypeStruct((planes, rows, width), BF),
            jax.ShapeDtypeStruct(known, jnp.int32), jax.ShapeDtypeStruct((planes, 8, rows), jnp.int32)],
        scratch_shapes=[pltpu.VMEM((rows, width), BF), pltpu.VMEM(known, jnp.int32),
            pltpu.VMEM((planes, 8, rows), jnp.int32), dma((2,)), dma((2,)), dma((devices,)), dma((devices,)),
            dma((planes,)), dma((planes,)), dma((planes,)), dma((planes,)), dma],
        compiler_params=pltpu.CompilerParams(
            collective_id=0, has_side_effects=True, vmem_limit_bytes=56 * 2**20
        ),
        cost_estimate=pl.CostEstimate(flops=10 * rows * width * width, bytes_accessed=20 * 2**20,
            transcendentals=HEADS * rows * rows),
        name="attend",
    )(tokens, project_in, project_in, project_in, project_out, *(v.reshape(1, width) for v in (gain1, bias1, gain2, bias2)),
        place.reshape(1, rows), cot, counts)


def layer_norm_back(d_normed, xhat, root, gain):
    scaled = d_normed * gain
    d_values = root * (
        scaled
        - jnp.mean(scaled, -1, keepdims=True)
        - xhat * jnp.mean(scaled * xhat, -1, keepdims=True)
    )
    sums = (jnp.sum(d_normed * xhat, 0, keepdims=True), jnp.sum(d_normed, 0, keepdims=True))
    return d_values, sums


def pass_kernel(
    rows, pieces, group,
    x, places, targets, target_rows, cot_col, eid, w_in, w_out,
    x_all, cot_all, act_o, dbef_o, part_o, o_down, o_up, own_out, cot_far, cot_slots, d_second,
    slots, arrived, packed_x, packed_c, dense, returned, d_part, from_down, from_up, x_tile, c_tile, stage,
    plane_send, plane_recv, cot_send, cot_recv, far_send, far_recv, back_send, back_recv, ag_send, ag_recv,
    rs_send, rs_down, rs_up, os_send, os_down, os_up, local_sem, stage_sem, own_sem, dense_sem,
):
    me, plane = lax.axis_index("expert"), lax.axis_index("hidden")
    _, devices, chunk, width = slots.shape
    experts = w_in.shape[0]
    height = rows // pieces
    tile_height = group * height
    tiles = pieces // group
    side, r = position(plane)
    middle, end = r == 1, r == 0
    step = 1 - 2 * side
    up, down = {"hidden": plane + step}, {"hidden": plane - step}
    physical = lambda rel: rel + side * (3 - 2 * rel)
    part_of = lambda j: pl.ds(pl.multiple_of(j * height, 16), height)
    tile_of = lambda i: pl.ds(pl.multiple_of(i * tile_height, 16), tile_height)
    peer_of = lambda off: lax.rem(me + off, devices)
    source_of = lambda off: lax.rem(me - off + devices, devices)

    def each(act, first, last):
        def body(i, carry):
            act(i)
            return carry

        lax.fori_loop(first, last, body, 0)

    def forward_rel(p):
        return jnp.where(end | (p > 2), p, jnp.where(p == 0, 1, jnp.where(p == 1, 2, 0)))

    def cot_rel(n):
        at_middle = jnp.where(n == 0, 2, jnp.where(n == 1, 0, jnp.where(n == 2, 3, 1)))
        return jnp.where(end, lax.rem(n + 1, 4), at_middle)

    barrier = pltpu.get_barrier_semaphore()
    greet = lambda device: pl.semaphore_signal(barrier, inc=1, device_id=device, device_id_type=MESH)
    each(lambda off: greet({"expert": peer_of(off)}), 1, devices)
    greet(up)

    @pl.when(middle)
    def _():
        greet(down)

    pl.semaphore_wait(barrier, devices + r)

    def far_copy(index):
        block = physical((0, 2, 3)[index])
        source = (cot_far if index == 2 else cot_col).at[block]
        device = down if index else up
        return remote(source, cot_far.at[block], far_send.at[index], far_recv.at[index], device)

    @pl.when(middle)
    def _():
        far_copy(0).start()
        far_copy(1).start()

    def slots_of(device, block, values):
        row = lax.broadcasted_iota(jnp.int32, (chunk, x.shape[0]), 0) + device * chunk
        return dot(ones_where(row == places[block, 0:1, :]), values[...]).astype(BF)

    def dispatch_copy(off, to, frm):
        return remote(
            slots.at[0, to], arrived.at[frm], plane_send.at[off], plane_recv.at[off], {"expert": to}
        )

    def dispatch(off):
        peer = peer_of(off)
        slots[0, peer] = slots_of(peer, plane, x)
        dispatch_copy(off, peer, me).start()

    each(dispatch, 1, devices)
    arrived[me] = slots_of(me, plane, x)

    def cot_copy(n, off, to, frm):
        slot = lax.rem(n + 1, 2)
        return remote(
            slots.at[slot, to], cot_slots.at[n, frm], cot_send.at[n, off], cot_recv.at[n, off], {"expert": to}
        )

    def cot_own(n):
        return pltpu.make_async_copy(slots.at[lax.rem(n + 1, 2), me], cot_slots.at[n, me], own_sem.at[n])

    def cot_sent(n):
        each(lambda off: cot_copy(n, off, peer_of(off), me).wait_send(), 1, devices)

    def send_cot(n, far):
        block = physical(cot_rel(n))

        def fetch(source):
            one = pltpu.make_async_copy(source.at[block], dense, dense_sem)
            one.start()
            one.wait()

        @pl.when(far)
        def _():
            fetch(cot_far)

        @pl.when(jnp.logical_not(far))
        def _():
            fetch(cot_col)

        def fill(off):
            peer = peer_of(off)
            slots[lax.rem(n + 1, 2), peer] = slots_of(peer, block, dense)
            cot_copy(n, off, peer, me).start()

        each(fill, 1, devices)
        slots[lax.rem(n + 1, 2), me] = slots_of(me, block, dense)
        cot_own(n).start()

    send_cot(jnp.int32(0), jnp.bool_(False))

    def pack(block, j):
        row = lax.broadcasted_iota(jnp.int32, (height, devices * chunk), 0) + j * height
        flat = arrived[...].reshape(devices * chunk, width)
        return dot(ones_where(row == targets[block]), flat).astype(BF)

    def gather_copy(way, block, j, own):
        source = packed_x.at[part_of(j)] if own else x_all.at[block, part_of(j)]
        return remote(
            source, x_all.at[block, part_of(j)], ag_send.at[way, block, j], ag_recv.at[block, j], down if way else up
        )

    @pl.when(middle)
    def _():
        far_copy(0).wait_recv()
        far_copy(2).start()

    each(lambda off: dispatch_copy(off, me, source_of(off)).wait_recv(), 1, devices)

    def send_own(j):
        packed_x[part_of(j)] = pack(plane, j)
        gather_copy(0, plane, j, True).start()

        @pl.when(middle)
        def _():
            gather_copy(1, plane, j, True).start()

    each(send_own, 0, pieces)
    keep_own = pltpu.make_async_copy(packed_x, x_all.at[plane, pl.ds(0, rows)], local_sem.at[0])
    keep_own.start()

    keep_own.wait()

    def got(rel, j):
        gather_copy(0, physical(rel), j, False).wait_recv()

    def relay(rel, way, j):
        got(rel, j)
        gather_copy(way, physical(rel), j, False).start()

    def keep_cot(n):
        there = cot_all.at[physical(cot_rel(n)), pl.ds(0, rows)]
        return pltpu.make_async_copy(packed_c, there, local_sem.at[1])

    def collect_cot(n):
        block = physical(cot_rel(n))

        @pl.when(n > 1)
        def _():
            cot_own(n).wait()

        each(lambda off: cot_copy(n, off, me, source_of(off)).wait_recv(), 1, devices)
        fetch = pltpu.make_async_copy(cot_slots.at[n], arrived, dense_sem)
        fetch.start()

        @pl.when(n > 0)
        def _():
            keep_cot(n).wait()

        fetch.wait()

        def one(j):
            packed_c[part_of(j)] = pack(block, j)

        each(one, 0, pieces)
        keep_cot(n).start()

    def sum_copy(rel, j, buffer, index, sems, device):
        return remote(
            d_part.at[physical(rel), part_of(j)],
            buffer.at[index, part_of(j)],
            rs_send.at[rel, j],
            sems.at[index, j],
            device,
        )

    def add(rel, j, buffer, index, sems):
        sum_copy(rel, j, buffer, index, sems, up).wait_recv()
        block = physical(rel)
        here = d_part[block, part_of(j)].astype(F32)
        d_part[block, part_of(j)] = (here + buffer[index, part_of(j)].astype(F32)).astype(BF)

    def out_copy(rel, j, source, buffer, index, sems, device):
        return remote(
            source, buffer.at[index, part_of(j)], os_send.at[rel, j], sems.at[index, j], device
        )

    def out_send(rel, j):
        source = part_o.at[physical(rel), part_of(j)]
        out_copy(rel, j, source, o_down, rel - 1, os_down, up).start()

    def out_sum(rel, j, buffers):
        pads = [t.at[pl.ds(0, height)] for t in (x_tile, c_tile, stage.at[0])]
        loads = [pltpu.make_async_copy(part_o.at[physical(rel), part_of(j)], pads[0], stage_sem.at[0])]
        loads[0].start()
        for n, (buffer, index, sems) in enumerate(buffers):
            piece = buffer.at[index, part_of(j)]
            out_copy(rel, j, piece, buffer, index, sems, up).wait_recv()
            loads.append(pltpu.make_async_copy(piece, pads[n + 1], stage_sem.at[n + 1]))
            loads[-1].start()
        for load in loads:
            load.wait()
        return sum(t[...].astype(F32) for t in pads[: len(loads)]).astype(BF)

    def out_relay(j):
        held = from_down.at[1, part_of(j)]
        held[...] = out_sum(2, j, [(o_down, 1, os_down)])
        out_copy(2, j, held, o_up, 1, os_up, up).start()

    outs = (act_o, dbef_o, part_o)

    def stage_copy(index, block, i):
        return pltpu.make_async_copy(
            stage.at[index], outs[index].at[block, tile_of(i)], stage_sem.at[index]
        )

    def load(block, i):
        one = pltpu.make_async_copy(x_all.at[block, tile_of(i)], x_tile, local_sem.at[0])
        one.start()
        one.wait()

    def chooser(block, i):
        start = pl.multiple_of(block * rows + i * tile_height, 16)
        owner = eid[pl.ds(start, tile_height), :]
        mine = [owner == float(e) for e in range(experts)]

        def choose(results):
            total = jnp.where(mine[0], results[0], 0.0)
            for mask, result in zip(mine[1:], results[1:]):
                total = jnp.where(mask, result, total)
            return total

        return choose

    def columns(body):
        def one(n, carry):
            body(pl.ds(pl.multiple_of(n * TILE, TILE), TILE))
            return carry

        lax.fori_loop(0, width // TILE, one, 0)

    def gelu_parts(choose, cols):
        before = choose([dot(x_tile[...], w_in[e, :, cols]) for e in range(experts)])
        square = before * before
        tanh = jnp.tanh(0.7978845608028654 * before * (1.0 + 0.044715 * square))
        return before, square, tanh, 0.5 * (1.0 + tanh)

    def forward_tile(block, i, first):
        load(block, i)
        choose = chooser(block, i)

        @pl.when(jnp.logical_not(first))
        def _():
            stage_copy(0, block, i).wait()
            stage_copy(2, block, i).wait()

        def activate(cols):
            before, _, _, half = gelu_parts(choose, cols)
            stage[0, :, cols] = (before * half).astype(BF)

        def produce(cols):
            results = [dot(stage[0], w_out[e, :, cols]) for e in range(experts)]
            stage[2, :, cols] = choose(results).astype(BF)

        columns(activate)
        columns(produce)
        stage_copy(0, block, i).start()
        stage_copy(2, block, i).start()

    def backward_tile(block, i, first):
        load(block, i)
        choose = chooser(block, i)

        @pl.when(jnp.logical_not(first))
        def _():
            stage_copy(1, block, i).wait()

        def before_back(cols):
            before, square, tanh, half = gelu_parts(choose, cols)
            results = [dot(packed_c[tile_of(i)], w_out[e, cols, :], ((1,), (1,))) for e in range(experts)]
            slope = half + 0.5 * before * (1.0 - tanh * tanh) * (
                0.7978845608028654 * (1.0 + 0.134145 * square)
            )
            stage[1, :, cols] = (choose(results) * slope).astype(BF)

        def members_back(cols):
            results = [dot(stage[1], w_in[e, cols, :], ((1,), (1,))) for e in range(experts)]
            d_part[block, tile_of(i), cols] = choose(results).astype(BF)

        columns(before_back)
        stage_copy(1, block, i).start()
        columns(members_back)

    def phase(p, carry):
        def come(j):
            @pl.when((p == 1) & middle)
            def _():
                relay(0, 0, j)
                relay(2, 1, j)

            @pl.when((p == 2) & middle)
            def _():
                relay(3, 1, j)

            @pl.when((p > 0) & (p < 4) & end)
            def _():
                got(p, j)

        def ahead(i):
            each(come, i * group, (i + 1) * group)

            @pl.when(p < 4)
            def _():
                forward_tile(physical(forward_rel(p)), i, (p == 0) & (i == 0))

            @pl.when((p == 3) & middle)
            def _():
                def pass_on(j):
                    add(2, j, from_down, 1, rs_down)
                    sum_copy(2, j, from_up, 1, rs_up, up).start()

                each(pass_on, i * group, (i + 1) * group)

        each(ahead, 0, tiles)

        @pl.when(p < 3)
        def _():
            @pl.when(p == 0)
            def _():
                each(lambda off: dispatch_copy(off, peer_of(off), me).wait_send(), 1, devices)

            @pl.when(p > 0)
            def _():
                cot_sent(p - 1)
                cot_own(p - 1).wait()

            @pl.when((p == 0) & end)
            def _():
                far_copy(1).wait_recv()

            @pl.when((p == 1) & end)
            def _():
                far_copy(2).wait_recv()

            send_cot(p + 1, (p == 1) | ((p == 0) & end))

        @pl.when(p == 4)
        def _():
            stage_copy(0, plane, 0).wait()
            stage_copy(2, plane, 0).wait()

            @pl.when(end)
            def _():
                each(lambda j: out_send(1, j), 0, pieces)
                each(lambda j: out_send(2, j), 0, pieces)

        rel = cot_rel(p - 1)

        def go(j):
            @pl.when((p < 4) & end)
            def _():
                sum_copy(rel, j, from_down, rel - 1, rs_down, up).start()

            @pl.when((p == 4) & middle)
            def _():
                add(3, j, from_down, 2, rs_down)
                sum_copy(3, j, from_up, 0, rs_up, up).start()

            @pl.when((p == 4) & middle & (j > 0))
            def _():
                add(0, j - 1, from_up, 0, rs_up)
                sum_copy(0, j - 1, from_up, 0, rs_up, down).start()

        def behind(i):
            backward_tile(physical(rel), i, (p == 1) & (i == 0))
            each(go, i * group, (i + 1) * group)

        @pl.when(p > 0)
        def _():
            collect_cot(p - 1)
            each(behind, 0, tiles)

        return carry

    lax.fori_loop(0, 5, phase, 0)
    stage_copy(1, plane, 0).wait()
    keep_cot(jnp.int32(3)).wait()

    @pl.when(middle)
    def _():
        add(0, pieces - 1, from_up, 0, rs_up)
        sum_copy(0, pieces - 1, from_up, 0, rs_up, down).start()

    def last(j):
        @pl.when(middle)
        def _():
            add(1, j, from_down, 0, rs_down)
            add(1, j, from_up, 1, rs_up)

        @pl.when(end)
        def _():
            add(0, j, from_up, 0, rs_up)

    each(last, 0, pieces)

    cot_sent(jnp.int32(2))

    def back_slots(device):
        row = lax.broadcasted_iota(jnp.int32, (rows, chunk), 0)
        return dot(ones_where(row == target_rows[device]), d_part[plane], ((0,), (0,))).astype(BF)

    def back_copy(off, to, frm):
        return remote(
            slots.at[1, to], returned.at[frm], back_send.at[off], back_recv.at[off], {"expert": to}
        )

    def back(off):
        peer = peer_of(off)
        slots[1, peer] = back_slots(peer)
        back_copy(off, peer, me).start()

    each(back, 1, devices)
    returned[me] = back_slots(me)

    @pl.when(middle)
    def _():
        each(out_relay, 0, pieces)

    each(lambda off: back_copy(off, me, source_of(off)).wait_recv(), 1, devices)
    slot = lax.broadcasted_iota(jnp.int32, (devices * chunk, x.shape[0]), 0)
    flat = returned[...].reshape(devices * chunk, width)
    d_second[...] = dot(ones_where(slot == places[plane, 0:1, :]), flat, ((0,), (0,))).astype(BF)

    @pl.when(middle)
    def _():
        def out_last(j):
            d_part[plane, part_of(j)] = out_sum(1, j, [(o_down, 0, os_down), (o_up, 1, os_up)])

        each(out_last, 0, pieces)

    @pl.when(end)
    def _():
        own = pltpu.make_async_copy(part_o.at[plane, pl.ds(0, rows)], d_part.at[plane], local_sem.at[0])
        own.start()
        own.wait()

    own = pltpu.make_async_copy(d_part.at[plane], own_out.at[pl.ds(0, rows)], local_sem.at[1])
    own.start()

    x_tile[...] = jnp.zeros(x_tile.shape, BF)
    whole_tiles = -(-rows // TILE) * TILE
    fills = []
    for array, stop in [(a, whole_tiles) for a in (x_all, cot_all, act_o, dbef_o)] + [(part_o, part_o.shape[1])]:
        for block in range(4):
            for start in range(rows, stop, tile_height):
                fills.append(array.at[block, pl.ds(start, min(tile_height, stop - start))])
    for start in range(rows, own_out.shape[0], tile_height):
        fills.append(own_out.at[pl.ds(start, min(tile_height, own_out.shape[0] - start))])
    for there in fills:
        fill = pltpu.make_async_copy(x_tile.at[pl.ds(0, there.shape[0])], there, local_sem.at[0])
        fill.start()
        fill.wait()
    own.wait()

    each(lambda off: back_copy(off, peer_of(off), me).wait_send(), 1, devices)
    cot_sent(jnp.int32(3))

    @pl.when(middle)
    def _():
        for index in range(3):
            far_copy(index).wait_send()

    def sent(j):
        gather_copy(0, plane, j, True).wait_send()

        @pl.when(middle)
        def _():
            gather_copy(1, plane, j, True).wait_send()
            gather_copy(0, physical(0), j, False).wait_send()
            for rel in (2, 3):
                gather_copy(1, physical(rel), j, False).wait_send()
            for rel in (0, 2, 3):
                sum_copy(rel, j, from_up, 0, rs_up, up).wait_send()
            out_copy(2, j, part_o.at[0, part_of(j)], o_up, 1, os_up, up).wait_send()

        @pl.when(end)
        def _():
            for rel in (1, 2, 3):
                sum_copy(rel, j, from_up, 0, rs_up, up).wait_send()
            for rel in (1, 2):
                out_copy(rel, j, part_o.at[0, part_of(j)], o_up, 1, os_up, up).wait_send()

    each(sent, 0, pieces)


def expert_pass(rows, pieces, group, number, room, x, places, targets, target, cot_col, eid, w_in, w_out):
    devices, _, chunk = target.shape
    width, hidden = w_in.shape[1:]
    planes = cot_col.shape[0]
    height = rows // pieces
    tall = group * height
    here, there = pl.BlockSpec(memory_space=pltpu.VMEM), pl.BlockSpec(memory_space=pl.ANY)
    dma = pltpu.SemaphoreType.DMA
    low = lambda *shape: jax.ShapeDtypeStruct(shape, BF)
    held = lambda *shape: pltpu.VMEM(shape, BF)
    wide = low(planes, devices * chunk, width)
    return pl.pallas_call(
        functools.partial(pass_kernel, rows, pieces, group),
        in_specs=[here] * 4 + [there] + [here] * 3,
        out_specs=[there] * 10 + [here],
        out_shape=[wide] * 4
        + [low(planes, room, width), low(3, rows, width), low(2, rows, width), low(room, width)]
        + [low(*cot_col.shape), low(planes, devices, chunk, width), low(*x.shape)],
        scratch_shapes=[
            held(2, devices, chunk, width),
            held(devices, chunk, width),
            held(rows, width),
            held(rows, width),
            held(*x.shape),
            held(devices, chunk, width),
            held(planes, rows, width),
            held(3, rows, width),
            held(2, rows, width),
            held(tall, width),
            held(height, width),
            held(3, tall, hidden),
            dma((devices,)),
            dma((devices,)),
            dma((planes, devices)),
            dma((planes, devices)),
            dma((3,)),
            dma((3,)),
            dma((devices,)),
            dma((devices,)),
            dma((2, planes, pieces)),
            dma((planes, pieces)),
            dma((planes, pieces)),
            dma((3, pieces)),
            dma((2, pieces)),
            dma((planes, pieces)),
            dma((3, pieces)),
            dma((2, pieces)),
            dma((2,)),
            dma((3,)),
            dma((planes,)),
            dma,
        ],
        compiler_params=pltpu.CompilerParams(
            collective_id=number, has_side_effects=True, vmem_limit_bytes=62 * 2**20
        ),
        cost_estimate=pl.CostEstimate(
            flops=20 * planes * rows * width * hidden,
            bytes_accessed=16 * planes * rows * width,
            transcendentals=planes * rows * hidden,
        ),
        name="expert_pass",
    )(x, places, targets, target, cot_col, eid, w_in, w_out)


def tail_kernel(
    pieces,
    tokens, residual, d_second, cot, q, k, v, att, lse, project_in, project_out, gain1, bias1, gain2,
    target_rows, own_in, partial,
    grad_tokens, summed_grads, small_out, out_slots,
    w_in, w_out, normed, d_branch, d_normed, grads, small, small_plane, small_near, small_far,
    core_buf, half_buf, plane_buf, own, o_far, o_near, mine, slot_tile,
    o_send, o_recv, out_sem, slot_sem,
    ar_send, ar_recv, near_send, near_recv, far_send, far_recv,
    w_sem, local_sem,
):
    me, plane = lax.axis_index("expert"), lax.axis_index("hidden")
    devices, planes = lax.axis_size("expert"), lax.axis_size("hidden")
    width = tokens.shape[1]
    quads, tall, quad = grads.shape
    other = lambda off: {"expert": lax.rem(me + off, devices)}
    across = lambda off: {"hidden": lax.rem(plane + off, planes)}

    barrier = pltpu.get_barrier_semaphore()

    def greet(off, carry):
        pl.semaphore_signal(barrier, inc=1, device_id=other(off), device_id_type=MESH)
        return carry

    lax.fori_loop(1, devices, greet, 0)
    for off in range(1, planes):
        pl.semaphore_signal(barrier, inc=1, device_id=across(off), device_id_type=MESH)

    def weights(j, slot):
        cols = lambda third: pl.ds(pl.multiple_of(third * width + j * quad, quad), quad)
        copies = [
            pltpu.make_async_copy(project_in.at[:, cols(third)], w_in.at[slot, third], w_sem.at[slot, third])
            for third in range(3)
        ]
        rows_out = pl.ds(pl.multiple_of(j * quad, quad), quad)
        copies.append(pltpu.make_async_copy(project_out.at[rows_out], w_out.at[slot], w_sem.at[slot, 3]))
        return copies

    for copy in weights(0, 0):
        copy.start()
    pl.semaphore_wait(barrier, devices - 1 + planes - 1)

    rows = own.shape[0]
    height = rows // pieces
    side = lax.div(plane, 2)
    r = plane + side * (3 - 2 * plane)
    middle = r == 1
    step = 1 - 2 * side
    up, down = {"hidden": plane + step}, {"hidden": plane - step}
    physical = lambda rel: rel + side * (3 - 2 * rel)
    part_of = lambda j: pl.ds(pl.multiple_of(j * height, 16), height)

    def out_copy(kind, j):
        source = partial.at[physical(3), part_of(j)] if kind == 0 else mine.at[kind - 1, part_of(j)]
        there = (o_far if kind == 0 else o_near).at[part_of(j)]
        return remote(source, there, o_send.at[kind, j], o_recv.at[kind, j], down if kind == 2 else up)

    def out_load(index):
        source = own_in if index == 2 else partial.at[physical(3 - 3 * index)]
        return pltpu.make_async_copy(source, own if index == 2 else mine.at[index], out_sem.at[index])

    @pl.when(r == 0)
    def _():
        def body(j, carry):
            out_copy(0, j).start()
            return carry

        lax.fori_loop(0, pieces, body, 0)

    for index in range(3):
        out_load(index).start()

    def out_add(kind, j, target):
        out_copy(kind, j).wait_recv()
        there = o_far if kind == 0 else o_near
        here = target[part_of(j)].astype(F32)
        target[part_of(j)] = (here + there[part_of(j)].astype(F32)).astype(BF)

    def out_turn(j):
        @pl.when(middle & (j < pieces))
        def _():
            out_add(0, j, mine.at[0])
            out_copy(1, j).start()

        @pl.when(middle & (j > 0) & (j <= pieces))
        def _():
            out_add(1, j - 1, mine.at[1])
            out_copy(2, j - 1).start()

        @pl.when((r == 0) & (j > 1) & (j <= pieces + 1))
        def _():
            out_add(2, j - 2, own)

    def out_slot_copy(device):
        slot = lax.rem(device, 2)
        return pltpu.make_async_copy(slot_tile.at[slot], out_slots.at[device], slot_sem.at[slot])

    def out_slot(device, carry):
        @pl.when(device > 1)
        def _():
            out_slot_copy(device - 2).wait()

        row = lax.broadcasted_iota(jnp.int32, (rows, slot_tile.shape[1]), 0)
        mask = ones_where(row == target_rows[device])
        slot_tile[lax.rem(device, 2)] = dot(mask, own[...], ((0,), (0,))).astype(BF)
        out_slot_copy(device).start()
        return carry

    bits = devices.bit_length() - 1
    bit = lambda i: lax.rem(lax.div(me, 1 << i), 2)
    partner = lambda i: {"expert": me + (1 << i) * (1 - 2 * bit(i))}
    half = tall // 2
    part = half // 2
    orders = [list(range(1, bits)), list(range(bits - 1, 0, -1))]
    levels = bits - 1
    last = part >> levels
    slice_len = last // planes

    def segment(a, level):
        start = bit(0) * half + a * part
        for i in range(level):
            start = start + bit(orders[a][i]) * (part >> (i + 1))
        return start

    def span(start, length):
        return pl.ds(pl.multiple_of(start, 16), length)

    slot_of = {}

    def sems(name, c):
        index = slot_of.setdefault(name, len(slot_of))
        return ar_send.at[index, c], ar_recv.at[index, c]

    def core_copy(c):
        source = grads.at[c, span((1 - bit(0)) * half, half)]
        return [remote(source, core_buf.at[c], *sems("core", c), partner(0))]

    def core_end(c):
        keep = span(bit(0) * half, half)
        grads[c, keep] = (grads[c, keep].astype(F32) + core_buf[c].astype(F32)).astype(BF)

    def halve_copy(level, c):
        copies = []
        length = part >> (level + 1)
        for a in range(2):
            i = orders[a][level]
            source = grads.at[c, span(segment(a, level) + (1 - bit(i)) * length, length)]
            buffer = half_buf.at[c, a, pl.ds(part - (part >> level), length)]
            copies.append(remote(source, buffer, *sems(("half", level, a), c), partner(i)))
        return copies

    def halve_end(level, c):
        length = part >> (level + 1)
        for a in range(2):
            keep = span(segment(a, level + 1), length)
            other_half = half_buf[c, a, pl.ds(part - (part >> level), length)]
            grads[c, keep] = (grads[c, keep].astype(F32) + other_half.astype(F32)).astype(BF)

    def plane_span(a, p):
        return span(segment(a, levels) + p * slice_len, slice_len)

    def plane_copy(c):
        copies = []
        for a in range(2):
            for off in range(1, planes):
                source = grads.at[c, plane_span(a, lax.rem(plane + off, planes))]
                buffer = plane_buf.at[c, a, off - 1]
                copies.append(remote(source, buffer, *sems(("plane", a, off), c), across(off)))
        return copies

    def plane_end(c):
        for a in range(2):
            keep = plane_span(a, plane)
            total = grads[c, keep].astype(F32)
            for off in range(planes - 1):
                total = total + plane_buf[c, a, off].astype(F32)
            grads[c, keep] = total.astype(BF)
        copies = [
            pltpu.make_async_copy(
                grads.at[c, plane_span(a, plane)],
                summed_grads.at[c, plane_span(a, plane)],
                local_sem.at[a],
            )
            for a in range(2)
        ]
        for copy in copies:
            copy.start()
        for copy in copies:
            copy.wait()

    def spread_copy(c):
        copies = []
        for a in range(2):
            for off in range(1, planes):
                keep = plane_span(a, plane)
                source, there = grads.at[c, keep], summed_grads.at[c, keep]
                copies.append(remote(source, there, *sems(("spread", a, off), c), across(off)))
        return copies

    def double_copy(level, c):
        copies = []
        for a in range(2):
            have = summed_grads.at[c, span(segment(a, level + 1), part >> (level + 1))]
            names = sems(("double", level, a), c)
            copies.append(remote(have, have, *names, partner(orders[a][level])))
        return copies

    def core_back_copy(c):
        have = summed_grads.at[c, span(bit(0) * half, half)]
        return [remote(have, have, *sems("core_back", c), partner(0))]

    nothing = lambda c: None
    stages = [(core_copy, core_end)]
    for level in range(levels):
        stages.append((functools.partial(halve_copy, level), functools.partial(halve_end, level)))
    stages.append((plane_copy, plane_end))
    stages.append((spread_copy, nothing))
    for level in reversed(range(levels)):
        stages.append((functools.partial(double_copy, level), nothing))
    stages.append((core_back_copy, nothing))

    def finish(stage, c):
        copies, end = stages[stage]
        for copy in copies(c):
            copy.wait_recv()
        for copy in copies(c):
            copy.wait_send()
        end(c)

    def near_copy(off):
        return remote(
            small, small_near.at[off - 1], near_send.at[off - 1], near_recv.at[off - 1], other(off)
        )

    def far_copy(off):
        return remote(
            small_plane, small_far.at[off - 1], far_send.at[off - 1], far_recv.at[off - 1], across(off)
        )

    def each_near(act):
        def body(off, carry):
            act(near_copy(off))
            return carry

        lax.fori_loop(1, devices, body, 0)

    scale = jnp.asarray(HEAD_DIM**-0.5, BF)
    lanes = 2 * HEAD_DIM
    xhat2, root2 = normalise(residual[...])
    d_values, sums = layer_norm_back(d_second[...].astype(F32), xhat2, root2, gain2[...])
    d_residual = cot[...].astype(F32) + d_values
    grad_tokens[...] = d_residual
    d_branch[...] = d_residual.astype(BF)
    small[...] = jnp.zeros(small.shape, F32)
    small[2:3, :], small[3:4, :] = sums
    normed[...] = (normalise(tokens[...].astype(F32))[0] * gain1[...] + bias1[...]).astype(BF)
    d_normed[...] = jnp.zeros(d_normed.shape, F32)

    def quarter(j):
        slot = lax.rem(j, 2)
        for copy in weights(j, slot):
            copy.wait()

        @pl.when(j < quads - 1)
        def _():
            for copy in weights(j + 1, 1 - slot):
                copy.start()

        out = dot(att[j], d_branch[...], ((0,), (0,))).astype(BF)
        for m in range(width // quad):
            grads[j, 3 * width + m * quad : 3 * width + (m + 1) * quad] = out[:, m * quad : (m + 1) * quad]
        d_att = dot(d_branch[...], w_out[slot], ((1,), (1,))).astype(BF)
        d_thirds = attention_back(j, q, k, v, d_att, lse, scale, lanes)
        total = 0.0
        for third, d_third in enumerate(d_thirds):
            grads[j, third * width : (third + 1) * width] = dot(
                normed[...], d_third, ((0,), (0,))
            ).astype(BF)
            total = total + dot(d_third, w_in[slot, third], ((1,), (1,)))
        d_normed[...] += total

        @pl.when(j == quads - 1)
        def _():
            xhat, root = normalise(tokens[...].astype(F32))
            d_first, first_sums = layer_norm_back(d_normed[...], xhat, root, gain1[...])
            grad_tokens[...] += d_first
            small[0:1, :], small[1:2, :] = first_sums

    count = len(stages)

    def tick(t, carry):
        @pl.when(t < quads)
        def _():
            quarter(t)
            for copy in stages[0][0](t):
                copy.start()

        for stage in range(count, 0, -1):
            c = t - stage

            @pl.when((c >= 0) & (c < quads))
            def _(stage=stage, c=c):
                finish(stage - 1, c)
                if stage < count:
                    for copy in stages[stage][0](c):
                        copy.start()

        @pl.when(t == 1)
        def _():
            for index in range(3):
                out_load(index).wait()

        @pl.when((t >= 1) & (t <= 2 + pieces))
        def _():
            out_turn(t - 1)

        @pl.when(t == quads + pieces)
        def _():
            lax.fori_loop(0, devices, out_slot, 0)
            for device in (devices - 2, devices - 1):
                out_slot_copy(device).wait()

        @pl.when(t == quads - 1)
        def _():
            each_near(lambda copy: copy.start())

        @pl.when(t == quads + 1)
        def _():
            each_near(lambda copy: copy.wait_recv())
            each_near(lambda copy: copy.wait_send())
            total = small[...]
            for off in range(devices - 1):
                total = total + small_near[off]
            small_plane[...] = total
            for off in range(1, planes):
                far_copy(off).start()

        @pl.when(t == quads + 3)
        def _():
            for off in range(1, planes):
                far_copy(off).wait_recv()
            for off in range(1, planes):
                far_copy(off).wait_send()
            total = small_plane[...]
            for off in range(planes - 1):
                total = total + small_far[off]
            small_out[...] = total

        return carry

    lax.fori_loop(0, max(quads + count, quads + pieces + 1), tick, 0)

    def outs_sent(j, carry):
        @pl.when(r == 0)
        def _():
            out_copy(0, j).wait_send()

        @pl.when(middle)
        def _():
            out_copy(1, j).wait_send()
            out_copy(2, j).wait_send()

        return carry

    lax.fori_loop(0, pieces, outs_sent, 0)


def attention_back(j, q, k, v, d_att, lse, scale, lanes):
    rows, quad = d_att.shape
    keep = tri(BLOCK)
    blocks = rows // BLOCK
    cut = lambda array, block: array[block * BLOCK : (block + 1) * BLOCK]
    d_q, d_k, d_v = [], [], []
    lane = lax.broadcasted_iota(jnp.int32, (BLOCK, lse.shape[1]), 1)
    for pair in range(quad // lanes):
        cols = slice(pair * lanes, (pair + 1) * lanes)
        query = q[j, :, cols] * scale
        key, value, d_pair = k[j, :, cols], v[j, :, cols], d_att[:, cols]
        keys, values = halves(key), halves(value)
        pair_q, pair_k, pair_v = [], [], []
        for head in range(2):
            index = j * (quad // HEAD_DIM) + 2 * pair + head
            q_parts = []
            k_parts, v_parts = [0.0] * blocks, [0.0] * blocks
            for q_block in range(blocks):
                level = jnp.sum(
                    jnp.where(lane == index, lse[q_block * BLOCK : (q_block + 1) * BLOCK, :], 0.0),
                    -1,
                    keepdims=True,
                )
                shares, d_shares, inner = [], [], 0.0
                for k_block in range(q_block + 1):
                    scores = dot(cut(query, q_block), cut(keys[head], k_block), ((1,), (1,)))
                    share = jnp.exp(scores - level)
                    if k_block == q_block:
                        share = jnp.where(keep, share, 0.0)
                    d_share = dot(cut(d_pair, q_block), cut(values[head], k_block), ((1,), (1,)))
                    inner = inner + jnp.sum(share * d_share, -1, keepdims=True)
                    shares.append(share)
                    d_shares.append(d_share)
                total = 0.0
                for k_block in range(q_block + 1):
                    d_scores = (shares[k_block] * (d_shares[k_block] - inner)).astype(BF)
                    total = total + dot(d_scores, cut(key, k_block))
                    k_parts[k_block] += dot(d_scores, cut(query, q_block), ((0,), (0,)))
                    v_parts[k_block] += dot(
                        shares[k_block].astype(BF), cut(d_pair, q_block), ((0,), (0,))
                    )
                q_parts.append(total * HEAD_DIM**-0.5)
            pair_q.append(jnp.concatenate(q_parts, 0))
            pair_k.append(jnp.concatenate(k_parts, 0))
            pair_v.append(jnp.concatenate(v_parts, 0))
        d_q.append(join(*pair_q).astype(BF))
        d_k.append(join(*pair_k).astype(BF))
        d_v.append(join(*pair_v).astype(BF))
    return [jnp.concatenate(parts, 1) for parts in (d_q, d_k, d_v)]


def tail(
    number, devices, planes, pieces, target, own, partial, tokens, residual, d_second, cot, q, k, v, att, lse, project_in, project_out,
    gain1, bias1, gain2,
):
    tokens_dev, width = tokens.shape
    quads, _, quad = q.shape
    tall = 4 * width
    bits = devices.bit_length() - 1
    part = tall // 4
    slice_len = (part >> (bits - 1)) // planes
    slots = 2 + 4 * (bits - 1) + 4 * (planes - 1)
    chunk = target.shape[2]
    rows = own.shape[0]
    here, there = pl.BlockSpec(memory_space=pltpu.VMEM), pl.BlockSpec(memory_space=pl.ANY)
    dma = pltpu.SemaphoreType.DMA
    low = lambda *shape: pltpu.VMEM(shape, BF)
    full = lambda *shape: pltpu.VMEM(shape, F32)
    return pl.pallas_call(
        functools.partial(tail_kernel, pieces),
        in_specs=[here] * 9 + [there] * 2 + [here] * 4 + [there] * 2,
        out_specs=[here, there, here, there],
        out_shape=[
            jax.ShapeDtypeStruct((tokens_dev, width), F32),
            jax.ShapeDtypeStruct((quads, tall, quad), BF),
            jax.ShapeDtypeStruct((8, width), F32),
            jax.ShapeDtypeStruct((devices, chunk, width), BF),
        ],
        scratch_shapes=[
            low(2, 3, width, quad),
            low(2, quad, width),
            low(tokens_dev, width),
            low(tokens_dev, width),
            full(tokens_dev, width),
            low(quads, tall, quad),
            full(8, width),
            full(8, width),
            full(devices - 1, 8, width),
            full(planes - 1, 8, width),
            low(quads, tall // 2, quad),
            low(quads, 2, part - (part >> (bits - 1)), quad),
            low(quads, 2, planes - 1, slice_len, quad),
            low(rows, width),
            low(rows, width),
            low(rows, width),
            low(2, rows, width),
            low(2, chunk, width),
            dma((3, pieces)),
            dma((3, pieces)),
            dma((3,)),
            dma((2,)),
            dma((slots, quads)),
            dma((slots, quads)),
            dma((devices - 1,)),
            dma((devices - 1,)),
            dma((planes - 1,)),
            dma((planes - 1,)),
            dma((2, 4)),
            dma((2,)),
        ],
        compiler_params=pltpu.CompilerParams(
            collective_id=number, has_side_effects=True, vmem_limit_bytes=62 * 2**20
        ),
        cost_estimate=pl.CostEstimate(
            flops=20 * tokens_dev * width * width,
            bytes_accessed=64 * 2**20,
            transcendentals=HEADS * tokens_dev * tokens_dev,
        ),
        name="tail",
    )(
        tokens, residual, d_second, cot, q, k, v, att, lse, project_in, project_out,
        *(x.reshape(1, width) for x in (gain1, bias1, gain2)), target, own, partial,
    )


def spread_kernel(summed, grad_in, grad_out):
    third = pl.program_id(1)

    @pl.when(third < 3)
    def _():
        grad_in[...] = summed[0].astype(F32)

    @pl.when(third == 3)
    def _():
        quad = summed.shape[2]
        for m in range(grad_out.shape[1] // quad):
            rows = slice(m * quad, (m + 1) * quad)
            grad_out[:, rows] = summed[0, rows].astype(F32)


def spread(summed):
    quads, tall, quad = summed.shape
    width = tall // 4
    return pl.pallas_call(
        spread_kernel,
        grid=(quads, 4),
        in_specs=[pl.BlockSpec((1, width, quad), lambda j, t: (j, t, 0))],
        out_specs=[
            pl.BlockSpec((width, quad), lambda j, t: (0, jnp.minimum(t, 2) * quads + j)),
            pl.BlockSpec((quad, width), lambda j, t: (j, 0)),
        ],
        out_shape=[
            jax.ShapeDtypeStruct((width, 3 * width), F32),
            jax.ShapeDtypeStruct((width, width), F32),
        ],
        compiler_params=pltpu.CompilerParams(vmem_limit_bytes=40 * 2**20),
        name="spread",
    )(summed)


def on_device(
    tokens,
    token_ids,
    hash_table,
    first_gain,
    first_bias,
    project_in,
    project_out,
    second_gain,
    second_bias,
    expert_in,
    expert_out,
    cotangent,
):
    rows_dev, width = tokens.shape
    expert_devs = lax.axis_size("expert")
    hidden_devs = lax.axis_size("hidden")
    local = expert_in.shape[0]
    experts = local * expert_devs
    capacity = 8 * ((3 * rows_dev + 8 * experts - 1) // (8 * experts))
    chunk = local * capacity

    owner = hash_table.at[token_ids].get(mode="promise_in_bounds")
    expert_ids = jnp.arange(experts, dtype=jnp.int32)
    onehot = owner[:, None] == expert_ids[None, :]
    earlier = lax.broadcasted_iota(jnp.int32, (rows_dev, rows_dev), 1) < lax.broadcasted_iota(
        jnp.int32, (rows_dev, rows_dev), 0
    )
    before_count = jnp.dot(earlier.astype(BF), onehot.astype(BF), preferred_element_type=F32)
    counts = jnp.sum(onehot.astype(jnp.int32), 0)
    grouped = counts.reshape(expert_devs, local)
    first_slot = (
        jnp.cumsum(grouped, 1) - grouped + jnp.arange(expert_devs, dtype=jnp.int32)[:, None] * chunk
    ).reshape(experts)
    place = jnp.sum(
        jnp.where(onehot, before_count.astype(jnp.int32) + first_slot[None, :], 0), 1
    )
    residual, second, query, keys, values, attended, lse, cot_col, all_counts, places = attend(
        expert_devs, hidden_devs, tokens, project_in, project_out,
        first_gain, first_bias, second_gain, second_bias, place, cotangent, counts,
    )
    all_counts = all_counts[:, :, 0, :experts].reshape(
        hidden_devs, expert_devs, expert_devs, local
    )
    group = lax.axis_index("expert")
    plane = lax.axis_index("hidden")
    group_counts = lax.dynamic_index_in_dim(all_counts, group, 2, keepdims=False)
    most = jnp.max(jnp.sum(all_counts, (1, 3)))

    starts = jnp.cumsum(group_counts, 2) - group_counts
    totals = jnp.sum(group_counts, 1)
    firsts = jnp.cumsum(totals, 1) - totals
    bases = jnp.cumsum(group_counts, 1) - group_counts + firsts[:, None, :]
    slot = jnp.arange(chunk, dtype=jnp.int32)[None, None, :]
    targets = jnp.full((hidden_devs, expert_devs, chunk), -1, jnp.int32)
    for l in range(local):
        offset = slot - starts[:, :, l : l + 1]
        inside = (offset >= 0) & (offset < group_counts[:, :, l : l + 1])
        targets = jnp.where(inside, bases[:, :, l : l + 1] + offset, targets)
    target_rows = lax.dynamic_index_in_dim(targets, plane, 0, keepdims=False)
    target = target_rows.reshape(-1)

    most_rows = expert_devs * chunk
    ends = jnp.cumsum(totals, 1)
    row = jnp.arange(most_rows, dtype=jnp.int32)[None, :]
    eid = sum((row >= ends[:, l : l + 1]).astype(jnp.int32) for l in range(local))
    has = jnp.stack(
        [jnp.any((eid == l).reshape(-1, TILE), 1).astype(jnp.int32) for l in range(local)], 1
    )
    eid = eid.astype(F32)

    def run(rows, pieces, group, number):
        x_all, cot_all, act, dbef, part, _, _, own, _, _, d_second = expert_pass(
            rows, pieces, group, number, room, second, places,
            targets.reshape(hidden_devs, 1, expert_devs * chunk),
            target_rows.reshape(expert_devs, 1, chunk), cot_col,
            eid[:, :rows].reshape(-1, 1), expert_in, expert_out,
        )
        return x_all, cot_all, act, dbef, part, own, d_second, jnp.zeros_like(d_second)

    def run_any():
        send = (place[None, :] == jnp.arange(most_rows, dtype=jnp.int32)[:, None]).astype(BF)
        pack = (target[None, :] == jnp.arange(most_rows, dtype=jnp.int32)[:, None]).astype(BF)

        def gather(values):
            slots = dot(send, values).astype(BF).reshape(expert_devs, chunk, width)
            arrived = lax.all_to_all(slots, "expert", 0, 0, tiled=True)
            packed = dot(pack, arrived.reshape(-1, width)).astype(BF)
            return lax.all_gather(packed, "hidden", axis=0, tiled=True)

        def add_up(partial):
            summed = lax.psum_scatter(partial, "hidden", scatter_dimension=0, tiled=True)
            return dot(pack, summed, ((0,), (0,))).astype(BF).reshape(expert_devs, chunk, width)

        x_rows, cot_rows = gather(second), gather(cotangent)
        act, dbef, part, dmem = expert_rows(
            x_rows, cot_rows, eid.reshape(-1, 1), has, expert_in, expert_out
        )
        returned = lax.all_to_all(add_up(dmem), "expert", 0, 0, tiled=True)
        d_second = dot(send, returned.reshape(-1, width), ((0,), (0,))).astype(BF)
        wide = (hidden_devs, most_rows, width)
        x_rows, cot_rows, act, dbef = (v.reshape(wide) for v in (x_rows, cot_rows, act, dbef))
        returned = lax.all_to_all(add_up(part), "expert", 0, 0, tiled=True)
        produced = dot(send, returned.reshape(-1, width), ((0,), (0,))).astype(BF)
        none = jnp.zeros((hidden_devs, room, width), BF)
        return x_rows, cot_rows, act, dbef, none, none[0], d_second, produced

    plans = [(768, 4, 2, 1), (832, 4, 2, 2), (896, 4, 2, 3)]
    plans = [plan for plan in plans if plan[0] < most_rows and hidden_devs == 4]
    room = max(plan[0] for plan in plans)
    pick = sum((most <= plan[0]).astype(jnp.int32) for plan in plans)
    branches = [run_any] + [functools.partial(run, *plan) for plan in reversed(plans)]
    x_all, cot_all, act, dbef, part, own, d_second, more = lax.switch(pick, branches)

    grad_tokens, summed, small, slots = tail(
        4, expert_devs, hidden_devs, 4, target_rows.reshape(expert_devs, 1, chunk), own, part,
        tokens, residual, d_second, cotangent, query, keys, values,
        attended, lse, project_in, project_out, first_gain, first_bias, second_gain,
    )
    slots, act = lax.optimization_barrier((slots, act))
    returned = lax.all_to_all(slots, "expert", 0, 0, tiled=True)
    slot_of = jnp.arange(most_rows, dtype=jnp.int32)[:, None]
    send = (place[None, :] == slot_of).astype(BF)
    produced = dot(send, returned.reshape(-1, width), ((0,), (0,)))
    block_out = (residual + (produced + more.astype(F32))).astype(BF)
    grad_in, grad_out = spread(summed)
    flat = lambda v: v.reshape(-1, width)
    grad_expert_in, grad_expert_out = expert_grads(
        flat(x_all), flat(cot_all), eid.reshape(-1, 1), has, flat(act), flat(dbef)
    )
    return (
        block_out,
        grad_tokens,
        small[0],
        small[1],
        grad_in,
        grad_out,
        small[2],
        small[3],
        grad_expert_in,
        grad_expert_out,
    )


def solution(mesh):
    rows = P(("expert", "hidden"), None)
    w_in, w_out = P("expert", None, "hidden"), P("expert", "hidden", None)
    return jax.shard_map(
        on_device,
        mesh=mesh,
        in_specs=(
            rows,
            P(("expert", "hidden")),
            P(),
            P(),
            P(),
            P(),
            P(),
            P(),
            P(),
            w_in,
            w_out,
            rows,
        ),
        out_specs=(rows, rows, P(), P(), P(), P(), P(), P(), w_in, w_out),
        check_vma=False,
    )
```

```python
import functools

import jax
import jax.numpy as jnp
from jax import lax
from jax.experimental import pallas as pl
from jax.experimental.pallas import tpu as pltpu
from jax.sharding import PartitionSpec as P

HEADS = 16
HEAD_DIM = 64
TILE = 256
SPAN = 512
BLOCK = 256
QUAD = 256
EPS = 1e-05
BF = jnp.bfloat16
F32 = jnp.float32


def dot(a, b, dims=((1,), (0,))):
    return lax.dot_general(a, b, (dims, ((), ())), preferred_element_type=F32)


def expert_kernel(local_experts, has, x, cot, eid, w_in, w_out, act_o, dbef_o, part_o, dmem_o):
    tile = pl.program_id(0)
    outs = (act_o, dbef_o, part_o, dmem_o)

    @pl.when(has[tile, 0] == 0)
    def _():
        for out in outs:
            out[...] = jnp.zeros(out.shape, out.dtype)

    for expert in range(local_experts):

        @pl.when(has[tile, expert] > 0)
        def _(expert=expert):
            mine = eid[...] == float(expert)
            before = dot(x[...], w_in[expert])
            d_after = dot(cot[...], w_out[expert], ((1,), (1,)))
            square = before * before
            inner = 0.7978845608028654 * before * (1.0 + 0.044715 * square)
            tanh = jnp.tanh(inner)
            half = 0.5 * (1.0 + tanh)
            act = (before * half).astype(BF)
            slope = half + 0.5 * before * (1.0 - tanh * tanh) * (
                0.7978845608028654 * (1.0 + 0.134145 * square)
            )
            dbef = (d_after * slope).astype(BF)
            part = dot(act, w_out[expert])
            dmem = dot(dbef, w_in[expert], ((1,), (1,)))
            news = (act.astype(F32), dbef.astype(F32), part, dmem)
            for out, new in zip(outs, news):
                old = 0.0 if expert == 0 else out[...].astype(F32)
                out[...] = jnp.where(mine, new, old).astype(BF)


def expert_rows(x, cot, eid, has, w_in, w_out):
    rows, width = x.shape
    experts, _, hidden = w_in.shape
    tiles = rows // TILE
    row_block = pl.BlockSpec((TILE, width), lambda t, has: (t, 0))
    hid_block = pl.BlockSpec((TILE, hidden), lambda t, has: (t, 0))
    whole = lambda shape: pl.BlockSpec(shape, lambda t, has: (0, 0, 0), pipeline_mode=pl.Buffered(1))
    return pl.pallas_call(
        functools.partial(expert_kernel, experts),
        grid_spec=pltpu.PrefetchScalarGridSpec(
            num_scalar_prefetch=1,
            grid=(tiles,),
            in_specs=[
                row_block,
                row_block,
                pl.BlockSpec((TILE, 1), lambda t, has: (t, 0)),
                whole(w_in.shape),
                whole(w_out.shape),
            ],
            out_specs=[hid_block, hid_block, row_block, row_block],
        ),
        out_shape=[
            jax.ShapeDtypeStruct((rows, hidden), BF),
            jax.ShapeDtypeStruct((rows, hidden), BF),
            jax.ShapeDtypeStruct((rows, width), BF),
            jax.ShapeDtypeStruct((rows, width), BF),
        ],
        compiler_params=pltpu.CompilerParams(vmem_limit_bytes=56 * 2**20),
        cost_estimate=pl.CostEstimate(
            flops=8 * rows * width * hidden,
            bytes_accessed=2 * (w_in.size + w_out.size + 6 * rows * width),
            transcendentals=rows * hidden,
        ),
        name="expert_rows",
    )(has, x, cot, eid, w_in, w_out)


def expert_grad_kernel(owner, tile, count, x, cot, eid, act, dbef, g_in, g_out):
    visit = pl.program_id(0)
    expert = owner[visit]

    @pl.when((visit == 0) | (owner[jnp.maximum(visit - 1, 0)] != expert))
    def _():
        g_in[...] = jnp.zeros(g_in.shape, F32)
        g_out[...] = jnp.zeros(g_out.shape, F32)

    @pl.when(visit < count[0])
    def _():
        mine = jnp.where(eid[...] == expert.astype(F32), 1.0, 0.0).astype(BF)
        g_in[0] += dot(x[...], dbef[...] * mine, ((0,), (0,)))
        g_out[0] += dot(act[...] * mine, cot[...], ((0,), (0,)))


def expert_grads(x, cot, eid, has, act, dbef):
    rows, width = x.shape
    hidden = act.shape[1]
    tiles, experts = has.shape
    wanted = has.at[0].set(1).T.reshape(-1)
    order = jnp.cumsum(wanted) - 1
    most = tiles + experts * 4
    count = jnp.sum(wanted).reshape(1)
    visit = jnp.minimum(jnp.arange(most, dtype=jnp.int32), count - 1)
    chosen = (wanted[None, :] > 0) & (order[None, :] == visit[:, None])
    index = jnp.sum(jnp.where(chosen, jnp.arange(tiles * experts, dtype=jnp.int32)[None, :], 0), 1)
    owner, tile = index // tiles, index % tiles
    row_block = pl.BlockSpec((TILE, width), lambda v, owner, tile, count: (tile[v], 0))
    hid_block = pl.BlockSpec((TILE, hidden), lambda v, owner, tile, count: (tile[v], 0))
    return pl.pallas_call(
        expert_grad_kernel,
        grid_spec=pltpu.PrefetchScalarGridSpec(
            num_scalar_prefetch=3,
            grid=(most,),
            in_specs=[
                row_block,
                row_block,
                pl.BlockSpec((TILE, 1), lambda v, owner, tile, count: (tile[v], 0)),
                hid_block,
                hid_block,
            ],
            out_specs=[
                pl.BlockSpec((1, width, hidden), lambda v, owner, tile, count: (owner[v], 0, 0)),
                pl.BlockSpec((1, hidden, width), lambda v, owner, tile, count: (owner[v], 0, 0)),
            ],
        ),
        out_shape=[
            jax.ShapeDtypeStruct((experts, width, hidden), F32),
            jax.ShapeDtypeStruct((experts, hidden, width), F32),
        ],
        compiler_params=pltpu.CompilerParams(vmem_limit_bytes=56 * 2**20),
        cost_estimate=pl.CostEstimate(
            flops=2 * rows * width * hidden,
            bytes_accessed=8 * experts * width * hidden + 6 * rows * width,
            transcendentals=0,
        ),
        name="expert_grads",
    )(owner, tile, count, x, cot, eid, act, dbef)


MESH = pl.DeviceIdType.MESH


def remote(src, dst, send_sem, recv_sem, device):
    return pltpu.make_async_remote_copy(
        src_ref=src,
        dst_ref=dst,
        send_sem=send_sem,
        recv_sem=recv_sem,
        device_id=device,
        device_id_type=MESH,
    )


def position(plane):
    side = lax.div(plane, 2)
    return side, plane + side * (3 - 2 * plane)


def ones_where(mask):
    return jnp.where(mask, 1.0, 0.0).astype(BF)


def halves(pair):
    left = lax.broadcasted_iota(jnp.int32, pair.shape, 1) < HEAD_DIM
    zero = jnp.zeros_like(pair)
    return (jnp.where(left, pair, zero), jnp.where(left, zero, pair))


def join(first, second):
    left = lax.broadcasted_iota(jnp.int32, first.shape, 1) < HEAD_DIM
    return jnp.where(left, first, second)


def tri(block):
    later = lax.broadcasted_iota(jnp.int32, (block, block), 1)
    return later <= lax.broadcasted_iota(jnp.int32, (block, block), 0)


def normalise(values):
    centered = values - jnp.mean(values, -1, keepdims=True)
    spread = jnp.mean(centered * centered, -1, keepdims=True)
    root = lax.rsqrt(spread + EPS)
    return centered * root, root


def attend_kernel(
    tokens, w_q, w_k, w_v, w_o, gain1, bias1, gain2, bias2, place, cot, counts,
    residual, second, q_out, k_out, v_out, att_out, lse, cot_col, all_counts, places,
    normed, known, known_places, col_send, col_recv, near_send, near_recv, far_send, far_recv,
    place_send, place_recv, local_sem,
):
    step = pl.program_id(0)
    rows = tokens.shape[0]
    lanes = 2 * HEAD_DIM
    me, plane = lax.axis_index("expert"), lax.axis_index("hidden")
    planes, devices = known.shape[:2]
    side, r = position(plane)
    middle = r == 1
    step_up = 1 - 2 * side
    up, down = {"hidden": plane + step_up}, {"hidden": plane - step_up}
    other = lambda off: {"expert": lax.rem(me + off, devices)}
    across = lambda off: {"hidden": lax.rem(plane + off, planes)}
    sender = lambda off: lax.rem(me - off + devices, devices)

    def col_copy(way, below):
        piece = cot_col.at[plane]
        return remote(cot, piece, col_send.at[way], col_recv.at[below], down if way else up)

    def place_copy(off, source):
        piece = known_places.at[source]
        return remote(piece, piece, place_send.at[off], place_recv.at[off], across(off))

    def near_copy(off, source):
        piece = known.at[plane, source]
        return remote(piece, piece, near_send.at[off], near_recv.at[off], other(off))

    def far_copy(off, source):
        piece = known.at[source]
        return remote(piece, piece, far_send.at[off], far_recv.at[off], across(off))

    def own_copy():
        return pltpu.make_async_copy(cot, cot_col.at[plane], local_sem)

    def each(act, count):
        def body(off, carry):
            act(off)
            return carry

        lax.fori_loop(1, count, body, 0)

    @pl.when(step == 0)
    def _():
        barrier = pltpu.get_barrier_semaphore()

        def greet(device):
            pl.semaphore_signal(barrier, inc=1, device_id=device, device_id_type=MESH)

        each(lambda off: greet(other(off)), devices)
        each(lambda off: greet(across(off)), planes)
        known[plane, me] = counts[...]
        known_places[plane] = jnp.broadcast_to(place[...], known_places.shape[1:])
        pl.semaphore_wait(barrier, devices + planes - 2)
        each(lambda off: near_copy(off, me).start(), devices)
        each(lambda off: place_copy(off, plane).start(), planes)

        @pl.when(r == 0)
        def _():
            col_copy(0, 0).start()

        @pl.when(middle)
        def _():
            col_copy(0, 1).start()
            col_copy(1, 1).start()

        own_copy().start()

    @pl.when(step == 1)
    def _():
        each(lambda off: near_copy(off, sender(off)).wait_recv(), devices)
        each(lambda off: far_copy(off, plane).start(), planes)

    @pl.when(step == 0)
    def _():
        source = tokens[...].astype(F32)
        normed[...] = (normalise(source)[0] * gain1[...] + bias1[...]).astype(BF)
        residual[...] = source
        lse[...] = jnp.zeros(lse.shape, F32)

    q_out[0] = dot(normed[...], w_q[...]).astype(BF)
    k_out[0] = dot(normed[...], w_k[...]).astype(BF)
    v_out[0] = dot(normed[...], w_v[...]).astype(BF)
    width = q_out.shape[2]
    keep = tri(BLOCK)
    lane = lax.broadcasted_iota(jnp.int32, (BLOCK, lse.shape[1]), 1)
    for pair in range(width // lanes):
        cols = slice(pair * lanes, (pair + 1) * lanes)
        query = q_out[0, :, cols] * jnp.asarray(HEAD_DIM**-0.5, BF)
        keys = halves(k_out[0, :, cols])
        values = v_out[0, :, cols]
        for q_block in range(rows // BLOCK):
            q_rows = slice(q_block * BLOCK, (q_block + 1) * BLOCK)
            results = []
            for head in range(2):
                scores = []
                for k_block in range(q_block + 1):
                    k_rows = slice(k_block * BLOCK, (k_block + 1) * BLOCK)
                    part = dot(query[q_rows], keys[head][k_rows], ((1,), (1,)))
                    scores.append(jnp.where(keep, part, -1e30) if k_block == q_block else part)
                top = functools.reduce(jnp.maximum, [jnp.max(s, -1, keepdims=True) for s in scores])
                weights = [jnp.exp(s - top) for s in scores]
                total = sum(jnp.sum(w, -1, keepdims=True) for w in weights)
                share = 1.0 / total
                out = sum(
                    dot((w * share).astype(BF), values[k * BLOCK : (k + 1) * BLOCK])
                    for k, w in enumerate(weights)
                )
                results.append(out)
                index = step * (width // HEAD_DIM) + 2 * pair + head
                lse[q_rows, :] = jnp.where(lane == index, top + jnp.log(total), lse[q_rows, :])
            att_out[0, q_rows, cols] = join(*results).astype(BF)
    residual[...] += dot(att_out[0], w_o[...])

    @pl.when(step == pl.num_programs(0) - 1)
    def _():
        second[...] = (normalise(residual[...])[0] * gain2[...] + bias2[...]).astype(BF)
        each(lambda off: far_copy(off, lax.rem(plane - off + planes, planes)).wait_recv(), planes)
        each(lambda off: place_copy(off, lax.rem(plane - off + planes, planes)).wait_recv(), planes)
        all_counts[...] = known[...]
        places[...] = known_places[...]
        own_copy().wait()
        col_copy(0, 1).wait_recv()
        col_copy(0, 0).wait_send()

        @pl.when(middle)
        def _():
            col_copy(0, 0).wait_recv()
            col_copy(1, 1).wait_send()

        each(lambda off: place_copy(off, plane).wait_send(), planes)
        each(lambda off: near_copy(off, me).wait_send(), devices)
        each(lambda off: far_copy(off, plane).wait_send(), planes)


def attend(
    devices, planes, tokens, project_in, project_out, gain1, bias1, gain2, bias2, place, cot, counts
):
    rows, width = tokens.shape
    dma = pltpu.SemaphoreType.DMA
    counts = jnp.broadcast_to(jnp.pad(counts, (0, 128 - counts.shape[0]))[None, :], (8, 128))
    known = (planes, devices, 8, 128)
    steps = width // QUAD
    whole = lambda shape: pl.BlockSpec(shape, lambda j: (0, 0))
    third = lambda k: pl.BlockSpec((width, QUAD), lambda j: (0, k * steps + j))
    cols = pl.BlockSpec((1, rows, QUAD), lambda j: (j, 0, 0))
    vector = whole((1, width))
    low = jax.ShapeDtypeStruct((rows, width), BF)
    split = jax.ShapeDtypeStruct((steps, rows, QUAD), BF)
    return pl.pallas_call(
        attend_kernel,
        grid=(steps,),
        in_specs=[whole((rows, width)), third(0), third(1), third(2),
            pl.BlockSpec((QUAD, width), lambda j: (j, 0)), vector, vector, vector, vector,
            whole((1, rows)), whole((rows, width)), whole((8, 128))],
        out_specs=[whole((rows, width)), whole((rows, width)), cols, cols, cols, cols, whole((rows, 128)),
            pl.BlockSpec(memory_space=pl.ANY), pl.BlockSpec(known, lambda j: (0, 0, 0, 0)),
            pl.BlockSpec((planes, 8, rows), lambda j: (0, 0, 0))],
        out_shape=[jax.ShapeDtypeStruct((rows, width), F32), low, split, split, split, split,
            jax.ShapeDtypeStruct((rows, 128), F32), jax.ShapeDtypeStruct((planes, rows, width), BF),
            jax.ShapeDtypeStruct(known, jnp.int32), jax.ShapeDtypeStruct((planes, 8, rows), jnp.int32)],
        scratch_shapes=[pltpu.VMEM((rows, width), BF), pltpu.VMEM(known, jnp.int32),
            pltpu.VMEM((planes, 8, rows), jnp.int32), dma((2,)), dma((2,)), dma((devices,)), dma((devices,)),
            dma((planes,)), dma((planes,)), dma((planes,)), dma((planes,)), dma],
        compiler_params=pltpu.CompilerParams(
            collective_id=0, has_side_effects=True, vmem_limit_bytes=56 * 2**20
        ),
        cost_estimate=pl.CostEstimate(flops=10 * rows * width * width, bytes_accessed=20 * 2**20,
            transcendentals=HEADS * rows * rows),
        name="attend",
    )(tokens, project_in, project_in, project_in, project_out, *(v.reshape(1, width) for v in (gain1, bias1, gain2, bias2)),
        place.reshape(1, rows), cot, counts)


def layer_norm_back(d_normed, xhat, root, gain):
    scaled = d_normed * gain
    d_values = root * (
        scaled
        - jnp.mean(scaled, -1, keepdims=True)
        - xhat * jnp.mean(scaled * xhat, -1, keepdims=True)
    )
    sums = (jnp.sum(d_normed * xhat, 0, keepdims=True), jnp.sum(d_normed, 0, keepdims=True))
    return d_values, sums


def pass_kernel(
    rows, pieces, group,
    x, places, targets, target_rows, cot_col, ends, w_in, w_out,
    x_all, cot_all, act_o, dbef_o, part_o, slope_o, o_down, o_up, own_out, cot_far, cot_slots, d_second,
    slots, arrived, packed_x, packed_c, dense, returned, d_part, from_down, from_up, x_tile, c_tile, stage,
    plane_send, plane_recv, cot_send, cot_recv, far_send, far_recv, back_send, back_recv, ag_send, ag_recv,
    rs_send, rs_down, rs_up, os_send, os_down, os_up, local_sem, stage_sem, own_sem, dense_sem,
):
    me, plane = lax.axis_index("expert"), lax.axis_index("hidden")
    _, devices, chunk, width = slots.shape
    experts = w_in.shape[0]
    height = rows // pieces
    tile_height = group * height
    tiles = pieces // group
    side, r = position(plane)
    middle, end = r == 1, r == 0
    step = 1 - 2 * side
    up, down = {"hidden": plane + step}, {"hidden": plane - step}
    physical = lambda rel: rel + side * (3 - 2 * rel)
    part_of = lambda j: pl.ds(pl.multiple_of(j * height, 16), height)
    tile_of = lambda i: pl.ds(pl.multiple_of(i * tile_height, 16), tile_height)
    peer_of = lambda off: lax.rem(me + off, devices)
    source_of = lambda off: lax.rem(me - off + devices, devices)

    def each(act, first, last):
        def body(i, carry):
            act(i)
            return carry

        lax.fori_loop(first, last, body, 0)

    def forward_rel(p):
        return jnp.where(end | (p > 2), p, jnp.where(p == 0, 1, jnp.where(p == 1, 2, 0)))

    def cot_rel(n):
        at_middle = jnp.where(n == 0, 2, jnp.where(n == 1, 0, jnp.where(n == 2, 3, 1)))
        return jnp.where(end, lax.rem(n + 1, 4), at_middle)

    barrier = pltpu.get_barrier_semaphore()
    greet = lambda device: pl.semaphore_signal(barrier, inc=1, device_id=device, device_id_type=MESH)
    each(lambda off: greet({"expert": peer_of(off)}), 1, devices)
    greet(up)

    @pl.when(middle)
    def _():
        greet(down)

    pl.semaphore_wait(barrier, devices + r)

    def far_copy(index):
        block = physical((0, 2, 3)[index])
        source = (cot_far if index == 2 else cot_col).at[block]
        device = down if index else up
        return remote(source, cot_far.at[block], far_send.at[index], far_recv.at[index], device)

    @pl.when(middle)
    def _():
        far_copy(0).start()
        far_copy(1).start()

    def slots_of(device, block, values):
        row = lax.broadcasted_iota(jnp.int32, (chunk, x.shape[0]), 0) + device * chunk
        return dot(ones_where(row == places[block, 0:1, :]), values[...]).astype(BF)

    def dispatch_copy(off, to, frm):
        return remote(
            slots.at[0, to], arrived.at[frm], plane_send.at[off], plane_recv.at[off], {"expert": to}
        )

    def dispatch(off):
        peer = peer_of(off)
        slots[0, peer] = slots_of(peer, plane, x)
        dispatch_copy(off, peer, me).start()

    each(dispatch, 1, devices)
    arrived[me] = slots_of(me, plane, x)

    def cot_copy(n, off, to, frm):
        slot = lax.rem(n + 1, 2)
        return remote(
            slots.at[slot, to], cot_slots.at[n, frm], cot_send.at[n, off], cot_recv.at[n, off], {"expert": to}
        )

    def cot_own(n):
        return pltpu.make_async_copy(slots.at[lax.rem(n + 1, 2), me], cot_slots.at[n, me], own_sem.at[n])

    def cot_sent(n):
        each(lambda off: cot_copy(n, off, peer_of(off), me).wait_send(), 1, devices)

    def send_cot(n, far):
        block = physical(cot_rel(n))

        def fetch(source):
            one = pltpu.make_async_copy(source.at[block], dense, dense_sem)
            one.start()
            one.wait()

        @pl.when(far)
        def _():
            fetch(cot_far)

        @pl.when(jnp.logical_not(far))
        def _():
            fetch(cot_col)

        def fill(off):
            peer = peer_of(off)
            slots[lax.rem(n + 1, 2), peer] = slots_of(peer, block, dense)
            cot_copy(n, off, peer, me).start()

        each(fill, 1, devices)
        slots[lax.rem(n + 1, 2), me] = slots_of(me, block, dense)
        cot_own(n).start()

    send_cot(jnp.int32(0), jnp.bool_(False))

    def pack(block, j):
        row = lax.broadcasted_iota(jnp.int32, (height, devices * chunk), 0) + j * height
        flat = arrived[...].reshape(devices * chunk, width)
        return dot(ones_where(row == targets[block]), flat).astype(BF)

    def gather_copy(way, block, j, own):
        source = packed_x.at[part_of(j)] if own else x_all.at[block, part_of(j)]
        return remote(
            source, x_all.at[block, part_of(j)], ag_send.at[way, block, j], ag_recv.at[block, j], down if way else up
        )

    @pl.when(middle)
    def _():
        far_copy(0).wait_recv()
        far_copy(2).start()

    each(lambda off: dispatch_copy(off, me, source_of(off)).wait_recv(), 1, devices)

    def send_own(j):
        packed_x[part_of(j)] = pack(plane, j)
        gather_copy(0, plane, j, True).start()

        @pl.when(middle)
        def _():
            gather_copy(1, plane, j, True).start()

    each(send_own, 0, pieces)
    keep_own = pltpu.make_async_copy(packed_x, x_all.at[plane, pl.ds(0, rows)], local_sem.at[0])
    keep_own.start()

    keep_own.wait()

    def got(rel, j):
        gather_copy(0, physical(rel), j, False).wait_recv()

    def relay(rel, way, j):
        got(rel, j)
        gather_copy(way, physical(rel), j, False).start()

    def keep_cot(n):
        there = cot_all.at[physical(cot_rel(n)), pl.ds(0, rows)]
        return pltpu.make_async_copy(packed_c, there, local_sem.at[1])

    def collect_cot(n):
        block = physical(cot_rel(n))

        @pl.when(n > 1)
        def _():
            cot_own(n).wait()

        each(lambda off: cot_copy(n, off, me, source_of(off)).wait_recv(), 1, devices)
        fetch = pltpu.make_async_copy(cot_slots.at[n], arrived, dense_sem)
        fetch.start()

        @pl.when(n > 0)
        def _():
            keep_cot(n).wait()

        fetch.wait()

        def one(j):
            packed_c[part_of(j)] = pack(block, j)

        each(one, 0, pieces)
        keep_cot(n).start()

    def sum_copy(rel, j, buffer, index, sems, device):
        return remote(
            d_part.at[physical(rel), part_of(j)],
            buffer.at[index, part_of(j)],
            rs_send.at[rel, j],
            sems.at[index, j],
            device,
        )

    def add(rel, j, buffer, index, sems):
        sum_copy(rel, j, buffer, index, sems, up).wait_recv()
        block = physical(rel)
        here = d_part[block, part_of(j)].astype(F32)
        d_part[block, part_of(j)] = (here + buffer[index, part_of(j)].astype(F32)).astype(BF)

    def out_copy(rel, j, source, buffer, index, sems, device):
        return remote(
            source, buffer.at[index, part_of(j)], os_send.at[rel, j], sems.at[index, j], device
        )

    def out_send(rel, j):
        source = part_o.at[physical(rel), part_of(j)]
        out_copy(rel, j, source, o_down, rel - 1, os_down, up).start()

    def out_sum(rel, j, buffers):
        pads = [t.at[pl.ds(0, height)] for t in (x_tile, c_tile, stage.at[0])]
        loads = [pltpu.make_async_copy(part_o.at[physical(rel), part_of(j)], pads[0], stage_sem.at[0])]
        loads[0].start()
        for n, (buffer, index, sems) in enumerate(buffers):
            piece = buffer.at[index, part_of(j)]
            out_copy(rel, j, piece, buffer, index, sems, up).wait_recv()
            loads.append(pltpu.make_async_copy(piece, pads[n + 1], stage_sem.at[n + 1]))
            loads[-1].start()
        for load in loads:
            load.wait()
        return sum(t[...].astype(F32) for t in pads[: len(loads)]).astype(BF)

    def out_relay(j):
        held = from_down.at[1, part_of(j)]
        held[...] = out_sum(2, j, [(o_down, 1, os_down)])
        out_copy(2, j, held, o_up, 1, os_up, up).start()

    outs = (act_o, dbef_o, part_o, slope_o)

    def stage_copy(index, block, i):
        return pltpu.make_async_copy(
            stage.at[index], outs[index].at[block, tile_of(i)], stage_sem.at[index]
        )

    def load(array, block, i):
        one = pltpu.make_async_copy(array.at[block, tile_of(i)], x_tile, local_sem.at[0])
        one.start()
        one.wait()

    def chooser(block, i):
        row = lax.broadcasted_iota(jnp.int32, (tile_height, 1), 0) + i * tile_height
        before = [row < ends[block, e : e + 1, 0:1] for e in range(experts)]
        mine = [before[e] & jnp.logical_not(before[e - 1]) if e else before[0] for e in range(experts)]

        def choose(results):
            total = jnp.where(mine[0], results[0], 0.0)
            for mask, result in zip(mine[1:], results[1:]):
                total = jnp.where(mask, result, total)
            return total

        return choose

    def columns(body):
        def one(n, carry):
            body(pl.ds(pl.multiple_of(n * SPAN, SPAN), SPAN))
            return carry

        lax.fori_loop(0, width // SPAN, one, 0)

    def staged(block, i):
        for index in (0, 2, 3):
            stage_copy(index, block, i).wait()

    def forward_tile(block, i):
        load(x_all, block, i)
        choose = chooser(block, i)

        @pl.when(i > 0)
        def _():
            staged(block, i)

        def activate(cols):
            before = choose([dot(x_tile[...], w_in[e, :, cols]) for e in range(experts)])
            square = before * before
            tanh = jnp.tanh(0.7978845608028654 * before * (1.0 + 0.044715 * square))
            half = 0.5 * (1.0 + tanh)
            slope = half + 0.5 * before * (1.0 - tanh * tanh) * (
                0.7978845608028654 * (1.0 + 0.134145 * square)
            )
            stage[0, :, cols] = (before * half).astype(BF)
            stage[3, :, cols] = slope.astype(BF)

        def produce(cols):
            results = [dot(stage[0], w_out[e, :, cols]) for e in range(experts)]
            stage[2, :, cols] = choose(results).astype(BF)

        columns(activate)
        columns(produce)
        for index in (0, 2, 3):
            stage_copy(index, block, i).start()

    def backward_tile(block, i, first):
        load(slope_o, block, i)
        choose = chooser(block, i)

        @pl.when(jnp.logical_not(first))
        def _():
            stage_copy(1, block, i).wait()

        def before_back(cols):
            results = [dot(packed_c[tile_of(i)], w_out[e, cols, :], ((1,), (1,))) for e in range(experts)]
            stage[1, :, cols] = (choose(results) * x_tile[:, cols].astype(F32)).astype(BF)

        def members_back(cols):
            results = [dot(stage[1], w_in[e, cols, :], ((1,), (1,))) for e in range(experts)]
            d_part[block, tile_of(i), cols] = choose(results).astype(BF)

        columns(before_back)
        stage_copy(1, block, i).start()
        columns(members_back)

    def phase(p, carry):
        def come(j):
            @pl.when((p == 1) & middle)
            def _():
                relay(0, 0, j)
                relay(2, 1, j)

            @pl.when((p == 2) & middle)
            def _():
                relay(3, 1, j)

            @pl.when((p > 0) & (p < 4) & end)
            def _():
                got(p, j)

        def ahead(i):
            each(come, i * group, (i + 1) * group)

            @pl.when(p < 4)
            def _():
                forward_tile(physical(forward_rel(p)), i)

            @pl.when((p == 3) & middle)
            def _():
                def pass_on(j):
                    add(2, j, from_down, 1, rs_down)
                    sum_copy(2, j, from_up, 1, rs_up, up).start()

                each(pass_on, i * group, (i + 1) * group)

        each(ahead, 0, tiles)

        @pl.when(p < 4)
        def _():
            staged(plane, 0)

        @pl.when(p < 3)
        def _():
            @pl.when(p == 0)
            def _():
                each(lambda off: dispatch_copy(off, peer_of(off), me).wait_send(), 1, devices)

            @pl.when(p > 0)
            def _():
                cot_sent(p - 1)
                cot_own(p - 1).wait()

            @pl.when((p == 0) & end)
            def _():
                far_copy(1).wait_recv()

            @pl.when((p == 1) & end)
            def _():
                far_copy(2).wait_recv()

            send_cot(p + 1, (p == 1) | ((p == 0) & end))

        @pl.when(p == 4)
        def _():
            @pl.when(end)
            def _():
                each(lambda j: out_send(2, j), 0, pieces)
                each(lambda j: out_send(1, j), 0, pieces)

        rel = cot_rel(p - 1)

        def go(j):
            @pl.when((p < 4) & end)
            def _():
                sum_copy(rel, j, from_down, rel - 1, rs_down, up).start()

            @pl.when((p == 4) & middle)
            def _():
                add(3, j, from_down, 2, rs_down)
                sum_copy(3, j, from_up, 0, rs_up, up).start()

            @pl.when((p == 4) & middle & (j > 0))
            def _():
                add(0, j - 1, from_up, 0, rs_up)
                sum_copy(0, j - 1, from_up, 0, rs_up, down).start()

        def behind(i):
            backward_tile(physical(rel), i, (p == 1) & (i == 0))
            each(go, i * group, (i + 1) * group)

        @pl.when(p > 0)
        def _():
            collect_cot(p - 1)
            each(behind, 0, tiles)

        return carry

    lax.fori_loop(0, 5, phase, 0)
    stage_copy(1, plane, 0).wait()
    keep_cot(jnp.int32(3)).wait()

    @pl.when(middle)
    def _():
        add(0, pieces - 1, from_up, 0, rs_up)
        sum_copy(0, pieces - 1, from_up, 0, rs_up, down).start()

    def last(j):
        @pl.when(middle)
        def _():
            add(1, j, from_down, 0, rs_down)
            add(1, j, from_up, 1, rs_up)

        @pl.when(end)
        def _():
            add(0, j, from_up, 0, rs_up)

    each(last, 0, pieces)

    cot_sent(jnp.int32(2))

    def back_slots(device):
        row = lax.broadcasted_iota(jnp.int32, (rows, chunk), 0)
        return dot(ones_where(row == target_rows[device]), d_part[plane], ((0,), (0,))).astype(BF)

    def back_copy(off, to, frm):
        return remote(
            slots.at[1, to], returned.at[frm], back_send.at[off], back_recv.at[off], {"expert": to}
        )

    def back(off):
        peer = peer_of(off)
        slots[1, peer] = back_slots(peer)
        back_copy(off, peer, me).start()

    each(back, 1, devices)
    returned[me] = back_slots(me)

    @pl.when(middle)
    def _():
        each(out_relay, 0, pieces)

    each(lambda off: back_copy(off, me, source_of(off)).wait_recv(), 1, devices)
    slot = lax.broadcasted_iota(jnp.int32, (devices * chunk, x.shape[0]), 0)
    flat = returned[...].reshape(devices * chunk, width)
    d_second[...] = dot(ones_where(slot == places[plane, 0:1, :]), flat, ((0,), (0,))).astype(BF)

    @pl.when(middle)
    def _():
        def out_last(j):
            d_part[plane, part_of(j)] = out_sum(1, j, [(o_down, 0, os_down), (o_up, 1, os_up)])

        each(out_last, 0, pieces)

    @pl.when(end)
    def _():
        own = pltpu.make_async_copy(part_o.at[plane, pl.ds(0, rows)], d_part.at[plane], local_sem.at[0])
        own.start()
        own.wait()

    own = pltpu.make_async_copy(d_part.at[plane], own_out.at[pl.ds(0, rows)], local_sem.at[1])
    own.start()

    x_tile[...] = jnp.zeros(x_tile.shape, BF)
    whole_tiles = -(-rows // TILE) * TILE
    fills = []
    for array, stop in [(a, whole_tiles) for a in (x_all, cot_all, act_o, dbef_o)] + [(part_o, part_o.shape[1])]:
        for block in range(4):
            for start in range(rows, stop, tile_height):
                fills.append(array.at[block, pl.ds(start, min(tile_height, stop - start))])
    for start in range(rows, own_out.shape[0], tile_height):
        fills.append(own_out.at[pl.ds(start, min(tile_height, own_out.shape[0] - start))])
    for there in fills:
        fill = pltpu.make_async_copy(x_tile.at[pl.ds(0, there.shape[0])], there, local_sem.at[0])
        fill.start()
        fill.wait()
    own.wait()

    each(lambda off: back_copy(off, peer_of(off), me).wait_send(), 1, devices)
    cot_sent(jnp.int32(3))

    @pl.when(middle)
    def _():
        for index in range(3):
            far_copy(index).wait_send()

    def sent(j):
        gather_copy(0, plane, j, True).wait_send()

        @pl.when(middle)
        def _():
            gather_copy(1, plane, j, True).wait_send()
            gather_copy(0, physical(0), j, False).wait_send()
            for rel in (2, 3):
                gather_copy(1, physical(rel), j, False).wait_send()
            for rel in (0, 2, 3):
                sum_copy(rel, j, from_up, 0, rs_up, up).wait_send()
            out_copy(2, j, part_o.at[0, part_of(j)], o_up, 1, os_up, up).wait_send()

        @pl.when(end)
        def _():
            for rel in (1, 2, 3):
                sum_copy(rel, j, from_up, 0, rs_up, up).wait_send()
            for rel in (1, 2):
                out_copy(rel, j, part_o.at[0, part_of(j)], o_up, 1, os_up, up).wait_send()

    each(sent, 0, pieces)


def expert_pass(rows, pieces, group, number, room, x, places, targets, target, cot_col, ends, w_in, w_out):
    devices, _, chunk = target.shape
    width, hidden = w_in.shape[1:]
    planes = cot_col.shape[0]
    height = rows // pieces
    tall = group * height
    here, there = pl.BlockSpec(memory_space=pltpu.VMEM), pl.BlockSpec(memory_space=pl.ANY)
    dma = pltpu.SemaphoreType.DMA
    low = lambda *shape: jax.ShapeDtypeStruct(shape, BF)
    held = lambda *shape: pltpu.VMEM(shape, BF)
    wide = low(planes, devices * chunk, width)
    return pl.pallas_call(
        functools.partial(pass_kernel, rows, pieces, group),
        in_specs=[here] * 4 + [there] + [here] * 3,
        out_specs=[there] * 11 + [here],
        out_shape=[wide] * 4
        + [low(planes, room, width), low(planes, rows, hidden), low(3, rows, width), low(2, rows, width), low(room, width)]
        + [low(*cot_col.shape), low(planes, devices, chunk, width), low(*x.shape)],
        scratch_shapes=[
            held(2, devices, chunk, width),
            held(devices, chunk, width),
            held(rows, width),
            held(rows, width),
            held(*x.shape),
            held(devices, chunk, width),
            held(planes, rows, width),
            held(3, rows, width),
            held(2, rows, width),
            held(tall, width),
            held(height, width),
            held(4, tall, hidden),
            dma((devices,)),
            dma((devices,)),
            dma((planes, devices)),
            dma((planes, devices)),
            dma((3,)),
            dma((3,)),
            dma((devices,)),
            dma((devices,)),
            dma((2, planes, pieces)),
            dma((planes, pieces)),
            dma((planes, pieces)),
            dma((3, pieces)),
            dma((2, pieces)),
            dma((planes, pieces)),
            dma((3, pieces)),
            dma((2, pieces)),
            dma((2,)),
            dma((4,)),
            dma((planes,)),
            dma,
        ],
        compiler_params=pltpu.CompilerParams(
            collective_id=number, has_side_effects=True, vmem_limit_bytes=62 * 2**20
        ),
        cost_estimate=pl.CostEstimate(
            flops=20 * planes * rows * width * hidden,
            bytes_accessed=16 * planes * rows * width,
            transcendentals=planes * rows * hidden,
        ),
        name="expert_pass",
    )(x, places, targets, target, cot_col, ends, w_in, w_out)


def tail_kernel(
    pieces,
    tokens, residual, d_second, cot, q, k, v, att, lse, project_in, project_out, gain1, bias1, gain2,
    target_rows, own_in, partial,
    grad_tokens, summed_grads, small_out, out_slots,
    w_in, w_out, normed, d_branch, d_normed, grads, small, small_plane, small_near, small_far,
    core_buf, half_buf, plane_buf, own, o_far, o_near, mine, slot_tile,
    o_send, o_recv, out_sem, slot_sem,
    ar_send, ar_recv, near_send, near_recv, far_send, far_recv,
    w_sem, local_sem,
):
    me, plane = lax.axis_index("expert"), lax.axis_index("hidden")
    devices, planes = lax.axis_size("expert"), lax.axis_size("hidden")
    width = tokens.shape[1]
    quads, tall, quad = grads.shape
    other = lambda off: {"expert": lax.rem(me + off, devices)}
    across = lambda off: {"hidden": lax.rem(plane + off, planes)}

    barrier = pltpu.get_barrier_semaphore()

    def greet(off, carry):
        pl.semaphore_signal(barrier, inc=1, device_id=other(off), device_id_type=MESH)
        return carry

    lax.fori_loop(1, devices, greet, 0)
    for off in range(1, planes):
        pl.semaphore_signal(barrier, inc=1, device_id=across(off), device_id_type=MESH)

    def weights(j, slot):
        cols = lambda third: pl.ds(pl.multiple_of(third * width + j * quad, quad), quad)
        copies = [
            pltpu.make_async_copy(project_in.at[:, cols(third)], w_in.at[slot, third], w_sem.at[slot, third])
            for third in range(3)
        ]
        rows_out = pl.ds(pl.multiple_of(j * quad, quad), quad)
        copies.append(pltpu.make_async_copy(project_out.at[rows_out], w_out.at[slot], w_sem.at[slot, 3]))
        return copies

    for copy in weights(0, 0):
        copy.start()
    pl.semaphore_wait(barrier, devices - 1 + planes - 1)

    rows = own.shape[0]
    height = rows // pieces
    side = lax.div(plane, 2)
    r = plane + side * (3 - 2 * plane)
    middle = r == 1
    step = 1 - 2 * side
    up, down = {"hidden": plane + step}, {"hidden": plane - step}
    physical = lambda rel: rel + side * (3 - 2 * rel)
    part_of = lambda j: pl.ds(pl.multiple_of(j * height, 16), height)

    def out_copy(kind, j):
        source = partial.at[physical(3), part_of(j)] if kind == 0 else mine.at[kind - 1, part_of(j)]
        there = (o_far if kind == 0 else o_near).at[part_of(j)]
        return remote(source, there, o_send.at[kind, j], o_recv.at[kind, j], down if kind == 2 else up)

    def out_load(index):
        source = own_in if index == 2 else partial.at[physical(3 - 3 * index)]
        return pltpu.make_async_copy(source, own if index == 2 else mine.at[index], out_sem.at[index])

    @pl.when(r == 0)
    def _():
        def body(j, carry):
            out_copy(0, j).start()
            return carry

        lax.fori_loop(0, pieces, body, 0)

    for index in range(3):
        out_load(index).start()

    def out_add(kind, j, target):
        out_copy(kind, j).wait_recv()
        there = o_far if kind == 0 else o_near
        here = target[part_of(j)].astype(F32)
        target[part_of(j)] = (here + there[part_of(j)].astype(F32)).astype(BF)

    def out_turn(j):
        @pl.when(middle & (j < pieces))
        def _():
            out_add(0, j, mine.at[0])
            out_copy(1, j).start()

        @pl.when(middle & (j > 0) & (j <= pieces))
        def _():
            out_add(1, j - 1, mine.at[1])
            out_copy(2, j - 1).start()

        @pl.when((r == 0) & (j > 1) & (j <= pieces + 1))
        def _():
            out_add(2, j - 2, own)

    def out_slot_copy(device):
        slot = lax.rem(device, 2)
        return pltpu.make_async_copy(slot_tile.at[slot], out_slots.at[device], slot_sem.at[slot])

    def out_slot(device, carry):
        @pl.when(device > 1)
        def _():
            out_slot_copy(device - 2).wait()

        row = lax.broadcasted_iota(jnp.int32, (rows, slot_tile.shape[1]), 0)
        mask = ones_where(row == target_rows[device])
        slot_tile[lax.rem(device, 2)] = dot(mask, own[...], ((0,), (0,))).astype(BF)
        out_slot_copy(device).start()
        return carry

    bits = devices.bit_length() - 1
    bit = lambda i: lax.rem(lax.div(me, 1 << i), 2)
    partner = lambda i: {"expert": me + (1 << i) * (1 - 2 * bit(i))}
    half = tall // 2
    part = half // 2
    orders = [list(range(1, bits)), list(range(bits - 1, 0, -1))]
    levels = bits - 1
    last = part >> levels
    slice_len = last // planes

    def segment(a, level):
        start = bit(0) * half + a * part
        for i in range(level):
            start = start + bit(orders[a][i]) * (part >> (i + 1))
        return start

    def span(start, length):
        return pl.ds(pl.multiple_of(start, 16), length)

    slot_of = {}

    def sems(name, c):
        index = slot_of.setdefault(name, len(slot_of))
        return ar_send.at[index, c], ar_recv.at[index, c]

    def core_copy(c):
        source = grads.at[c, span((1 - bit(0)) * half, half)]
        return [remote(source, core_buf.at[c], *sems("core", c), partner(0))]

    def core_end(c):
        keep = span(bit(0) * half, half)
        grads[c, keep] = (grads[c, keep].astype(F32) + core_buf[c].astype(F32)).astype(BF)

    def halve_copy(level, c):
        copies = []
        length = part >> (level + 1)
        for a in range(2):
            i = orders[a][level]
            source = grads.at[c, span(segment(a, level) + (1 - bit(i)) * length, length)]
            buffer = half_buf.at[c, a, pl.ds(part - (part >> level), length)]
            copies.append(remote(source, buffer, *sems(("half", level, a), c), partner(i)))
        return copies

    def halve_end(level, c):
        length = part >> (level + 1)
        for a in range(2):
            keep = span(segment(a, level + 1), length)
            other_half = half_buf[c, a, pl.ds(part - (part >> level), length)]
            grads[c, keep] = (grads[c, keep].astype(F32) + other_half.astype(F32)).astype(BF)

    def plane_span(a, p):
        return span(segment(a, levels) + p * slice_len, slice_len)

    def plane_copy(c):
        copies = []
        for a in range(2):
            for off in range(1, planes):
                source = grads.at[c, plane_span(a, lax.rem(plane + off, planes))]
                buffer = plane_buf.at[c, a, off - 1]
                copies.append(remote(source, buffer, *sems(("plane", a, off), c), across(off)))
        return copies

    def plane_end(c):
        for a in range(2):
            keep = plane_span(a, plane)
            total = grads[c, keep].astype(F32)
            for off in range(planes - 1):
                total = total + plane_buf[c, a, off].astype(F32)
            grads[c, keep] = total.astype(BF)
        copies = [
            pltpu.make_async_copy(
                grads.at[c, plane_span(a, plane)],
                summed_grads.at[c, plane_span(a, plane)],
                local_sem.at[a],
            )
            for a in range(2)
        ]
        for copy in copies:
            copy.start()
        for copy in copies:
            copy.wait()

    def spread_copy(c):
        copies = []
        for a in range(2):
            for off in range(1, planes):
                keep = plane_span(a, plane)
                source, there = grads.at[c, keep], summed_grads.at[c, keep]
                copies.append(remote(source, there, *sems(("spread", a, off), c), across(off)))
        return copies

    def double_copy(level, c):
        copies = []
        for a in range(2):
            have = summed_grads.at[c, span(segment(a, level + 1), part >> (level + 1))]
            names = sems(("double", level, a), c)
            copies.append(remote(have, have, *names, partner(orders[a][level])))
        return copies

    def core_back_copy(c):
        have = summed_grads.at[c, span(bit(0) * half, half)]
        return [remote(have, have, *sems("core_back", c), partner(0))]

    nothing = lambda c: None
    stages = [(core_copy, core_end)]
    for level in range(levels):
        stages.append((functools.partial(halve_copy, level), functools.partial(halve_end, level)))
    stages.append((plane_copy, plane_end))
    stages.append((spread_copy, nothing))
    for level in reversed(range(levels)):
        stages.append((functools.partial(double_copy, level), nothing))
    stages.append((core_back_copy, nothing))

    def finish(stage, c):
        copies, end = stages[stage]
        for copy in copies(c):
            copy.wait_recv()
        for copy in copies(c):
            copy.wait_send()
        end(c)

    def near_copy(off):
        return remote(
            small, small_near.at[off - 1], near_send.at[off - 1], near_recv.at[off - 1], other(off)
        )

    def far_copy(off):
        return remote(
            small_plane, small_far.at[off - 1], far_send.at[off - 1], far_recv.at[off - 1], across(off)
        )

    def each_near(act):
        def body(off, carry):
            act(near_copy(off))
            return carry

        lax.fori_loop(1, devices, body, 0)

    scale = jnp.asarray(HEAD_DIM**-0.5, BF)
    lanes = 2 * HEAD_DIM
    xhat2, root2 = normalise(residual[...])
    d_values, sums = layer_norm_back(d_second[...].astype(F32), xhat2, root2, gain2[...])
    d_residual = cot[...].astype(F32) + d_values
    grad_tokens[...] = d_residual
    d_branch[...] = d_residual.astype(BF)
    small[...] = jnp.zeros(small.shape, F32)
    small[2:3, :], small[3:4, :] = sums
    normed[...] = (normalise(tokens[...].astype(F32))[0] * gain1[...] + bias1[...]).astype(BF)
    d_normed[...] = jnp.zeros(d_normed.shape, F32)

    def quarter(j):
        slot = lax.rem(j, 2)
        for copy in weights(j, slot):
            copy.wait()

        @pl.when(j < quads - 1)
        def _():
            for copy in weights(j + 1, 1 - slot):
                copy.start()

        out = dot(att[j], d_branch[...], ((0,), (0,))).astype(BF)
        for m in range(width // quad):
            grads[j, 3 * width + m * quad : 3 * width + (m + 1) * quad] = out[:, m * quad : (m + 1) * quad]
        d_att = dot(d_branch[...], w_out[slot], ((1,), (1,))).astype(BF)
        d_thirds = attention_back(j, q, k, v, d_att, lse, scale, lanes)
        total = 0.0
        for third, d_third in enumerate(d_thirds):
            grads[j, third * width : (third + 1) * width] = dot(
                normed[...], d_third, ((0,), (0,))
            ).astype(BF)
            total = total + dot(d_third, w_in[slot, third], ((1,), (1,)))
        d_normed[...] += total

        @pl.when(j == quads - 1)
        def _():
            xhat, root = normalise(tokens[...].astype(F32))
            d_first, first_sums = layer_norm_back(d_normed[...], xhat, root, gain1[...])
            grad_tokens[...] += d_first
            small[0:1, :], small[1:2, :] = first_sums

    count = len(stages)

    def tick(t, carry):
        @pl.when(t < quads)
        def _():
            quarter(t)
            for copy in stages[0][0](t):
                copy.start()

        for stage in range(count, 0, -1):
            c = t - stage

            @pl.when((c >= 0) & (c < quads))
            def _(stage=stage, c=c):
                finish(stage - 1, c)
                if stage < count:
                    for copy in stages[stage][0](c):
                        copy.start()

        @pl.when(t == 1)
        def _():
            for index in range(3):
                out_load(index).wait()

        @pl.when((t >= 1) & (t <= 2 + pieces))
        def _():
            out_turn(t - 1)

        @pl.when(t == quads + pieces)
        def _():
            lax.fori_loop(0, devices, out_slot, 0)
            for device in (devices - 2, devices - 1):
                out_slot_copy(device).wait()

        @pl.when(t == quads - 1)
        def _():
            each_near(lambda copy: copy.start())

        @pl.when(t == quads + 1)
        def _():
            each_near(lambda copy: copy.wait_recv())
            each_near(lambda copy: copy.wait_send())
            total = small[...]
            for off in range(devices - 1):
                total = total + small_near[off]
            small_plane[...] = total
            for off in range(1, planes):
                far_copy(off).start()

        @pl.when(t == quads + 3)
        def _():
            for off in range(1, planes):
                far_copy(off).wait_recv()
            for off in range(1, planes):
                far_copy(off).wait_send()
            total = small_plane[...]
            for off in range(planes - 1):
                total = total + small_far[off]
            small_out[...] = total

        return carry

    lax.fori_loop(0, max(quads + count, quads + pieces + 1), tick, 0)

    def outs_sent(j, carry):
        @pl.when(r == 0)
        def _():
            out_copy(0, j).wait_send()

        @pl.when(middle)
        def _():
            out_copy(1, j).wait_send()
            out_copy(2, j).wait_send()

        return carry

    lax.fori_loop(0, pieces, outs_sent, 0)


def attention_back(j, q, k, v, d_att, lse, scale, lanes):
    rows, quad = d_att.shape
    keep = tri(BLOCK)
    blocks = rows // BLOCK
    cut = lambda array, block: array[block * BLOCK : (block + 1) * BLOCK]
    d_q, d_k, d_v = [], [], []
    lane = lax.broadcasted_iota(jnp.int32, (BLOCK, lse.shape[1]), 1)
    for pair in range(quad // lanes):
        cols = slice(pair * lanes, (pair + 1) * lanes)
        query = q[j, :, cols] * scale
        key, value, d_pair = k[j, :, cols], v[j, :, cols], d_att[:, cols]
        keys, values = halves(key), halves(value)
        pair_q, pair_k, pair_v = [], [], []
        for head in range(2):
            index = j * (quad // HEAD_DIM) + 2 * pair + head
            q_parts = []
            k_parts, v_parts = [0.0] * blocks, [0.0] * blocks
            for q_block in range(blocks):
                level = jnp.sum(
                    jnp.where(lane == index, lse[q_block * BLOCK : (q_block + 1) * BLOCK, :], 0.0),
                    -1,
                    keepdims=True,
                )
                shares, d_shares, inner = [], [], 0.0
                for k_block in range(q_block + 1):
                    scores = dot(cut(query, q_block), cut(keys[head], k_block), ((1,), (1,)))
                    share = jnp.exp(scores - level)
                    if k_block == q_block:
                        share = jnp.where(keep, share, 0.0)
                    d_share = dot(cut(d_pair, q_block), cut(values[head], k_block), ((1,), (1,)))
                    inner = inner + jnp.sum(share * d_share, -1, keepdims=True)
                    shares.append(share)
                    d_shares.append(d_share)
                total = 0.0
                for k_block in range(q_block + 1):
                    d_scores = (shares[k_block] * (d_shares[k_block] - inner)).astype(BF)
                    total = total + dot(d_scores, cut(key, k_block))
                    k_parts[k_block] += dot(d_scores, cut(query, q_block), ((0,), (0,)))
                    v_parts[k_block] += dot(
                        shares[k_block].astype(BF), cut(d_pair, q_block), ((0,), (0,))
                    )
                q_parts.append(total * HEAD_DIM**-0.5)
            pair_q.append(jnp.concatenate(q_parts, 0))
            pair_k.append(jnp.concatenate(k_parts, 0))
            pair_v.append(jnp.concatenate(v_parts, 0))
        d_q.append(join(*pair_q).astype(BF))
        d_k.append(join(*pair_k).astype(BF))
        d_v.append(join(*pair_v).astype(BF))
    return [jnp.concatenate(parts, 1) for parts in (d_q, d_k, d_v)]


def tail(
    number, devices, planes, pieces, target, own, partial, tokens, residual, d_second, cot, q, k, v, att, lse, project_in, project_out,
    gain1, bias1, gain2,
):
    tokens_dev, width = tokens.shape
    quads, _, quad = q.shape
    tall = 4 * width
    bits = devices.bit_length() - 1
    part = tall // 4
    slice_len = (part >> (bits - 1)) // planes
    slots = 2 + 4 * (bits - 1) + 4 * (planes - 1)
    chunk = target.shape[2]
    rows = own.shape[0]
    here, there = pl.BlockSpec(memory_space=pltpu.VMEM), pl.BlockSpec(memory_space=pl.ANY)
    dma = pltpu.SemaphoreType.DMA
    low = lambda *shape: pltpu.VMEM(shape, BF)
    full = lambda *shape: pltpu.VMEM(shape, F32)
    return pl.pallas_call(
        functools.partial(tail_kernel, pieces),
        in_specs=[here] * 9 + [there] * 2 + [here] * 4 + [there] * 2,
        out_specs=[here, there, here, there],
        out_shape=[
            jax.ShapeDtypeStruct((tokens_dev, width), F32),
            jax.ShapeDtypeStruct((quads, tall, quad), BF),
            jax.ShapeDtypeStruct((8, width), F32),
            jax.ShapeDtypeStruct((devices, chunk, width), BF),
        ],
        scratch_shapes=[
            low(2, 3, width, quad),
            low(2, quad, width),
            low(tokens_dev, width),
            low(tokens_dev, width),
            full(tokens_dev, width),
            low(quads, tall, quad),
            full(8, width),
            full(8, width),
            full(devices - 1, 8, width),
            full(planes - 1, 8, width),
            low(quads, tall // 2, quad),
            low(quads, 2, part - (part >> (bits - 1)), quad),
            low(quads, 2, planes - 1, slice_len, quad),
            low(rows, width),
            low(rows, width),
            low(rows, width),
            low(2, rows, width),
            low(2, chunk, width),
            dma((3, pieces)),
            dma((3, pieces)),
            dma((3,)),
            dma((2,)),
            dma((slots, quads)),
            dma((slots, quads)),
            dma((devices - 1,)),
            dma((devices - 1,)),
            dma((planes - 1,)),
            dma((planes - 1,)),
            dma((2, 4)),
            dma((2,)),
        ],
        compiler_params=pltpu.CompilerParams(
            collective_id=number, has_side_effects=True, vmem_limit_bytes=62 * 2**20
        ),
        cost_estimate=pl.CostEstimate(
            flops=20 * tokens_dev * width * width,
            bytes_accessed=64 * 2**20,
            transcendentals=HEADS * tokens_dev * tokens_dev,
        ),
        name="tail",
    )(
        tokens, residual, d_second, cot, q, k, v, att, lse, project_in, project_out,
        *(x.reshape(1, width) for x in (gain1, bias1, gain2)), target, own, partial,
    )


def spread_kernel(summed, grad_in, grad_out):
    third = pl.program_id(1)

    @pl.when(third < 3)
    def _():
        grad_in[...] = summed[0].astype(F32)

    @pl.when(third == 3)
    def _():
        quad = summed.shape[2]
        for m in range(grad_out.shape[1] // quad):
            rows = slice(m * quad, (m + 1) * quad)
            grad_out[:, rows] = summed[0, rows].astype(F32)


def spread(summed):
    quads, tall, quad = summed.shape
    width = tall // 4
    return pl.pallas_call(
        spread_kernel,
        grid=(quads, 4),
        in_specs=[pl.BlockSpec((1, width, quad), lambda j, t: (j, t, 0))],
        out_specs=[
            pl.BlockSpec((width, quad), lambda j, t: (0, jnp.minimum(t, 2) * quads + j)),
            pl.BlockSpec((quad, width), lambda j, t: (j, 0)),
        ],
        out_shape=[
            jax.ShapeDtypeStruct((width, 3 * width), F32),
            jax.ShapeDtypeStruct((width, width), F32),
        ],
        compiler_params=pltpu.CompilerParams(vmem_limit_bytes=60 * 2**20),
        name="spread",
    )(summed)


def on_device(
    tokens,
    token_ids,
    hash_table,
    first_gain,
    first_bias,
    project_in,
    project_out,
    second_gain,
    second_bias,
    expert_in,
    expert_out,
    cotangent,
):
    rows_dev, width = tokens.shape
    expert_devs = lax.axis_size("expert")
    hidden_devs = lax.axis_size("hidden")
    local = expert_in.shape[0]
    experts = local * expert_devs
    capacity = 8 * ((3 * rows_dev + 8 * experts - 1) // (8 * experts))
    chunk = local * capacity

    owner = hash_table.at[token_ids].get(mode="promise_in_bounds")
    expert_ids = jnp.arange(experts, dtype=jnp.int32)
    onehot = owner[:, None] == expert_ids[None, :]
    earlier = lax.broadcasted_iota(jnp.int32, (rows_dev, rows_dev), 1) < lax.broadcasted_iota(
        jnp.int32, (rows_dev, rows_dev), 0
    )
    before_count = jnp.dot(earlier.astype(BF), onehot.astype(BF), preferred_element_type=F32)
    counts = jnp.sum(onehot.astype(jnp.int32), 0)
    grouped = counts.reshape(expert_devs, local)
    first_slot = (
        jnp.cumsum(grouped, 1) - grouped + jnp.arange(expert_devs, dtype=jnp.int32)[:, None] * chunk
    ).reshape(experts)
    place = jnp.sum(
        jnp.where(onehot, before_count.astype(jnp.int32) + first_slot[None, :], 0), 1
    )
    residual, second, query, keys, values, attended, lse, cot_col, all_counts, places = attend(
        expert_devs, hidden_devs, tokens, project_in, project_out,
        first_gain, first_bias, second_gain, second_bias, place, cotangent, counts,
    )
    all_counts = all_counts[:, :, 0, :experts].reshape(
        hidden_devs, expert_devs, expert_devs, local
    )
    group = lax.axis_index("expert")
    plane = lax.axis_index("hidden")
    group_counts = lax.dynamic_index_in_dim(all_counts, group, 2, keepdims=False)
    most = jnp.max(jnp.sum(all_counts, (1, 3)))

    starts = jnp.cumsum(group_counts, 2) - group_counts
    totals = jnp.sum(group_counts, 1)
    firsts = jnp.cumsum(totals, 1) - totals
    bases = jnp.cumsum(group_counts, 1) - group_counts + firsts[:, None, :]
    slot = jnp.arange(chunk, dtype=jnp.int32)[None, None, :]
    targets = jnp.full((hidden_devs, expert_devs, chunk), -1, jnp.int32)
    for l in range(local):
        offset = slot - starts[:, :, l : l + 1]
        inside = (offset >= 0) & (offset < group_counts[:, :, l : l + 1])
        targets = jnp.where(inside, bases[:, :, l : l + 1] + offset, targets)
    target_rows = lax.dynamic_index_in_dim(targets, plane, 0, keepdims=False)
    target = target_rows.reshape(-1)

    most_rows = expert_devs * chunk
    ends = jnp.cumsum(totals, 1)
    bounds = jnp.broadcast_to(ends[:, :, None], (hidden_devs, local, 128))
    row = jnp.arange(most_rows, dtype=jnp.int32)[None, :]
    eid = sum((row >= ends[:, l : l + 1]).astype(jnp.int32) for l in range(local))
    has = jnp.stack(
        [jnp.any((eid == l).reshape(-1, TILE), 1).astype(jnp.int32) for l in range(local)], 1
    )
    eid = eid.astype(F32)

    def run(rows, pieces, group, number):
        x_all, cot_all, act, dbef, part, _, _, _, own, _, _, d_second = expert_pass(
            rows, pieces, group, number, room, second, places,
            targets.reshape(hidden_devs, 1, expert_devs * chunk),
            target_rows.reshape(expert_devs, 1, chunk), cot_col,
            bounds, expert_in, expert_out,
        )
        return x_all, cot_all, act, dbef, part, own, d_second, jnp.zeros_like(d_second)

    def run_any():
        send = (place[None, :] == jnp.arange(most_rows, dtype=jnp.int32)[:, None]).astype(BF)
        pack = (target[None, :] == jnp.arange(most_rows, dtype=jnp.int32)[:, None]).astype(BF)

        def gather(values):
            slots = dot(send, values).astype(BF).reshape(expert_devs, chunk, width)
            arrived = lax.all_to_all(slots, "expert", 0, 0, tiled=True)
            packed = dot(pack, arrived.reshape(-1, width)).astype(BF)
            return lax.all_gather(packed, "hidden", axis=0, tiled=True)

        def add_up(partial):
            summed = lax.psum_scatter(partial, "hidden", scatter_dimension=0, tiled=True)
            return dot(pack, summed, ((0,), (0,))).astype(BF).reshape(expert_devs, chunk, width)

        x_rows, cot_rows = gather(second), gather(cotangent)
        act, dbef, part, dmem = expert_rows(
            x_rows, cot_rows, eid.reshape(-1, 1), has, expert_in, expert_out
        )
        returned = lax.all_to_all(add_up(dmem), "expert", 0, 0, tiled=True)
        d_second = dot(send, returned.reshape(-1, width), ((0,), (0,))).astype(BF)
        wide = (hidden_devs, most_rows, width)
        x_rows, cot_rows, act, dbef = (v.reshape(wide) for v in (x_rows, cot_rows, act, dbef))
        returned = lax.all_to_all(add_up(part), "expert", 0, 0, tiled=True)
        produced = dot(send, returned.reshape(-1, width), ((0,), (0,))).astype(BF)
        none = jnp.zeros((hidden_devs, room, width), BF)
        return x_rows, cot_rows, act, dbef, none, none[0], d_second, produced

    plans = [(768, 4, 2, 1), (832, 4, 2, 2), (896, 4, 2, 3)]
    plans = [plan for plan in plans if plan[0] < most_rows and hidden_devs == 4]
    room = max(plan[0] for plan in plans)
    pick = sum((most <= plan[0]).astype(jnp.int32) for plan in plans)
    branches = [run_any] + [functools.partial(run, *plan) for plan in reversed(plans)]
    x_all, cot_all, act, dbef, part, own, d_second, more = lax.switch(pick, branches)

    grad_tokens, summed, small, slots = tail(
        4, expert_devs, hidden_devs, 4, target_rows.reshape(expert_devs, 1, chunk), own, part,
        tokens, residual, d_second, cotangent, query, keys, values,
        attended, lse, project_in, project_out, first_gain, first_bias, second_gain,
    )
    slots, act = lax.optimization_barrier((slots, act))
    returned = lax.all_to_all(slots, "expert", 0, 0, tiled=True)
    slot_of = jnp.arange(most_rows, dtype=jnp.int32)[:, None]
    send = (place[None, :] == slot_of).astype(BF)
    produced = dot(send, returned.reshape(-1, width), ((0,), (0,)))
    block_out = (residual + (produced + more.astype(F32))).astype(BF)
    grad_in, grad_out = spread(summed)
    flat = lambda v: v.reshape(-1, width)
    grad_expert_in, grad_expert_out = expert_grads(
        flat(x_all), flat(cot_all), eid.reshape(-1, 1), has, flat(act), flat(dbef)
    )
    return (
        block_out,
        grad_tokens,
        small[0],
        small[1],
        grad_in,
        grad_out,
        small[2],
        small[3],
        grad_expert_in,
        grad_expert_out,
    )


def solution(mesh):
    rows = P(("expert", "hidden"), None)
    w_in, w_out = P("expert", None, "hidden"), P("expert", "hidden", None)
    return jax.shard_map(
        on_device,
        mesh=mesh,
        in_specs=(
            rows,
            P(("expert", "hidden")),
            P(),
            P(),
            P(),
            P(),
            P(),
            P(),
            P(),
            w_in,
            w_out,
            rows,
        ),
        out_specs=(rows, rows, P(), P(), P(), P(), P(), P(), w_in, w_out),
        check_vma=False,
    )
```

```python
import functools

import jax
import jax.numpy as jnp
from jax import lax
from jax.experimental import pallas as pl
from jax.experimental.pallas import tpu as pltpu
from jax.sharding import PartitionSpec as P

HEADS = 16
HEAD_DIM = 64
TILE = 256
SPAN = 512
BLOCK = 256
QUAD = 256
EPS = 1e-05
BF = jnp.bfloat16
F32 = jnp.float32


def dot(a, b, dims=((1,), (0,))):
    return lax.dot_general(a, b, (dims, ((), ())), preferred_element_type=F32)


def expert_kernel(local_experts, has, x, cot, eid, w_in, w_out, act_o, dbef_o, part_o, dmem_o):
    tile = pl.program_id(0)
    outs = (act_o, dbef_o, part_o, dmem_o)

    @pl.when(has[tile, 0] == 0)
    def _():
        for out in outs:
            out[...] = jnp.zeros(out.shape, out.dtype)

    for expert in range(local_experts):

        @pl.when(has[tile, expert] > 0)
        def _(expert=expert):
            mine = eid[...] == float(expert)
            before = dot(x[...], w_in[expert])
            d_after = dot(cot[...], w_out[expert], ((1,), (1,)))
            square = before * before
            inner = 0.7978845608028654 * before * (1.0 + 0.044715 * square)
            tanh = jnp.tanh(inner)
            half = 0.5 * (1.0 + tanh)
            act = (before * half).astype(BF)
            slope = half + 0.5 * before * (1.0 - tanh * tanh) * (
                0.7978845608028654 * (1.0 + 0.134145 * square)
            )
            dbef = (d_after * slope).astype(BF)
            part = dot(act, w_out[expert])
            dmem = dot(dbef, w_in[expert], ((1,), (1,)))
            news = (act.astype(F32), dbef.astype(F32), part, dmem)
            for out, new in zip(outs, news):
                old = 0.0 if expert == 0 else out[...].astype(F32)
                out[...] = jnp.where(mine, new, old).astype(BF)


def expert_rows(x, cot, eid, has, w_in, w_out):
    rows, width = x.shape
    experts, _, hidden = w_in.shape
    tiles = rows // TILE
    row_block = pl.BlockSpec((TILE, width), lambda t, has: (t, 0))
    hid_block = pl.BlockSpec((TILE, hidden), lambda t, has: (t, 0))
    whole = lambda shape: pl.BlockSpec(shape, lambda t, has: (0, 0, 0), pipeline_mode=pl.Buffered(1))
    return pl.pallas_call(
        functools.partial(expert_kernel, experts),
        grid_spec=pltpu.PrefetchScalarGridSpec(
            num_scalar_prefetch=1,
            grid=(tiles,),
            in_specs=[
                row_block,
                row_block,
                pl.BlockSpec((TILE, 1), lambda t, has: (t, 0)),
                whole(w_in.shape),
                whole(w_out.shape),
            ],
            out_specs=[hid_block, hid_block, row_block, row_block],
        ),
        out_shape=[
            jax.ShapeDtypeStruct((rows, hidden), BF),
            jax.ShapeDtypeStruct((rows, hidden), BF),
            jax.ShapeDtypeStruct((rows, width), BF),
            jax.ShapeDtypeStruct((rows, width), BF),
        ],
        compiler_params=pltpu.CompilerParams(vmem_limit_bytes=56 * 2**20),
        cost_estimate=pl.CostEstimate(
            flops=8 * rows * width * hidden,
            bytes_accessed=2 * (w_in.size + w_out.size + 6 * rows * width),
            transcendentals=rows * hidden,
        ),
        name="expert_rows",
    )(has, x, cot, eid, w_in, w_out)


def expert_grad_kernel(owner, tile, low, high, count, x, cot, act, dbef, g_in, g_out):
    visit = pl.program_id(0)
    expert = owner[visit]

    @pl.when((visit == 0) | (owner[jnp.maximum(visit - 1, 0)] != expert))
    def _():
        g_in[...] = jnp.zeros(g_in.shape, F32)
        g_out[...] = jnp.zeros(g_out.shape, F32)

    @pl.when(visit < count[0])
    def _():
        row = lax.broadcasted_iota(jnp.int32, (TILE, 1), 0)
        mine = ones_where((row >= low[visit]) & (row < high[visit]))
        g_in[0] += dot(x[...], dbef[...] * mine, ((0,), (0,)))
        g_out[0] += dot(act[...] * mine, cot[...], ((0,), (0,)))


def expert_grads(x, cot, lows, highs, act, dbef):
    rows, width = x.shape
    hidden = act.shape[1]
    experts, tiles = lows.shape
    some = (highs > lows) | (jnp.arange(tiles, dtype=jnp.int32) == 0)[None, :]
    wanted = some.astype(jnp.int32).reshape(-1)
    order = jnp.cumsum(wanted) - 1
    most = tiles + experts * 4
    count = jnp.sum(wanted).reshape(1)
    visit = jnp.minimum(jnp.arange(most, dtype=jnp.int32), count - 1)
    chosen = (wanted[None, :] > 0) & (order[None, :] == visit[:, None])
    choose = lambda values: jnp.sum(jnp.where(chosen, values.reshape(1, -1), 0), 1)
    index = choose(jnp.arange(tiles * experts, dtype=jnp.int32))
    owner, tile = index // tiles, index % tiles
    row_block = pl.BlockSpec((TILE, width), lambda v, owner, tile, *_: (tile[v], 0))
    hid_block = pl.BlockSpec((TILE, hidden), lambda v, owner, tile, *_: (tile[v], 0))
    return pl.pallas_call(
        expert_grad_kernel,
        grid_spec=pltpu.PrefetchScalarGridSpec(
            num_scalar_prefetch=5,
            grid=(most,),
            in_specs=[row_block, row_block, hid_block, hid_block],
            out_specs=[
                pl.BlockSpec((1, width, hidden), lambda v, owner, *_: (owner[v], 0, 0)),
                pl.BlockSpec((1, hidden, width), lambda v, owner, *_: (owner[v], 0, 0)),
            ],
        ),
        out_shape=[
            jax.ShapeDtypeStruct((experts, width, hidden), F32),
            jax.ShapeDtypeStruct((experts, hidden, width), F32),
        ],
        compiler_params=pltpu.CompilerParams(vmem_limit_bytes=56 * 2**20),
        cost_estimate=pl.CostEstimate(
            flops=2 * rows * width * hidden,
            bytes_accessed=8 * experts * width * hidden + 6 * rows * width,
            transcendentals=0,
        ),
        name="expert_grads",
    )(owner, tile, choose(lows), choose(highs), count, x, cot, act, dbef)


MESH = pl.DeviceIdType.MESH


def remote(src, dst, send_sem, recv_sem, device):
    return pltpu.make_async_remote_copy(
        src_ref=src,
        dst_ref=dst,
        send_sem=send_sem,
        recv_sem=recv_sem,
        device_id=device,
        device_id_type=MESH,
    )


def position(plane):
    side = lax.div(plane, 2)
    return side, plane + side * (3 - 2 * plane)


def ones_where(mask):
    return jnp.where(mask, 1.0, 0.0).astype(BF)


def halves(pair):
    left = lax.broadcasted_iota(jnp.int32, pair.shape, 1) < HEAD_DIM
    zero = jnp.zeros_like(pair)
    return (jnp.where(left, pair, zero), jnp.where(left, zero, pair))


def join(first, second):
    left = lax.broadcasted_iota(jnp.int32, first.shape, 1) < HEAD_DIM
    return jnp.where(left, first, second)


def tri(block):
    later = lax.broadcasted_iota(jnp.int32, (block, block), 1)
    return later <= lax.broadcasted_iota(jnp.int32, (block, block), 0)


def normalise(values):
    centered = values - jnp.mean(values, -1, keepdims=True)
    spread = jnp.mean(centered * centered, -1, keepdims=True)
    root = lax.rsqrt(spread + EPS)
    return centered * root, root


def attend_kernel(
    tokens, w_q, w_k, w_v, w_o, gain1, bias1, gain2, bias2, place, cot, counts,
    residual, second, q_out, k_out, v_out, att_out, lse, cot_col, all_counts, places,
    normed, known, known_places, col_send, col_recv, near_send, near_recv, far_send, far_recv,
    place_send, place_recv, local_sem,
):
    step = pl.program_id(0)
    rows = tokens.shape[0]
    lanes = 2 * HEAD_DIM
    me, plane = lax.axis_index("expert"), lax.axis_index("hidden")
    planes, devices = known.shape[:2]
    side, r = position(plane)
    middle = r == 1
    step_up = 1 - 2 * side
    up, down = {"hidden": plane + step_up}, {"hidden": plane - step_up}
    other = lambda off: {"expert": lax.rem(me + off, devices)}
    across = lambda off: {"hidden": lax.rem(plane + off, planes)}
    sender = lambda off: lax.rem(me - off + devices, devices)

    def col_copy(way, below):
        piece = cot_col.at[plane]
        return remote(cot, piece, col_send.at[way], col_recv.at[below], down if way else up)

    def place_copy(off, source):
        piece = known_places.at[source]
        return remote(piece, piece, place_send.at[off], place_recv.at[off], across(off))

    def near_copy(off, source):
        piece = known.at[plane, source]
        return remote(piece, piece, near_send.at[off], near_recv.at[off], other(off))

    def far_copy(off, source):
        piece = known.at[source]
        return remote(piece, piece, far_send.at[off], far_recv.at[off], across(off))

    def own_copy():
        return pltpu.make_async_copy(cot, cot_col.at[plane], local_sem)

    def each(act, count):
        def body(off, carry):
            act(off)
            return carry

        lax.fori_loop(1, count, body, 0)

    @pl.when(step == 0)
    def _():
        barrier = pltpu.get_barrier_semaphore()

        def greet(device):
            pl.semaphore_signal(barrier, inc=1, device_id=device, device_id_type=MESH)

        each(lambda off: greet(other(off)), devices)
        each(lambda off: greet(across(off)), planes)
        known[plane, me] = counts[...]
        known_places[plane] = jnp.broadcast_to(place[...], known_places.shape[1:])
        pl.semaphore_wait(barrier, devices + planes - 2)
        each(lambda off: near_copy(off, me).start(), devices)
        each(lambda off: place_copy(off, plane).start(), planes)

        @pl.when(r == 0)
        def _():
            col_copy(0, 0).start()

        @pl.when(middle)
        def _():
            col_copy(0, 1).start()
            col_copy(1, 1).start()

        own_copy().start()

    @pl.when(step == 1)
    def _():
        each(lambda off: near_copy(off, sender(off)).wait_recv(), devices)
        each(lambda off: far_copy(off, plane).start(), planes)

    @pl.when(step == 0)
    def _():
        source = tokens[...].astype(F32)
        normed[...] = (normalise(source)[0] * gain1[...] + bias1[...]).astype(BF)
        residual[...] = source
        lse[...] = jnp.zeros(lse.shape, F32)

    q_out[0] = dot(normed[...], w_q[...]).astype(BF)
    k_out[0] = dot(normed[...], w_k[...]).astype(BF)
    v_out[0] = dot(normed[...], w_v[...]).astype(BF)
    width = q_out.shape[2]
    keep = tri(BLOCK)
    lane = lax.broadcasted_iota(jnp.int32, (BLOCK, lse.shape[1]), 1)
    for pair in range(width // lanes):
        cols = slice(pair * lanes, (pair + 1) * lanes)
        query = q_out[0, :, cols] * jnp.asarray(HEAD_DIM**-0.5, BF)
        keys = halves(k_out[0, :, cols])
        values = v_out[0, :, cols]
        for q_block in range(rows // BLOCK):
            q_rows = slice(q_block * BLOCK, (q_block + 1) * BLOCK)
            results = []
            for head in range(2):
                scores = []
                for k_block in range(q_block + 1):
                    k_rows = slice(k_block * BLOCK, (k_block + 1) * BLOCK)
                    part = dot(query[q_rows], keys[head][k_rows], ((1,), (1,)))
                    scores.append(jnp.where(keep, part, -1e30) if k_block == q_block else part)
                top = functools.reduce(jnp.maximum, [jnp.max(s, -1, keepdims=True) for s in scores])
                weights = [jnp.exp(s - top) for s in scores]
                total = sum(jnp.sum(w, -1, keepdims=True) for w in weights)
                share = 1.0 / total
                out = sum(
                    dot((w * share).astype(BF), values[k * BLOCK : (k + 1) * BLOCK])
                    for k, w in enumerate(weights)
                )
                results.append(out)
                index = step * (width // HEAD_DIM) + 2 * pair + head
                lse[q_rows, :] = jnp.where(lane == index, top + jnp.log(total), lse[q_rows, :])
            att_out[0, q_rows, cols] = join(*results).astype(BF)
    residual[...] += dot(att_out[0], w_o[...])

    @pl.when(step == pl.num_programs(0) - 1)
    def _():
        second[...] = (normalise(residual[...])[0] * gain2[...] + bias2[...]).astype(BF)
        each(lambda off: far_copy(off, lax.rem(plane - off + planes, planes)).wait_recv(), planes)
        each(lambda off: place_copy(off, lax.rem(plane - off + planes, planes)).wait_recv(), planes)
        all_counts[...] = known[...]
        places[...] = known_places[...]
        own_copy().wait()
        col_copy(0, 1).wait_recv()
        col_copy(0, 0).wait_send()

        @pl.when(middle)
        def _():
            col_copy(0, 0).wait_recv()
            col_copy(1, 1).wait_send()

        each(lambda off: place_copy(off, plane).wait_send(), planes)
        each(lambda off: near_copy(off, me).wait_send(), devices)
        each(lambda off: far_copy(off, plane).wait_send(), planes)


def attend(
    devices, planes, tokens, project_in, project_out, gain1, bias1, gain2, bias2, place, cot, counts
):
    rows, width = tokens.shape
    dma = pltpu.SemaphoreType.DMA
    counts = jnp.broadcast_to(jnp.pad(counts, (0, 128 - counts.shape[0]))[None, :], (8, 128))
    known = (planes, devices, 8, 128)
    steps = width // QUAD
    whole = lambda shape: pl.BlockSpec(shape, lambda j: (0, 0))
    third = lambda k: pl.BlockSpec((width, QUAD), lambda j: (0, k * steps + j))
    cols = pl.BlockSpec((1, rows, QUAD), lambda j: (j, 0, 0))
    vector = whole((1, width))
    low = jax.ShapeDtypeStruct((rows, width), BF)
    split = jax.ShapeDtypeStruct((steps, rows, QUAD), BF)
    return pl.pallas_call(
        attend_kernel,
        grid=(steps,),
        in_specs=[whole((rows, width)), third(0), third(1), third(2),
            pl.BlockSpec((QUAD, width), lambda j: (j, 0)), vector, vector, vector, vector,
            whole((1, rows)), whole((rows, width)), whole((8, 128))],
        out_specs=[whole((rows, width)), whole((rows, width)), cols, cols, cols, cols, whole((rows, 128)),
            pl.BlockSpec(memory_space=pl.ANY), pl.BlockSpec(known, lambda j: (0, 0, 0, 0)),
            pl.BlockSpec((planes, 8, rows), lambda j: (0, 0, 0))],
        out_shape=[jax.ShapeDtypeStruct((rows, width), F32), low, split, split, split, split,
            jax.ShapeDtypeStruct((rows, 128), F32), jax.ShapeDtypeStruct((planes, rows, width), BF),
            jax.ShapeDtypeStruct(known, jnp.int32), jax.ShapeDtypeStruct((planes, 8, rows), jnp.int32)],
        scratch_shapes=[pltpu.VMEM((rows, width), BF), pltpu.VMEM(known, jnp.int32),
            pltpu.VMEM((planes, 8, rows), jnp.int32), dma((2,)), dma((2,)), dma((devices,)), dma((devices,)),
            dma((planes,)), dma((planes,)), dma((planes,)), dma((planes,)), dma],
        compiler_params=pltpu.CompilerParams(
            collective_id=0, has_side_effects=True, vmem_limit_bytes=56 * 2**20
        ),
        cost_estimate=pl.CostEstimate(flops=10 * rows * width * width, bytes_accessed=20 * 2**20,
            transcendentals=HEADS * rows * rows),
        name="attend",
    )(tokens, project_in, project_in, project_in, project_out, *(v.reshape(1, width) for v in (gain1, bias1, gain2, bias2)),
        place.reshape(1, rows), cot, counts)


def layer_norm_back(d_normed, xhat, root, gain):
    scaled = d_normed * gain
    d_values = root * (
        scaled
        - jnp.mean(scaled, -1, keepdims=True)
        - xhat * jnp.mean(scaled * xhat, -1, keepdims=True)
    )
    sums = (jnp.sum(d_normed * xhat, 0, keepdims=True), jnp.sum(d_normed, 0, keepdims=True))
    return d_values, sums


def pass_kernel(
    rows, pieces, group,
    x, places, targets, target_rows, cot_col, ends, w_in, w_out,
    x_all, cot_all, act_o, dbef_o, part_o, slope_o, o_down, o_up, own_out, cot_far, cot_slots, d_second,
    slots, arrived, packed_x, packed_c, dense, returned, d_part, from_down, from_up, x_tile, c_tile, stage,
    plane_send, plane_recv, cot_send, cot_recv, far_send, far_recv, back_send, back_recv, ag_send, ag_recv,
    rs_send, rs_down, rs_up, os_send, os_down, os_up, local_sem, stage_sem, own_sem, dense_sem,
):
    me, plane = lax.axis_index("expert"), lax.axis_index("hidden")
    _, devices, chunk, width = slots.shape
    experts = w_in.shape[0]
    height = rows // pieces
    tile_height = group * height
    tiles = pieces // group
    side, r = position(plane)
    middle, end = r == 1, r == 0
    step = 1 - 2 * side
    up, down = {"hidden": plane + step}, {"hidden": plane - step}
    physical = lambda rel: rel + side * (3 - 2 * rel)
    part_of = lambda j: pl.ds(pl.multiple_of(j * height, 16), height)
    tile_of = lambda i: pl.ds(pl.multiple_of(i * tile_height, 16), tile_height)
    peer_of = lambda off: lax.rem(me + off, devices)
    source_of = lambda off: lax.rem(me - off + devices, devices)

    def each(act, first, last):
        def body(i, carry):
            act(i)
            return carry

        lax.fori_loop(first, last, body, 0)

    def forward_rel(p):
        return jnp.where(end | (p > 2), p, jnp.where(p == 0, 1, jnp.where(p == 1, 2, 0)))

    def cot_rel(n):
        at_middle = jnp.where(n == 0, 2, jnp.where(n == 1, 0, jnp.where(n == 2, 3, 1)))
        return jnp.where(end, lax.rem(n + 1, 4), at_middle)

    barrier = pltpu.get_barrier_semaphore()
    greet = lambda device: pl.semaphore_signal(barrier, inc=1, device_id=device, device_id_type=MESH)
    each(lambda off: greet({"expert": peer_of(off)}), 1, devices)
    greet(up)

    @pl.when(middle)
    def _():
        greet(down)

    pl.semaphore_wait(barrier, devices + r)

    def far_copy(index):
        block = physical((0, 2, 3)[index])
        source = (cot_far if index == 2 else cot_col).at[block]
        device = down if index else up
        return remote(source, cot_far.at[block], far_send.at[index], far_recv.at[index], device)

    @pl.when(middle)
    def _():
        far_copy(0).start()
        far_copy(1).start()

    def slots_of(device, block, values):
        row = lax.broadcasted_iota(jnp.int32, (chunk, x.shape[0]), 0) + device * chunk
        return dot(ones_where(row == places[block, 0:1, :]), values[...]).astype(BF)

    def dispatch_copy(off, to, frm):
        return remote(
            slots.at[0, to], arrived.at[frm], plane_send.at[off], plane_recv.at[off], {"expert": to}
        )

    def dispatch(off):
        peer = peer_of(off)
        slots[0, peer] = slots_of(peer, plane, x)
        dispatch_copy(off, peer, me).start()

    each(dispatch, 1, devices)
    arrived[me] = slots_of(me, plane, x)

    def cot_copy(n, off, to, frm):
        slot = lax.rem(n + 1, 2)
        return remote(
            slots.at[slot, to], cot_slots.at[n, frm], cot_send.at[n, off], cot_recv.at[n, off], {"expert": to}
        )

    def cot_own(n):
        return pltpu.make_async_copy(slots.at[lax.rem(n + 1, 2), me], cot_slots.at[n, me], own_sem.at[n])

    def cot_sent(n):
        each(lambda off: cot_copy(n, off, peer_of(off), me).wait_send(), 1, devices)

    def send_cot(n, far):
        block = physical(cot_rel(n))

        def fetch(source):
            one = pltpu.make_async_copy(source.at[block], dense, dense_sem)
            one.start()
            one.wait()

        @pl.when(far)
        def _():
            fetch(cot_far)

        @pl.when(jnp.logical_not(far))
        def _():
            fetch(cot_col)

        def fill(off):
            peer = peer_of(off)
            slots[lax.rem(n + 1, 2), peer] = slots_of(peer, block, dense)
            cot_copy(n, off, peer, me).start()

        each(fill, 1, devices)
        slots[lax.rem(n + 1, 2), me] = slots_of(me, block, dense)
        cot_own(n).start()

    send_cot(jnp.int32(0), jnp.bool_(False))

    def pack(block, j):
        row = lax.broadcasted_iota(jnp.int32, (height, devices * chunk), 0) + j * height
        flat = arrived[...].reshape(devices * chunk, width)
        return dot(ones_where(row == targets[block]), flat).astype(BF)

    def gather_copy(way, block, j, own):
        source = packed_x.at[part_of(j)] if own else x_all.at[block, part_of(j)]
        return remote(
            source, x_all.at[block, part_of(j)], ag_send.at[way, block, j], ag_recv.at[block, j], down if way else up
        )

    @pl.when(middle)
    def _():
        far_copy(0).wait_recv()
        far_copy(2).start()

    each(lambda off: dispatch_copy(off, me, source_of(off)).wait_recv(), 1, devices)

    def send_own(j):
        packed_x[part_of(j)] = pack(plane, j)
        gather_copy(0, plane, j, True).start()

        @pl.when(middle)
        def _():
            gather_copy(1, plane, j, True).start()

    each(send_own, 0, pieces)
    keep_own = pltpu.make_async_copy(packed_x, x_all.at[plane, pl.ds(0, rows)], local_sem.at[0])
    keep_own.start()

    keep_own.wait()

    def got(rel, j):
        gather_copy(0, physical(rel), j, False).wait_recv()

    def relay(rel, way, j):
        got(rel, j)
        gather_copy(way, physical(rel), j, False).start()

    def keep_cot(n):
        there = cot_all.at[physical(cot_rel(n)), pl.ds(0, rows)]
        return pltpu.make_async_copy(packed_c, there, local_sem.at[1])

    def collect_cot(n):
        block = physical(cot_rel(n))

        @pl.when(n > 1)
        def _():
            cot_own(n).wait()

        each(lambda off: cot_copy(n, off, me, source_of(off)).wait_recv(), 1, devices)
        fetch = pltpu.make_async_copy(cot_slots.at[n], arrived, dense_sem)
        fetch.start()

        @pl.when(n > 0)
        def _():
            keep_cot(n).wait()

        fetch.wait()

        def one(j):
            packed_c[part_of(j)] = pack(block, j)

        each(one, 0, pieces)
        keep_cot(n).start()

    def sum_copy(rel, j, buffer, index, sems, device):
        return remote(
            d_part.at[physical(rel), part_of(j)],
            buffer.at[index, part_of(j)],
            rs_send.at[rel, j],
            sems.at[index, j],
            device,
        )

    def add(rel, j, buffer, index, sems):
        sum_copy(rel, j, buffer, index, sems, up).wait_recv()
        block = physical(rel)
        here = d_part[block, part_of(j)].astype(F32)
        d_part[block, part_of(j)] = (here + buffer[index, part_of(j)].astype(F32)).astype(BF)

    def out_copy(rel, j, source, buffer, index, sems, device):
        return remote(
            source, buffer.at[index, part_of(j)], os_send.at[rel, j], sems.at[index, j], device
        )

    def out_send(rel, j):
        source = part_o.at[physical(rel), part_of(j)]
        out_copy(rel, j, source, o_down, rel - 1, os_down, up).start()

    def out_sum(rel, j, buffers):
        pads = [t.at[pl.ds(0, height)] for t in (x_tile, c_tile, stage.at[0])]
        loads = [pltpu.make_async_copy(part_o.at[physical(rel), part_of(j)], pads[0], stage_sem.at[0])]
        loads[0].start()
        for n, (buffer, index, sems) in enumerate(buffers):
            piece = buffer.at[index, part_of(j)]
            out_copy(rel, j, piece, buffer, index, sems, up).wait_recv()
            loads.append(pltpu.make_async_copy(piece, pads[n + 1], stage_sem.at[n + 1]))
            loads[-1].start()
        for load in loads:
            load.wait()
        return sum(t[...].astype(F32) for t in pads[: len(loads)]).astype(BF)

    def out_relay(j):
        held = from_down.at[1, part_of(j)]
        held[...] = out_sum(2, j, [(o_down, 1, os_down)])
        out_copy(2, j, held, o_up, 1, os_up, up).start()

    outs = (act_o, dbef_o, part_o, slope_o)

    def stage_copy(index, block, i):
        return pltpu.make_async_copy(
            stage.at[index], outs[index].at[block, tile_of(i)], stage_sem.at[index]
        )

    def load(array, block, i):
        one = pltpu.make_async_copy(array.at[block, tile_of(i)], x_tile, local_sem.at[0])
        one.start()
        one.wait()

    def chooser(block, i):
        row = lax.broadcasted_iota(jnp.int32, (tile_height, 1), 0) + i * tile_height
        before = [row < ends[block, e : e + 1, 0:1] for e in range(experts)]
        mine = [before[e] & jnp.logical_not(before[e - 1]) if e else before[0] for e in range(experts)]

        def choose(results):
            total = jnp.where(mine[0], results[0], 0.0)
            for mask, result in zip(mine[1:], results[1:]):
                total = jnp.where(mask, result, total)
            return total

        return choose

    def columns(body):
        def one(n, carry):
            body(pl.ds(pl.multiple_of(n * SPAN, SPAN), SPAN))
            return carry

        lax.fori_loop(0, width // SPAN, one, 0)

    def staged(block, i):
        for index in (0, 2, 3):
            stage_copy(index, block, i).wait()

    def forward_tile(block, i):
        load(x_all, block, i)
        choose = chooser(block, i)

        @pl.when(i > 0)
        def _():
            staged(block, i)

        def activate(cols):
            before = choose([dot(x_tile[...], w_in[e, :, cols]) for e in range(experts)])
            square = before * before
            tanh = jnp.tanh(0.7978845608028654 * before * (1.0 + 0.044715 * square))
            half = 0.5 * (1.0 + tanh)
            slope = half + 0.5 * before * (1.0 - tanh * tanh) * (
                0.7978845608028654 * (1.0 + 0.134145 * square)
            )
            stage[0, :, cols] = (before * half).astype(BF)
            stage[3, :, cols] = slope.astype(BF)

        def produce(cols):
            results = [dot(stage[0], w_out[e, :, cols]) for e in range(experts)]
            stage[2, :, cols] = choose(results).astype(BF)

        columns(activate)
        columns(produce)
        for index in (0, 2, 3):
            stage_copy(index, block, i).start()

    def backward_tile(block, i, first):
        load(slope_o, block, i)
        choose = chooser(block, i)

        @pl.when(jnp.logical_not(first))
        def _():
            stage_copy(1, block, i).wait()

        def before_back(cols):
            results = [dot(packed_c[tile_of(i)], w_out[e, cols, :], ((1,), (1,))) for e in range(experts)]
            stage[1, :, cols] = (choose(results) * x_tile[:, cols].astype(F32)).astype(BF)

        def members_back(cols):
            results = [dot(stage[1], w_in[e, cols, :], ((1,), (1,))) for e in range(experts)]
            d_part[block, tile_of(i), cols] = choose(results).astype(BF)

        columns(before_back)
        stage_copy(1, block, i).start()
        columns(members_back)

    def phase(p, carry):
        def come(j):
            @pl.when((p == 1) & middle)
            def _():
                relay(0, 0, j)
                relay(2, 1, j)

            @pl.when((p == 2) & middle)
            def _():
                relay(3, 1, j)

            @pl.when((p > 0) & (p < 4) & end)
            def _():
                got(p, j)

        def ahead(i):
            each(come, i * group, (i + 1) * group)

            @pl.when(p < 4)
            def _():
                forward_tile(physical(forward_rel(p)), i)

            @pl.when((p == 3) & middle)
            def _():
                def pass_on(j):
                    add(2, j, from_down, 1, rs_down)
                    sum_copy(2, j, from_up, 1, rs_up, up).start()

                each(pass_on, i * group, (i + 1) * group)

        each(ahead, 0, tiles)

        @pl.when(p < 4)
        def _():
            staged(plane, 0)

        @pl.when(p < 3)
        def _():
            @pl.when(p == 0)
            def _():
                each(lambda off: dispatch_copy(off, peer_of(off), me).wait_send(), 1, devices)

            @pl.when(p > 0)
            def _():
                cot_sent(p - 1)
                cot_own(p - 1).wait()

            @pl.when((p == 0) & end)
            def _():
                far_copy(1).wait_recv()

            @pl.when((p == 1) & end)
            def _():
                far_copy(2).wait_recv()

            send_cot(p + 1, (p == 1) | ((p == 0) & end))

        @pl.when(p == 4)
        def _():
            @pl.when(end)
            def _():
                each(lambda j: out_send(2, j), 0, pieces)
                each(lambda j: out_send(1, j), 0, pieces)

        rel = cot_rel(p - 1)

        def go(j):
            @pl.when((p < 4) & end)
            def _():
                sum_copy(rel, j, from_down, rel - 1, rs_down, up).start()

            @pl.when((p == 4) & middle)
            def _():
                add(3, j, from_down, 2, rs_down)
                sum_copy(3, j, from_up, 0, rs_up, up).start()

            @pl.when((p == 4) & middle & (j > 0))
            def _():
                add(0, j - 1, from_up, 0, rs_up)
                sum_copy(0, j - 1, from_up, 0, rs_up, down).start()

        def behind(i):
            backward_tile(physical(rel), i, (p == 1) & (i == 0))
            each(go, i * group, (i + 1) * group)

        @pl.when(p > 0)
        def _():
            collect_cot(p - 1)
            each(behind, 0, tiles)

        return carry

    lax.fori_loop(0, 5, phase, 0)
    stage_copy(1, plane, 0).wait()
    keep_cot(jnp.int32(3)).wait()

    @pl.when(middle)
    def _():
        add(0, pieces - 1, from_up, 0, rs_up)
        sum_copy(0, pieces - 1, from_up, 0, rs_up, down).start()

    def last(j):
        @pl.when(middle)
        def _():
            add(1, j, from_down, 0, rs_down)
            add(1, j, from_up, 1, rs_up)

        @pl.when(end)
        def _():
            add(0, j, from_up, 0, rs_up)

    each(last, 0, pieces)

    cot_sent(jnp.int32(2))

    def back_slots(device):
        row = lax.broadcasted_iota(jnp.int32, (rows, chunk), 0)
        return dot(ones_where(row == target_rows[device]), d_part[plane], ((0,), (0,))).astype(BF)

    def back_copy(off, to, frm):
        return remote(
            slots.at[1, to], returned.at[frm], back_send.at[off], back_recv.at[off], {"expert": to}
        )

    def back(off):
        peer = peer_of(off)
        slots[1, peer] = back_slots(peer)
        back_copy(off, peer, me).start()

    each(back, 1, devices)
    returned[me] = back_slots(me)

    @pl.when(middle)
    def _():
        each(out_relay, 0, pieces)

    each(lambda off: back_copy(off, me, source_of(off)).wait_recv(), 1, devices)
    slot = lax.broadcasted_iota(jnp.int32, (devices * chunk, x.shape[0]), 0)
    flat = returned[...].reshape(devices * chunk, width)
    d_second[...] = dot(ones_where(slot == places[plane, 0:1, :]), flat, ((0,), (0,))).astype(BF)

    @pl.when(middle)
    def _():
        def out_last(j):
            d_part[plane, part_of(j)] = out_sum(1, j, [(o_down, 0, os_down), (o_up, 1, os_up)])

        each(out_last, 0, pieces)

    @pl.when(end)
    def _():
        own = pltpu.make_async_copy(part_o.at[plane, pl.ds(0, rows)], d_part.at[plane], local_sem.at[0])
        own.start()
        own.wait()

    own = pltpu.make_async_copy(d_part.at[plane], own_out.at[pl.ds(0, rows)], local_sem.at[1])
    own.start()

    x_tile[...] = jnp.zeros(x_tile.shape, BF)
    whole_tiles = -(-rows // TILE) * TILE
    fills = []
    for array, stop in [(a, whole_tiles) for a in (x_all, cot_all, act_o, dbef_o)] + [(part_o, part_o.shape[1])]:
        for block in range(4):
            for start in range(rows, stop, tile_height):
                fills.append(array.at[block, pl.ds(start, min(tile_height, stop - start))])
    for start in range(rows, own_out.shape[0], tile_height):
        fills.append(own_out.at[pl.ds(start, min(tile_height, own_out.shape[0] - start))])
    for there in fills:
        fill = pltpu.make_async_copy(x_tile.at[pl.ds(0, there.shape[0])], there, local_sem.at[0])
        fill.start()
        fill.wait()
    own.wait()

    each(lambda off: back_copy(off, peer_of(off), me).wait_send(), 1, devices)
    cot_sent(jnp.int32(3))

    @pl.when(middle)
    def _():
        for index in range(3):
            far_copy(index).wait_send()

    def sent(j):
        gather_copy(0, plane, j, True).wait_send()

        @pl.when(middle)
        def _():
            gather_copy(1, plane, j, True).wait_send()
            gather_copy(0, physical(0), j, False).wait_send()
            for rel in (2, 3):
                gather_copy(1, physical(rel), j, False).wait_send()
            for rel in (0, 2, 3):
                sum_copy(rel, j, from_up, 0, rs_up, up).wait_send()
            out_copy(2, j, part_o.at[0, part_of(j)], o_up, 1, os_up, up).wait_send()

        @pl.when(end)
        def _():
            for rel in (1, 2, 3):
                sum_copy(rel, j, from_up, 0, rs_up, up).wait_send()
            for rel in (1, 2):
                out_copy(rel, j, part_o.at[0, part_of(j)], o_up, 1, os_up, up).wait_send()

    each(sent, 0, pieces)


def expert_pass(rows, pieces, group, number, room, x, places, targets, target, cot_col, ends, w_in, w_out):
    devices, _, chunk = target.shape
    width, hidden = w_in.shape[1:]
    planes = cot_col.shape[0]
    height = rows // pieces
    tall = group * height
    here, there = pl.BlockSpec(memory_space=pltpu.VMEM), pl.BlockSpec(memory_space=pl.ANY)
    dma = pltpu.SemaphoreType.DMA
    low = lambda *shape: jax.ShapeDtypeStruct(shape, BF)
    held = lambda *shape: pltpu.VMEM(shape, BF)
    wide = low(planes, devices * chunk, width)
    return pl.pallas_call(
        functools.partial(pass_kernel, rows, pieces, group),
        in_specs=[here] * 4 + [there] + [here] * 3,
        out_specs=[there] * 11 + [here],
        out_shape=[wide] * 4
        + [low(planes, room, width), low(planes, rows, hidden), low(3, rows, width), low(2, rows, width), low(room, width)]
        + [low(*cot_col.shape), low(planes, devices, chunk, width), low(*x.shape)],
        scratch_shapes=[
            held(2, devices, chunk, width),
            held(devices, chunk, width),
            held(rows, width),
            held(rows, width),
            held(*x.shape),
            held(devices, chunk, width),
            held(planes, rows, width),
            held(3, rows, width),
            held(2, rows, width),
            held(tall, width),
            held(height, width),
            held(4, tall, hidden),
            dma((devices,)),
            dma((devices,)),
            dma((planes, devices)),
            dma((planes, devices)),
            dma((3,)),
            dma((3,)),
            dma((devices,)),
            dma((devices,)),
            dma((2, planes, pieces)),
            dma((planes, pieces)),
            dma((planes, pieces)),
            dma((3, pieces)),
            dma((2, pieces)),
            dma((planes, pieces)),
            dma((3, pieces)),
            dma((2, pieces)),
            dma((2,)),
            dma((4,)),
            dma((planes,)),
            dma,
        ],
        compiler_params=pltpu.CompilerParams(
            collective_id=number, has_side_effects=True, vmem_limit_bytes=62 * 2**20
        ),
        cost_estimate=pl.CostEstimate(
            flops=20 * planes * rows * width * hidden,
            bytes_accessed=16 * planes * rows * width,
            transcendentals=planes * rows * hidden,
        ),
        name="expert_pass",
    )(x, places, targets, target, cot_col, ends, w_in, w_out)


def tail_kernel(
    pieces,
    tokens, residual, d_second, cot, q, k, v, att, lse, project_in, project_out, gain1, bias1, gain2,
    target_rows, own_in, partial,
    grad_tokens, summed_grads, small_out, out_slots,
    w_in, w_out, normed, d_branch, d_normed, grads, small, small_plane, small_near, small_far,
    core_buf, half_buf, plane_buf, own, o_far, o_near, mine, slot_tile,
    o_send, o_recv, out_sem, slot_sem,
    ar_send, ar_recv, near_send, near_recv, far_send, far_recv,
    w_sem, local_sem,
):
    me, plane = lax.axis_index("expert"), lax.axis_index("hidden")
    devices, planes = lax.axis_size("expert"), lax.axis_size("hidden")
    width = tokens.shape[1]
    quads, tall, quad = grads.shape
    other = lambda off: {"expert": lax.rem(me + off, devices)}
    across = lambda off: {"hidden": lax.rem(plane + off, planes)}

    barrier = pltpu.get_barrier_semaphore()

    def greet(off, carry):
        pl.semaphore_signal(barrier, inc=1, device_id=other(off), device_id_type=MESH)
        return carry

    lax.fori_loop(1, devices, greet, 0)
    for off in range(1, planes):
        pl.semaphore_signal(barrier, inc=1, device_id=across(off), device_id_type=MESH)

    def weights(j, slot):
        cols = lambda third: pl.ds(pl.multiple_of(third * width + j * quad, quad), quad)
        copies = [
            pltpu.make_async_copy(project_in.at[:, cols(third)], w_in.at[slot, third], w_sem.at[slot, third])
            for third in range(3)
        ]
        rows_out = pl.ds(pl.multiple_of(j * quad, quad), quad)
        copies.append(pltpu.make_async_copy(project_out.at[rows_out], w_out.at[slot], w_sem.at[slot, 3]))
        return copies

    for copy in weights(0, 0):
        copy.start()
    pl.semaphore_wait(barrier, devices - 1 + planes - 1)

    rows = own.shape[0]
    height = rows // pieces
    side = lax.div(plane, 2)
    r = plane + side * (3 - 2 * plane)
    middle = r == 1
    step = 1 - 2 * side
    up, down = {"hidden": plane + step}, {"hidden": plane - step}
    physical = lambda rel: rel + side * (3 - 2 * rel)
    part_of = lambda j: pl.ds(pl.multiple_of(j * height, 16), height)

    def out_copy(kind, j):
        source = partial.at[physical(3), part_of(j)] if kind == 0 else mine.at[kind - 1, part_of(j)]
        there = (o_far if kind == 0 else o_near).at[part_of(j)]
        return remote(source, there, o_send.at[kind, j], o_recv.at[kind, j], down if kind == 2 else up)

    def out_load(index):
        source = own_in if index == 2 else partial.at[physical(3 - 3 * index)]
        return pltpu.make_async_copy(source, own if index == 2 else mine.at[index], out_sem.at[index])

    @pl.when(r == 0)
    def _():
        def body(j, carry):
            out_copy(0, j).start()
            return carry

        lax.fori_loop(0, pieces, body, 0)

    for index in range(3):
        out_load(index).start()

    def out_add(kind, j, target):
        out_copy(kind, j).wait_recv()
        there = o_far if kind == 0 else o_near
        here = target[part_of(j)].astype(F32)
        target[part_of(j)] = (here + there[part_of(j)].astype(F32)).astype(BF)

    def out_turn(j):
        @pl.when(middle & (j < pieces))
        def _():
            out_add(0, j, mine.at[0])
            out_copy(1, j).start()

        @pl.when(middle & (j > 0) & (j <= pieces))
        def _():
            out_add(1, j - 1, mine.at[1])
            out_copy(2, j - 1).start()

        @pl.when((r == 0) & (j > 1) & (j <= pieces + 1))
        def _():
            out_add(2, j - 2, own)

    def out_slot_copy(device):
        slot = lax.rem(device, 2)
        return pltpu.make_async_copy(slot_tile.at[slot], out_slots.at[device], slot_sem.at[slot])

    def out_slot(device, carry):
        @pl.when(device > 1)
        def _():
            out_slot_copy(device - 2).wait()

        row = lax.broadcasted_iota(jnp.int32, (rows, slot_tile.shape[1]), 0)
        mask = ones_where(row == target_rows[device])
        slot_tile[lax.rem(device, 2)] = dot(mask, own[...], ((0,), (0,))).astype(BF)
        out_slot_copy(device).start()
        return carry

    bits = devices.bit_length() - 1
    bit = lambda i: lax.rem(lax.div(me, 1 << i), 2)
    partner = lambda i: {"expert": me + (1 << i) * (1 - 2 * bit(i))}
    half = tall // 2
    part = half // 2
    orders = [list(range(1, bits)), list(range(bits - 1, 0, -1))]
    levels = bits - 1
    last = part >> levels
    slice_len = last // planes

    def segment(a, level):
        start = bit(0) * half + a * part
        for i in range(level):
            start = start + bit(orders[a][i]) * (part >> (i + 1))
        return start

    def span(start, length):
        return pl.ds(pl.multiple_of(start, 16), length)

    slot_of = {}

    def sems(name, c):
        index = slot_of.setdefault(name, len(slot_of))
        return ar_send.at[index, c], ar_recv.at[index, c]

    def core_copy(c):
        source = grads.at[c, span((1 - bit(0)) * half, half)]
        return [remote(source, core_buf.at[c], *sems("core", c), partner(0))]

    def core_end(c):
        keep = span(bit(0) * half, half)
        grads[c, keep] = (grads[c, keep].astype(F32) + core_buf[c].astype(F32)).astype(BF)

    def halve_copy(level, c):
        copies = []
        length = part >> (level + 1)
        for a in range(2):
            i = orders[a][level]
            source = grads.at[c, span(segment(a, level) + (1 - bit(i)) * length, length)]
            buffer = half_buf.at[c, a, pl.ds(part - (part >> level), length)]
            copies.append(remote(source, buffer, *sems(("half", level, a), c), partner(i)))
        return copies

    def halve_end(level, c):
        length = part >> (level + 1)
        for a in range(2):
            keep = span(segment(a, level + 1), length)
            other_half = half_buf[c, a, pl.ds(part - (part >> level), length)]
            grads[c, keep] = (grads[c, keep].astype(F32) + other_half.astype(F32)).astype(BF)

    def plane_span(a, p):
        return span(segment(a, levels) + p * slice_len, slice_len)

    def plane_copy(c):
        copies = []
        for a in range(2):
            for off in range(1, planes):
                source = grads.at[c, plane_span(a, lax.rem(plane + off, planes))]
                buffer = plane_buf.at[c, a, off - 1]
                copies.append(remote(source, buffer, *sems(("plane", a, off), c), across(off)))
        return copies

    def plane_end(c):
        for a in range(2):
            keep = plane_span(a, plane)
            total = grads[c, keep].astype(F32)
            for off in range(planes - 1):
                total = total + plane_buf[c, a, off].astype(F32)
            grads[c, keep] = total.astype(BF)
        copies = [
            pltpu.make_async_copy(
                grads.at[c, plane_span(a, plane)],
                summed_grads.at[c, plane_span(a, plane)],
                local_sem.at[a],
            )
            for a in range(2)
        ]
        for copy in copies:
            copy.start()
        for copy in copies:
            copy.wait()

    def spread_copy(c):
        copies = []
        for a in range(2):
            for off in range(1, planes):
                keep = plane_span(a, plane)
                source, there = grads.at[c, keep], summed_grads.at[c, keep]
                copies.append(remote(source, there, *sems(("spread", a, off), c), across(off)))
        return copies

    def double_copy(level, c):
        copies = []
        for a in range(2):
            have = summed_grads.at[c, span(segment(a, level + 1), part >> (level + 1))]
            names = sems(("double", level, a), c)
            copies.append(remote(have, have, *names, partner(orders[a][level])))
        return copies

    def core_back_copy(c):
        have = summed_grads.at[c, span(bit(0) * half, half)]
        return [remote(have, have, *sems("core_back", c), partner(0))]

    nothing = lambda c: None
    stages = [(core_copy, core_end)]
    for level in range(levels):
        stages.append((functools.partial(halve_copy, level), functools.partial(halve_end, level)))
    stages.append((plane_copy, plane_end))
    stages.append((spread_copy, nothing))
    for level in reversed(range(levels)):
        stages.append((functools.partial(double_copy, level), nothing))
    stages.append((core_back_copy, nothing))

    def finish(stage, c):
        copies, end = stages[stage]
        for copy in copies(c):
            copy.wait_recv()
        for copy in copies(c):
            copy.wait_send()
        end(c)

    def near_copy(off):
        return remote(
            small, small_near.at[off - 1], near_send.at[off - 1], near_recv.at[off - 1], other(off)
        )

    def far_copy(off):
        return remote(
            small_plane, small_far.at[off - 1], far_send.at[off - 1], far_recv.at[off - 1], across(off)
        )

    def each_near(act):
        def body(off, carry):
            act(near_copy(off))
            return carry

        lax.fori_loop(1, devices, body, 0)

    scale = jnp.asarray(HEAD_DIM**-0.5, BF)
    lanes = 2 * HEAD_DIM
    xhat2, root2 = normalise(residual[...])
    d_values, sums = layer_norm_back(d_second[...].astype(F32), xhat2, root2, gain2[...])
    d_residual = cot[...].astype(F32) + d_values
    grad_tokens[...] = d_residual
    d_branch[...] = d_residual.astype(BF)
    small[...] = jnp.zeros(small.shape, F32)
    small[2:3, :], small[3:4, :] = sums
    normed[...] = (normalise(tokens[...].astype(F32))[0] * gain1[...] + bias1[...]).astype(BF)
    d_normed[...] = jnp.zeros(d_normed.shape, F32)

    def quarter(j):
        slot = lax.rem(j, 2)
        for copy in weights(j, slot):
            copy.wait()

        @pl.when(j < quads - 1)
        def _():
            for copy in weights(j + 1, 1 - slot):
                copy.start()

        out = dot(att[j], d_branch[...], ((0,), (0,))).astype(BF)
        for m in range(width // quad):
            grads[j, 3 * width + m * quad : 3 * width + (m + 1) * quad] = out[:, m * quad : (m + 1) * quad]
        d_att = dot(d_branch[...], w_out[slot], ((1,), (1,))).astype(BF)
        d_thirds = attention_back(j, q, k, v, d_att, lse, scale, lanes)
        total = 0.0
        for third, d_third in enumerate(d_thirds):
            grads[j, third * width : (third + 1) * width] = dot(
                normed[...], d_third, ((0,), (0,))
            ).astype(BF)
            total = total + dot(d_third, w_in[slot, third], ((1,), (1,)))
        d_normed[...] += total

        @pl.when(j == quads - 1)
        def _():
            xhat, root = normalise(tokens[...].astype(F32))
            d_first, first_sums = layer_norm_back(d_normed[...], xhat, root, gain1[...])
            grad_tokens[...] += d_first
            small[0:1, :], small[1:2, :] = first_sums

    count = len(stages)

    def tick(t, carry):
        @pl.when(t < quads)
        def _():
            quarter(t)
            for copy in stages[0][0](t):
                copy.start()

        for stage in range(count, 0, -1):
            c = t - stage

            @pl.when((c >= 0) & (c < quads))
            def _(stage=stage, c=c):
                finish(stage - 1, c)
                if stage < count:
                    for copy in stages[stage][0](c):
                        copy.start()

        @pl.when(t == 1)
        def _():
            for index in range(3):
                out_load(index).wait()

        @pl.when((t >= 1) & (t <= 2 + pieces))
        def _():
            out_turn(t - 1)

        @pl.when(t == quads + pieces)
        def _():
            lax.fori_loop(0, devices, out_slot, 0)
            for device in (devices - 2, devices - 1):
                out_slot_copy(device).wait()

        @pl.when(t == quads - 1)
        def _():
            each_near(lambda copy: copy.start())

        @pl.when(t == quads + 1)
        def _():
            each_near(lambda copy: copy.wait_recv())
            each_near(lambda copy: copy.wait_send())
            total = small[...]
            for off in range(devices - 1):
                total = total + small_near[off]
            small_plane[...] = total
            for off in range(1, planes):
                far_copy(off).start()

        @pl.when(t == quads + 3)
        def _():
            for off in range(1, planes):
                far_copy(off).wait_recv()
            for off in range(1, planes):
                far_copy(off).wait_send()
            total = small_plane[...]
            for off in range(planes - 1):
                total = total + small_far[off]
            small_out[...] = total

        return carry

    lax.fori_loop(0, max(quads + count, quads + pieces + 1), tick, 0)

    def outs_sent(j, carry):
        @pl.when(r == 0)
        def _():
            out_copy(0, j).wait_send()

        @pl.when(middle)
        def _():
            out_copy(1, j).wait_send()
            out_copy(2, j).wait_send()

        return carry

    lax.fori_loop(0, pieces, outs_sent, 0)


def attention_back(j, q, k, v, d_att, lse, scale, lanes):
    rows, quad = d_att.shape
    keep = tri(BLOCK)
    blocks = rows // BLOCK
    cut = lambda array, block: array[block * BLOCK : (block + 1) * BLOCK]
    d_q, d_k, d_v = [], [], []
    lane = lax.broadcasted_iota(jnp.int32, (BLOCK, lse.shape[1]), 1)
    for pair in range(quad // lanes):
        cols = slice(pair * lanes, (pair + 1) * lanes)
        query = q[j, :, cols] * scale
        key, value, d_pair = k[j, :, cols], v[j, :, cols], d_att[:, cols]
        keys, values = halves(key), halves(value)
        pair_q, pair_k, pair_v = [], [], []
        for head in range(2):
            index = j * (quad // HEAD_DIM) + 2 * pair + head
            q_parts = []
            k_parts, v_parts = [0.0] * blocks, [0.0] * blocks
            for q_block in range(blocks):
                level = jnp.sum(
                    jnp.where(lane == index, lse[q_block * BLOCK : (q_block + 1) * BLOCK, :], 0.0),
                    -1,
                    keepdims=True,
                )
                shares, d_shares, inner = [], [], 0.0
                for k_block in range(q_block + 1):
                    scores = dot(cut(query, q_block), cut(keys[head], k_block), ((1,), (1,)))
                    share = jnp.exp(scores - level)
                    if k_block == q_block:
                        share = jnp.where(keep, share, 0.0)
                    d_share = dot(cut(d_pair, q_block), cut(values[head], k_block), ((1,), (1,)))
                    inner = inner + jnp.sum(share * d_share, -1, keepdims=True)
                    shares.append(share)
                    d_shares.append(d_share)
                total = 0.0
                for k_block in range(q_block + 1):
                    d_scores = (shares[k_block] * (d_shares[k_block] - inner)).astype(BF)
                    total = total + dot(d_scores, cut(key, k_block))
                    k_parts[k_block] += dot(d_scores, cut(query, q_block), ((0,), (0,)))
                    v_parts[k_block] += dot(
                        shares[k_block].astype(BF), cut(d_pair, q_block), ((0,), (0,))
                    )
                q_parts.append(total * HEAD_DIM**-0.5)
            pair_q.append(jnp.concatenate(q_parts, 0))
            pair_k.append(jnp.concatenate(k_parts, 0))
            pair_v.append(jnp.concatenate(v_parts, 0))
        d_q.append(join(*pair_q).astype(BF))
        d_k.append(join(*pair_k).astype(BF))
        d_v.append(join(*pair_v).astype(BF))
    return [jnp.concatenate(parts, 1) for parts in (d_q, d_k, d_v)]


def tail(
    number, devices, planes, pieces, target, own, partial, tokens, residual, d_second, cot, q, k, v, att, lse, project_in, project_out,
    gain1, bias1, gain2,
):
    tokens_dev, width = tokens.shape
    quads, _, quad = q.shape
    tall = 4 * width
    bits = devices.bit_length() - 1
    part = tall // 4
    slice_len = (part >> (bits - 1)) // planes
    slots = 2 + 4 * (bits - 1) + 4 * (planes - 1)
    chunk = target.shape[2]
    rows = own.shape[0]
    here, there = pl.BlockSpec(memory_space=pltpu.VMEM), pl.BlockSpec(memory_space=pl.ANY)
    dma = pltpu.SemaphoreType.DMA
    low = lambda *shape: pltpu.VMEM(shape, BF)
    full = lambda *shape: pltpu.VMEM(shape, F32)
    return pl.pallas_call(
        functools.partial(tail_kernel, pieces),
        in_specs=[here] * 9 + [there] * 2 + [here] * 4 + [there] * 2,
        out_specs=[here, there, here, there],
        out_shape=[
            jax.ShapeDtypeStruct((tokens_dev, width), F32),
            jax.ShapeDtypeStruct((quads, tall, quad), BF),
            jax.ShapeDtypeStruct((8, width), F32),
            jax.ShapeDtypeStruct((devices, chunk, width), BF),
        ],
        scratch_shapes=[
            low(2, 3, width, quad),
            low(2, quad, width),
            low(tokens_dev, width),
            low(tokens_dev, width),
            full(tokens_dev, width),
            low(quads, tall, quad),
            full(8, width),
            full(8, width),
            full(devices - 1, 8, width),
            full(planes - 1, 8, width),
            low(quads, tall // 2, quad),
            low(quads, 2, part - (part >> (bits - 1)), quad),
            low(quads, 2, planes - 1, slice_len, quad),
            low(rows, width),
            low(rows, width),
            low(rows, width),
            low(2, rows, width),
            low(2, chunk, width),
            dma((3, pieces)),
            dma((3, pieces)),
            dma((3,)),
            dma((2,)),
            dma((slots, quads)),
            dma((slots, quads)),
            dma((devices - 1,)),
            dma((devices - 1,)),
            dma((planes - 1,)),
            dma((planes - 1,)),
            dma((2, 4)),
            dma((2,)),
        ],
        compiler_params=pltpu.CompilerParams(
            collective_id=number, has_side_effects=True, vmem_limit_bytes=62 * 2**20
        ),
        cost_estimate=pl.CostEstimate(
            flops=20 * tokens_dev * width * width,
            bytes_accessed=64 * 2**20,
            transcendentals=HEADS * tokens_dev * tokens_dev,
        ),
        name="tail",
    )(
        tokens, residual, d_second, cot, q, k, v, att, lse, project_in, project_out,
        *(x.reshape(1, width) for x in (gain1, bias1, gain2)), target, own, partial,
    )


def spread_kernel(summed, grad_in, grad_out):
    third = pl.program_id(1)

    @pl.when(third < 3)
    def _():
        grad_in[...] = summed[0].astype(F32)

    @pl.when(third == 3)
    def _():
        quad = summed.shape[2]
        for m in range(grad_out.shape[1] // quad):
            rows = slice(m * quad, (m + 1) * quad)
            grad_out[:, rows] = summed[0, rows].astype(F32)


def spread(summed):
    quads, tall, quad = summed.shape
    width = tall // 4
    return pl.pallas_call(
        spread_kernel,
        grid=(quads, 4),
        in_specs=[pl.BlockSpec((1, width, quad), lambda j, t: (j, t, 0))],
        out_specs=[
            pl.BlockSpec((width, quad), lambda j, t: (0, jnp.minimum(t, 2) * quads + j)),
            pl.BlockSpec((quad, width), lambda j, t: (j, 0)),
        ],
        out_shape=[
            jax.ShapeDtypeStruct((width, 3 * width), F32),
            jax.ShapeDtypeStruct((width, width), F32),
        ],
        compiler_params=pltpu.CompilerParams(vmem_limit_bytes=60 * 2**20),
        name="spread",
    )(summed)


def on_device(
    tokens,
    token_ids,
    hash_table,
    first_gain,
    first_bias,
    project_in,
    project_out,
    second_gain,
    second_bias,
    expert_in,
    expert_out,
    cotangent,
):
    rows_dev, width = tokens.shape
    expert_devs = lax.axis_size("expert")
    hidden_devs = lax.axis_size("hidden")
    local = expert_in.shape[0]
    experts = local * expert_devs
    capacity = 8 * ((3 * rows_dev + 8 * experts - 1) // (8 * experts))
    chunk = local * capacity

    owner = hash_table.at[token_ids].get(mode="promise_in_bounds")
    expert_ids = jnp.arange(experts, dtype=jnp.int32)
    onehot = owner[:, None] == expert_ids[None, :]
    earlier = lax.broadcasted_iota(jnp.int32, (rows_dev, rows_dev), 1) < lax.broadcasted_iota(
        jnp.int32, (rows_dev, rows_dev), 0
    )
    before_count = jnp.dot(earlier.astype(BF), onehot.astype(BF), preferred_element_type=F32)
    counts = jnp.sum(onehot.astype(jnp.int32), 0)
    grouped = counts.reshape(expert_devs, local)
    first_slot = (
        jnp.cumsum(grouped, 1) - grouped + jnp.arange(expert_devs, dtype=jnp.int32)[:, None] * chunk
    ).reshape(experts)
    place = jnp.sum(
        jnp.where(onehot, before_count.astype(jnp.int32) + first_slot[None, :], 0), 1
    )
    residual, second, query, keys, values, attended, lse, cot_col, all_counts, places = attend(
        expert_devs, hidden_devs, tokens, project_in, project_out,
        first_gain, first_bias, second_gain, second_bias, place, cotangent, counts,
    )
    all_counts = all_counts[:, :, 0, :experts].reshape(
        hidden_devs, expert_devs, expert_devs, local
    )
    group = lax.axis_index("expert")
    plane = lax.axis_index("hidden")
    group_counts = lax.dynamic_index_in_dim(all_counts, group, 2, keepdims=False)
    most = jnp.max(jnp.sum(all_counts, (1, 3)))

    starts = jnp.cumsum(group_counts, 2) - group_counts
    totals = jnp.sum(group_counts, 1)
    firsts = jnp.cumsum(totals, 1) - totals
    bases = jnp.cumsum(group_counts, 1) - group_counts + firsts[:, None, :]
    slot = jnp.arange(chunk, dtype=jnp.int32)[None, None, :]
    targets = jnp.full((hidden_devs, expert_devs, chunk), -1, jnp.int32)
    for l in range(local):
        offset = slot - starts[:, :, l : l + 1]
        inside = (offset >= 0) & (offset < group_counts[:, :, l : l + 1])
        targets = jnp.where(inside, bases[:, :, l : l + 1] + offset, targets)
    target_rows = lax.dynamic_index_in_dim(targets, plane, 0, keepdims=False)
    target = target_rows.reshape(-1)

    most_rows = expert_devs * chunk
    ends = jnp.cumsum(totals, 1)
    bounds = jnp.broadcast_to(ends[:, :, None], (hidden_devs, local, 128))
    row = jnp.arange(most_rows, dtype=jnp.int32)[None, :]
    base = jnp.arange(0, most_rows, TILE, dtype=jnp.int32)[None, None, :]
    in_tile = lambda edge: jnp.clip(edge.T[:, :, None] - base, 0, TILE).reshape(local, -1)
    lows, highs = in_tile(firsts), in_tile(ends)

    def run(rows, pieces, group, number):
        x_all, cot_all, act, dbef, part, _, _, _, own, _, _, d_second = expert_pass(
            rows, pieces, group, number, room, second, places,
            targets.reshape(hidden_devs, 1, expert_devs * chunk),
            target_rows.reshape(expert_devs, 1, chunk), cot_col,
            bounds, expert_in, expert_out,
        )
        return x_all, cot_all, act, dbef, part, own, d_second, jnp.zeros_like(d_second)

    def run_any():
        eid = sum((row >= ends[:, l : l + 1]).astype(jnp.int32) for l in range(local))
        has = jnp.stack(
            [jnp.any((eid == l).reshape(-1, TILE), 1).astype(jnp.int32) for l in range(local)], 1
        )
        eid = eid.astype(F32)
        send = (place[None, :] == jnp.arange(most_rows, dtype=jnp.int32)[:, None]).astype(BF)
        pack = (target[None, :] == jnp.arange(most_rows, dtype=jnp.int32)[:, None]).astype(BF)

        def gather(values):
            slots = dot(send, values).astype(BF).reshape(expert_devs, chunk, width)
            arrived = lax.all_to_all(slots, "expert", 0, 0, tiled=True)
            packed = dot(pack, arrived.reshape(-1, width)).astype(BF)
            return lax.all_gather(packed, "hidden", axis=0, tiled=True)

        def add_up(partial):
            summed = lax.psum_scatter(partial, "hidden", scatter_dimension=0, tiled=True)
            return dot(pack, summed, ((0,), (0,))).astype(BF).reshape(expert_devs, chunk, width)

        x_rows, cot_rows = gather(second), gather(cotangent)
        act, dbef, part, dmem = expert_rows(
            x_rows, cot_rows, eid.reshape(-1, 1), has, expert_in, expert_out
        )
        returned = lax.all_to_all(add_up(dmem), "expert", 0, 0, tiled=True)
        d_second = dot(send, returned.reshape(-1, width), ((0,), (0,))).astype(BF)
        wide = (hidden_devs, most_rows, width)
        x_rows, cot_rows, act, dbef = (v.reshape(wide) for v in (x_rows, cot_rows, act, dbef))
        returned = lax.all_to_all(add_up(part), "expert", 0, 0, tiled=True)
        produced = dot(send, returned.reshape(-1, width), ((0,), (0,))).astype(BF)
        none = jnp.zeros((hidden_devs, room, width), BF)
        return x_rows, cot_rows, act, dbef, none, none[0], d_second, produced

    plans = [(768, 4, 2, 1), (832, 4, 2, 2), (896, 4, 2, 3)]
    plans = [plan for plan in plans if plan[0] < most_rows and hidden_devs == 4]
    room = max(plan[0] for plan in plans)
    pick = sum((most <= plan[0]).astype(jnp.int32) for plan in plans)
    branches = [run_any] + [functools.partial(run, *plan) for plan in reversed(plans)]
    x_all, cot_all, act, dbef, part, own, d_second, more = lax.switch(pick, branches)

    grad_tokens, summed, small, slots = tail(
        4, expert_devs, hidden_devs, 4, target_rows.reshape(expert_devs, 1, chunk), own, part,
        tokens, residual, d_second, cotangent, query, keys, values,
        attended, lse, project_in, project_out, first_gain, first_bias, second_gain,
    )
    slots, act = lax.optimization_barrier((slots, act))
    returned = lax.all_to_all(slots, "expert", 0, 0, tiled=True)
    slot_of = jnp.arange(most_rows, dtype=jnp.int32)[:, None]
    send = (place[None, :] == slot_of).astype(BF)
    produced = dot(send, returned.reshape(-1, width), ((0,), (0,)))
    block_out = (residual + (produced + more.astype(F32))).astype(BF)
    grad_in, grad_out = spread(summed)
    flat = lambda v: v.reshape(-1, width)
    grad_expert_in, grad_expert_out = expert_grads(
        flat(x_all), flat(cot_all), lows, highs, flat(act), flat(dbef)
    )
    return (
        block_out,
        grad_tokens,
        small[0],
        small[1],
        grad_in,
        grad_out,
        small[2],
        small[3],
        grad_expert_in,
        grad_expert_out,
    )


def solution(mesh):
    rows = P(("expert", "hidden"), None)
    w_in, w_out = P("expert", None, "hidden"), P("expert", "hidden", None)
    return jax.shard_map(
        on_device,
        mesh=mesh,
        in_specs=(
            rows,
            P(("expert", "hidden")),
            P(),
            P(),
            P(),
            P(),
            P(),
            P(),
            P(),
            w_in,
            w_out,
            rows,
        ),
        out_specs=(rows, rows, P(), P(), P(), P(), P(), P(), w_in, w_out),
        check_vma=False,
    )
```
